128 devices in a mesh: clus: 128 (over y, z, x, core).
Axes of the slice: x: 4, y: 4, z: 4, core: 2. Of those that a mesh axis runs over, the one named last changes fastest.
Arguments:
- charges: float32 [32, 1048576], P(None, 'clus'), may hold values from -6 to 6
- positions: float32 [3, 1048576], P(None, 'clus'), may hold values from -2 to 2
- quad_weights: float32 [1048576], P('clus'), may hold values from 0.1 to 1
- leaf_basis: float32 [4096, 64, 256], P('clus'), may hold values from -0.375 to 0.375
- leaf_nodes: float32 [3, 262144], P(None, 'clus'), may hold values from -2 to 2
- leaf_transfer: float32 [64, 262144], P(None, 'clus'), may hold values from -0.75 to 0.75
- mid_nodes: float32 [3, 8192], P(None, 'clus'), may hold values from -2 to 2
- mid_transfer: float32 [64, 8192], P(None, 'clus'), may hold values from -0.75 to 0.75
- top_nodes: float32 [3, 1024], replicated, may hold values from -2 to 2
- near_list: int32 [4096, 27], P('clus'), may hold values from 0 to 4095, as said below
- near_count: int32 [4096], P('clus'), may hold values from 1 to 27, as said below
- far_list: int32 [4096, 16], P('clus'), may hold values from 0 to 4095, as said below
- mid_mask: int32 [128, 128], P('clus'), may hold values 0 or 1
- top_mask: int32 [16, 16], replicated, may hold values 0 or 1
Outputs:
- potential: float32 [32, 1048576], P(None, 'clus')
The draws below stay inside these ranges and needn't reach their ends.
Inputs may be any that keep to these rules, and one draw needn't show every extreme that they name: `near_list`: every entry names a leaf of the device that owns the row's leaf or of the device just before or after it in a cycle over devices (the last device's next one being the first); the entries of one row are distinct and differ from those of the row's far_list. `far_list`: the same locality holds: sources lie on the owning device or its two cyclic neighbours; entries of one row are distinct. `near_count`: some leaf has all 27 slots live in every draw.
All inputs are finite; a program needn't handle non-finite values. No bound on the sum of `mid_mask` on one device may be relied on, other than what follows from the above.
Results may differ from the reference program's by a relative error of at most 0.0003.
Values sent between devices are 32-bit elements; how exact they have to be, the bound alone decides.
No kernel may reach another device: no remote copies, remote signals or barrier semaphores. Data moves between devices by JAX's collectives and lax.ppermute only.
A program may use at most 128 MiB of HBM per device.

```python
import math
import jax
import jax.numpy as jnp
from jax import lax

LEAF = 256
RANK = 64
NRHS = 32
LEAF_DEV = 32
NEAR_MAX = 27
FAR2 = 16
GROUP = 8
LEAVES = 4096
POINTS = 1048576
TOP = 16
N_CLUS = 128


def window_leaves(key):
    leaf_keys = jax.random.split(key, LEAVES)
    shuffled = jax.vmap(lambda single: jax.random.permutation(single, 3 * LEAF_DEV))(leaf_keys)
    leaf_index = jnp.arange(LEAVES, dtype=jnp.int32)
    first_leaf = leaf_index // LEAF_DEV * LEAF_DEV - LEAF_DEV
    return ((first_leaf[:, None] + shuffled.astype(jnp.int32)) % LEAVES).astype(jnp.int32)


def draw_near_list(key, part):
    chosen = window_leaves(key)
    return chosen[:, :NEAR_MAX]


def draw_far_list(key, part):
    chosen = window_leaves(key)
    return chosen[:, NEAR_MAX:NEAR_MAX + FAR2]


def draw_near_count(key, part):
    key = jax.random.fold_in(key, 11)
    level_key, count_key, pick_key = jax.random.split(key, 3)
    devices = LEAVES // LEAF_DEV
    levels = jax.random.randint(level_key, (devices,), NEAR_MAX // 4 + 1, NEAR_MAX + 1)
    per_leaf = jnp.repeat(levels, LEAF_DEV)
    counts = jax.random.randint(count_key, (LEAVES,), per_leaf // 2 + 1, per_leaf + 1)
    picked = jax.random.randint(pick_key, (), 0, LEAVES)
    counts = jnp.where(jnp.arange(LEAVES) == picked, NEAR_MAX, counts)
    return counts.astype(jnp.int32)


def set_ends(array, own_key, low, high):
    longest = array.shape.index(max(array.shape))
    spots = []
    for shift in (0, 1):
        where = [jax.random.randint(jax.random.fold_in(own_key, axis), (), 0, length) for axis, length in enumerate(array.shape)]
        where[longest] = (where[longest] + shift) % array.shape[longest]
        spots.append(tuple(where))
    return array.at[spots[0]].set(low).at[spots[1]].set(high)


def block_scale(own_key, shape, pieces, smallest, largest):
    level, own = 1.0, jax.random.fold_in(own_key, 6)
    for position, blocks in pieces:
        steps = jnp.exp(jax.random.uniform(jax.random.fold_in(own, position), (blocks,), jnp.float32, smallest / len(pieces), largest / len(pieces)))
        level = level * jnp.repeat(steps, shape[position] // blocks).reshape([-1 if axis == position else 1 for axis in range(len(shape))])
    return level


def centred(stream_key, extent, scale, bound, cuts=(), kind=jnp.bfloat16):
    drawn = jax.random.normal(stream_key, extent, jnp.float32) * scale
    if len(cuts) > 0:
        drawn = block_scale(stream_key, extent, cuts, -0.22, 0.18) * drawn
    return jnp.clip(drawn, min=-bound, max=bound).astype(kind)


def setup_inputs(seed: int = 0) -> dict:
    keys = jax.random.split(jax.random.key(seed), 15)
    charges = centred(keys[0], (NRHS, POINTS), 1.0, 6.0, ((1, 128),), jnp.float32)
    positions = jnp.clip(jax.random.uniform(keys[1], (3, POINTS), jnp.float32, -2.0, 2.0) * block_scale(keys[1], (3, POINTS), ((1, 128),), -0.4, 0.0), -2.0, 2.0)
    quad_weights = jnp.clip(jnp.exp(math.log(1.0) - 2.3025851 * jax.random.uniform(keys[2], (POINTS,), jnp.float32) ** block_scale(keys[2], (POINTS,), ((0, 128),), -0.2, 0.2)), 0.1, 1.0)
    leaf_basis = centred(keys[3], (LEAVES, RANK, LEAF), LEAF ** -0.5, 0.375, ((0, 128),), jnp.float32)
    leaf_nodes = jnp.clip(jax.random.uniform(keys[4], (3, LEAVES * RANK), jnp.float32, -2.0, 2.0) * block_scale(keys[4], (3, LEAVES * RANK), ((1, 128),), -0.4, 0.0), -2.0, 2.0)
    leaf_transfer = centred(keys[5], (RANK, LEAVES * RANK), RANK ** -0.5, 0.75, ((1, 128),), jnp.float32)
    mid_nodes = jnp.clip(jax.random.uniform(keys[6], (3, N_CLUS * RANK), jnp.float32, -2.0, 2.0) * block_scale(keys[6], (3, N_CLUS * RANK), ((1, 128),), -0.4, 0.0), -2.0, 2.0)
    mid_transfer = centred(keys[7], (RANK, N_CLUS * RANK), RANK ** -0.5, 0.75, ((1, 128),), jnp.float32)
    top_nodes = jnp.clip(jax.random.uniform(keys[8], (3, TOP * RANK), jnp.float32, -2.0, 2.0), -2.0, 2.0)
    near_list = draw_near_list(jax.random.fold_in(keys[14], 71), 0)
    near_count = draw_near_count(jax.random.fold_in(keys[14], 71), 0)
    far_list = draw_far_list(jax.random.fold_in(keys[14], 71), 0)
    mid_mask = set_ends((jax.random.randint(keys[12], (N_CLUS, N_CLUS), 0, 4) < 1).astype(jnp.int32), jax.random.fold_in(keys[12], 1), 0, 1)
    top_mask = set_ends((jax.random.randint(keys[13], (TOP, TOP), 0, 2) < 1).astype(jnp.int32), jax.random.fold_in(keys[13], 1), 0, 1)
    return {"charges": charges, "positions": positions, "quad_weights": quad_weights, "leaf_basis": leaf_basis, "leaf_nodes": leaf_nodes, "leaf_transfer": leaf_transfer, "mid_nodes": mid_nodes, "mid_transfer": mid_transfer, "top_nodes": top_nodes, "near_list": near_list, "near_count": near_count, "far_list": far_list, "mid_mask": mid_mask, "top_mask": top_mask}


smoothing = 0.05
inv_four_pi = 1.0 / (4.0 * math.pi)
highest = lax.Precision.HIGHEST

def green(source, target):
    first = source[0][..., :, None] - target[0][..., None, :]
    second = source[1][..., :, None] - target[1][..., None, :]
    third = source[2][..., :, None] - target[2][..., None, :]
    total = first * first + second * second + third * third
    return inv_four_pi / jnp.sqrt(total + smoothing * smoothing)

def reference(charges, positions, quad_weights, leaf_basis, leaf_nodes, leaf_transfer, mid_nodes, mid_transfer, top_nodes, near_list, near_count, far_list, mid_mask, top_mask):
    leaf_charges = charges.reshape(NRHS, LEAVES, LEAF)
    leaf_points = positions.reshape(3, LEAVES, LEAF)
    leaf_weights = quad_weights.reshape(LEAVES, LEAF)
    leaf_coef = jnp.einsum('rlb,lkb->rlk', leaf_charges, leaf_basis, precision=highest)
    block_coef = leaf_coef.reshape(NRHS, N_CLUS, LEAF_DEV * RANK)
    transfer_blocks = leaf_transfer.reshape(RANK, N_CLUS, LEAF_DEV * RANK)
    mid_coef = jnp.einsum('rpj,qpj->rpq', block_coef, transfer_blocks, precision=highest)
    mid_blocks = mid_transfer.reshape(RANK, N_CLUS, RANK)
    upward = jnp.einsum('rpk,qpk->rpq', mid_coef, mid_blocks, precision=highest)
    top_coef = upward.reshape(NRHS, TOP, GROUP, RANK).sum(axis=2).reshape(NRHS, TOP * RANK)
    top_kernel = green(top_nodes, top_nodes)
    top_select = jnp.repeat(jnp.repeat(top_mask.T.astype(jnp.float32), RANK, axis=0), RANK, axis=1)
    top_field = jnp.dot(top_coef, top_kernel * top_select, precision=highest).reshape(NRHS, TOP, RANK)
    mid_flat = mid_coef.reshape(NRHS, N_CLUS * RANK)

    def mid_one(cluster):
        target = lax.dynamic_slice_in_dim(mid_nodes, cluster * RANK, RANK, 1)
        select = jnp.repeat(mid_mask[cluster].astype(jnp.float32), RANK)[:, None]
        return jnp.dot(mid_flat, green(mid_nodes, target) * select, precision=highest)
    mid_field = jnp.transpose(lax.map(mid_one, jnp.arange(N_CLUS)), (1, 0, 2))
    top_down = jnp.repeat(top_field, GROUP, axis=1)
    mid_field = mid_field + jnp.einsum('rpq,qpk->rpk', top_down, mid_blocks, precision=highest)
    leaf_down = jnp.einsum('rpq,qpj->rpj', mid_field, transfer_blocks, precision=highest)
    leaf_down = leaf_down.reshape(NRHS, LEAVES, RANK)
    node_blocks = leaf_nodes.reshape(3, LEAVES, RANK)

    def block_work(block):
        first_leaf = block * LEAF_DEV
        far_rows = lax.dynamic_slice_in_dim(far_list, first_leaf, LEAF_DEV, 0)
        source_coef = jnp.take(leaf_coef, far_rows, axis=1)
        source_nodes = jnp.take(node_blocks, far_rows, axis=1)
        target_nodes = lax.dynamic_slice_in_dim(node_blocks, first_leaf, LEAF_DEV, 1)
        coupling = green(source_nodes, target_nodes[:, :, None, :])
        far_field = jnp.einsum('rlfj,lfji->rli', source_coef, coupling, precision=highest)
        far_field = far_field + lax.dynamic_slice_in_dim(leaf_down, first_leaf, LEAF_DEV, 1)
        own_basis = lax.dynamic_slice_in_dim(leaf_basis, first_leaf, LEAF_DEV, 0)
        far_out = jnp.einsum('rlk,lkb->rlb', far_field, own_basis, precision=highest)
        near_rows = lax.dynamic_slice_in_dim(near_list, first_leaf, LEAF_DEV, 0)
        counts = lax.dynamic_slice_in_dim(near_count, first_leaf, LEAF_DEV, 0)
        target_points = lax.dynamic_slice_in_dim(leaf_points, first_leaf, LEAF_DEV, 1)

        def slot(index, total):
            chosen = lax.dynamic_index_in_dim(near_rows, index, 1, keepdims=False)
            live = (index < counts).astype(jnp.float32)
            source_points = jnp.take(leaf_points, chosen, axis=1)
            weighted = jnp.take(leaf_weights, chosen, axis=0) * live[:, None]
            block_kernel = green(source_points, target_points) * weighted[:, :, None]
            source_charges = jnp.take(leaf_charges, chosen, axis=1)
            return total + jnp.einsum('rlb,lba->rla', source_charges, block_kernel, precision=highest)
        near_out = lax.fori_loop(0, NEAR_MAX, slot, jnp.zeros((NRHS, LEAF_DEV, LEAF), jnp.float32))
        return far_out + near_out
    result = lax.map(block_work, jnp.arange(N_CLUS))
    return jnp.transpose(result, (1, 0, 2, 3)).reshape(NRHS, POINTS)
```

```python
import functools
import math

import jax
import jax.numpy as jnp
from jax import lax
from jax.experimental import pallas as pl
from jax.experimental.pallas import tpu as pltpu
from jax.sharding import PartitionSpec as P

LEAF = 256
RANK = 64
NRHS = 32
LEAF_DEV = 32
NEAR_MAX = 27
FAR2 = 16
GROUP = 8

STEP = 4
LIST = 1024
FEAT = 64
UNROLL = 4

smoothing = 0.05
inv_four_pi = 1.0 / (4.0 * math.pi)
highest = lax.Precision.HIGHEST
bf16 = jnp.bfloat16
f32 = jnp.float32
NN = (((1,), (0,)), ((), ()))
NT = (((1,), (1,)), ((), ()))
SMEM = pl.BlockSpec(memory_space=pltpu.SMEM)
VMEM = pl.BlockSpec(memory_space=pltpu.VMEM)


def product(left, right, dims, precision=None):
    return lax.dot_general(left, right, dims, precision=precision, preferred_element_type=f32)


def green(source, target):
    first = source[0][..., :, None] - target[0][..., None, :]
    second = source[1][..., :, None] - target[1][..., None, :]
    third = source[2][..., :, None] - target[2][..., None, :]
    total = first * first + second * second + third * third
    return inv_four_pi / jnp.sqrt(total + smoothing * smoothing)


def source_rows(out, points):
    width = points.shape[1]
    out[0:3] = points
    out[3:4] = jnp.sum(points * points, axis=0, keepdims=True)
    out[4:5] = jnp.ones((1, width), f32)
    out[5:8] = jnp.zeros((3, width), f32)


def target_rows(out, points):
    width = points.shape[1]
    out[0:3] = points * -2.0
    out[3:4] = jnp.ones((1, width), f32)
    out[4:5] = jnp.sum(points * points, axis=0, keepdims=True) + smoothing * smoothing
    out[5:8] = jnp.zeros((3, width), f32)


def three(rows):
    first = rows.astype(bf16).astype(f32)
    rest = rows - first
    second = rest.astype(bf16).astype(f32)
    third = (rest - second).astype(bf16).astype(f32)
    return first, second, third


def source_features(rows):
    a, b, c = three(rows)
    return jnp.concatenate([a, a, b, a, c, b, b, c], axis=0)


def target_features(rows):
    a, b, c = three(rows)
    return jnp.concatenate([a, b, a, c, a, b, c, b], axis=0)


def two(values):
    high = values.astype(bf16)
    low = (values - high.astype(f32)).astype(bf16)
    return high, low


def upward_kernel(
    code_ref,
    charges_ref,
    points_ref,
    weights_ref,
    basis_ref,
    nodes_ref,
    transfer_ref,
    mid_nodes_ref,
    mid_transfer_ref,
    pack_ref,
    target_ref,
    coef_ref,
    node_target_ref,
    level_ref,
    list_ref,
    total,
    counts,
):
    step = pl.program_id(0)

    @pl.when(step == 0)
    def _():
        total[...] = jnp.zeros_like(total)
        counts[0] = 0

    charges = charges_ref[...]
    points = points_ref[...]
    pack_ref[0:NRHS] = charges * (weights_ref[...] * inv_four_pi)
    source_rows(pack_ref.at[NRHS : NRHS + 8], points)
    target_rows(target_ref, points)
    for leaf in range(STEP):
        own = charges[:, leaf * LEAF : (leaf + 1) * LEAF]
        coef = product(own, basis_ref[leaf], NT, highest)
        coef_ref[0:NRHS, leaf * RANK : (leaf + 1) * RANK] = coef
    source_rows(coef_ref.at[NRHS : NRHS + 8], nodes_ref[...])
    target_rows(node_target_ref, nodes_ref[...])
    total[...] += product(coef_ref[0:NRHS], transfer_ref[...], NT, highest)

    count = counts[0]
    for slot in range(STEP * NEAR_MAX):
        code = code_ref[step * (STEP * NEAR_MAX) + slot]
        shift = lax.shift_right_logical(code, 12) & 31
        place = lax.shift_right_logical(count, shift) & (LIST - 1)
        list_ref[lax.shift_left(lax.shift_right_logical(code, 17), 10) + place] = code
        count = count + lax.shift_left(1, shift)
    counts[0] = count

    @pl.when(step == pl.num_programs(0) - 1)
    def _():
        mid_coef = total[...]
        level_ref[0:NRHS] = mid_coef
        level_ref[NRHS : 2 * NRHS] = product(mid_coef, mid_transfer_ref[...], NT, highest)
        source_rows(level_ref.at[2 * NRHS : 2 * NRHS + 8], mid_nodes_ref[...])
        for phase in range(3):
            number = lax.shift_right_logical(count, 10 * phase) & (LIST - 1)
            for spare in range(8):
                list_ref[phase * LIST + number + spare] = LEAF_DEV * 64
            list_ref[phase * LIST + LIST - 1] = number


def upward(codes, charges, points, weights, basis, nodes, transfer, mid_nodes, mid_transfer):
    lanes = lambda rows, width: pl.BlockSpec((rows, width), lambda i: (0, i))
    fixed = lambda rows, width: pl.BlockSpec((rows, width), lambda i: (0, 0))
    wide, narrow = STEP * LEAF, STEP * RANK
    shape = jax.ShapeDtypeStruct
    return pl.pallas_call(
        upward_kernel,
        grid=(LEAF_DEV // STEP,),
        in_specs=[
            SMEM,
            lanes(NRHS, wide),
            lanes(3, wide),
            lanes(1, wide),
            pl.BlockSpec((STEP, RANK, LEAF), lambda i: (i, 0, 0)),
            lanes(3, narrow),
            lanes(RANK, narrow),
            fixed(3, RANK),
            fixed(RANK, RANK),
        ],
        out_specs=[
            lanes(NRHS + 8, wide),
            lanes(8, wide),
            lanes(NRHS + 8, narrow),
            lanes(8, narrow),
            fixed(2 * NRHS + 8, RANK),
            SMEM,
        ],
        out_shape=[
            shape((NRHS + 8, LEAF_DEV * LEAF), f32),
            shape((8, LEAF_DEV * LEAF), f32),
            shape((NRHS + 8, LEAF_DEV * RANK), f32),
            shape((8, LEAF_DEV * RANK), f32),
            shape((2 * NRHS + 8, RANK), f32),
            shape((4 * LIST,), jnp.int32),
        ],
        scratch_shapes=[pltpu.VMEM((NRHS, RANK), f32), pltpu.SMEM((1,), jnp.int32)],
        name="upward",
    )(codes, charges, points, weights, basis, nodes, transfer, mid_nodes, mid_transfer)


def near_kernel(phase, list_ref, pack_ref, target_ref, *refs):
    if phase == 0:
        (out_ref, source, target, sides, squares, highs, lows) = refs
        out_ref[...] = jnp.zeros_like(out_ref)
    else:
        (before_ref, out_ref, source, target, sides, squares, highs, lows) = refs
        out_ref[...] = before_ref[...]

    def prepare(leaf, _):
        start = pl.multiple_of(leaf * LEAF, LEAF)
        features = source_features(pack_ref[NRHS : NRHS + 8, pl.ds(start, LEAF)])
        source[leaf] = features.T.astype(bf16)
        target[leaf] = target_features(target_ref[:, pl.ds(start, LEAF)]).astype(bf16)
        high, low = two(pack_ref[0:NRHS, pl.ds(start, LEAF)])
        sides[leaf, 0:NRHS] = high
        sides[leaf, NRHS : 2 * NRHS] = low
        return 0

    lax.fori_loop(0, LEAF_DEV, prepare, 0)

    def item(index):
        code = list_ref[phase * LIST + index]
        return lax.shift_right_logical(code, 6) & 63, code & 63

    def distances(index, slot):
        to, of = item(index)
        squares[slot] = product(source[of], target[to], NN)

    def values(slot):
        for row in range(0, LEAF, 64):
            high, low = two(lax.rsqrt(squares[slot, row : row + 64]))
            highs[slot, row : row + 64] = high
            lows[slot, row : row + 64] = low

    def apply(index, slot):
        to, of = item(index)
        upper = product(sides[of], highs[slot], NN)
        lower = product(sides[of, 0:NRHS], lows[slot], NN)
        out_ref[to] += upper[0:NRHS] + upper[NRHS : 2 * NRHS] + lower

    distances(0, 0)
    distances(1, 1)
    values(0)

    def step(number, _):
        for part in range(UNROLL):
            index = number * UNROLL + part
            apply(index, part % 2)
            values((part + 1) % 2)
            distances(index + 2, part % 2)
        return 0

    length = list_ref[phase * LIST + LIST - 1]
    lax.fori_loop(0, lax.div(length + (UNROLL - 1), UNROLL), step, 0)


def near(phase, lists, pack, targets, before):
    operands = (lists, pack, targets) + (() if before is None else (before,))
    rows = LEAF_DEV + 1
    return pl.pallas_call(
        functools.partial(near_kernel, phase),
        in_specs=[SMEM] + [VMEM] * (len(operands) - 1),
        out_specs=VMEM,
        out_shape=jax.ShapeDtypeStruct((rows, NRHS, LEAF), f32),
        scratch_shapes=[
            pltpu.VMEM((LEAF_DEV, LEAF, FEAT), bf16),
            pltpu.VMEM((rows, FEAT, LEAF), bf16),
            pltpu.VMEM((LEAF_DEV, 2 * NRHS, LEAF), bf16),
            pltpu.VMEM((2, LEAF, LEAF), f32),
            pltpu.VMEM((2, LEAF, LEAF), bf16),
            pltpu.VMEM((2, LEAF, LEAF), bf16),
        ],
        compiler_params=pltpu.CompilerParams(vmem_limit_bytes=40 * 2**20),
        cost_estimate=pl.CostEstimate(flops=20_000_000_000, bytes_accessed=4_000_000, transcendentals=14_000_000),
        name="near" + str(phase),
    )(*operands)


def final_kernel(near_ref, field_ref, basis_ref, out_ref):
    for leaf in range(STEP):
        field = field_ref[:, leaf * RANK : (leaf + 1) * RANK]
        far = product(field, basis_ref[leaf], NN, highest)
        out_ref[:, leaf * LEAF : (leaf + 1) * LEAF] = far + near_ref[leaf]


def final(near_out, field, basis):
    return pl.pallas_call(
        final_kernel,
        grid=(LEAF_DEV // STEP,),
        in_specs=[
            pl.BlockSpec((STEP, NRHS, LEAF), lambda i: (i, 0, 0)),
            pl.BlockSpec((NRHS, STEP * RANK), lambda i: (0, i)),
            pl.BlockSpec((STEP, RANK, LEAF), lambda i: (i, 0, 0)),
        ],
        out_specs=pl.BlockSpec((NRHS, STEP * LEAF), lambda i: (0, i)),
        out_shape=jax.ShapeDtypeStruct((NRHS, LEAF_DEV * LEAF), f32),
        name="final",
    )(near_out, field, basis)


def shards(
    charges,
    positions,
    quad_weights,
    leaf_basis,
    leaf_nodes,
    leaf_transfer,
    mid_nodes,
    mid_transfer,
    top_nodes,
    near_list,
    near_count,
    far_list,
    mid_mask,
    top_mask,
):
    devices = lax.axis_size("clus")
    myself = lax.axis_index("clus")
    top_count = devices // GROUP
    partner = [(i, i ^ 1) for i in range(devices)]
    cross = [(i, (i + 1 if i % 2 else i - 1) % devices) for i in range(devices)]
    partner_step = jnp.where(myself % 2 == 0, 1, devices - 1)

    def phase_of(leaves):
        away = (leaves // LEAF_DEV - myself) % devices
        return jnp.where(away == 0, 0, jnp.where(away == partner_step, 1, 2))

    live = jnp.arange(NEAR_MAX)[None, :] < near_count[:, None]
    phase = jnp.where(live, phase_of(near_list), 3)
    leaf_row = jnp.arange(LEAF_DEV, dtype=jnp.int32)[:, None]
    codes = (phase << 17) | ((10 * phase) << 12) | (leaf_row << 6) | (near_list % LEAF_DEV)

    pack, targets, coef, node_targets, level, lists = upward(
        codes.reshape(-1).astype(jnp.int32),
        charges,
        positions,
        quad_weights.reshape(1, -1),
        leaf_basis,
        leaf_nodes,
        leaf_transfer,
        mid_nodes,
        mid_transfer,
    )
    pack_partner = lax.ppermute(pack, "clus", partner)
    coef_partner = lax.ppermute(coef, "clus", partner)
    pack_cross = lax.ppermute(pack, "clus", cross)
    coef_cross = lax.ppermute(coef, "clus", cross)
    everyone = lax.all_gather(level, "clus", axis=0, tiled=False)

    near_out = near(0, lists, pack, targets, None)
    near_out = near(1, lists, pack_partner, targets, near_out)
    near_out = near(2, lists, pack_cross, targets, near_out)

    flat = jnp.transpose(everyone, (1, 0, 2)).reshape(2 * NRHS + 8, devices * RANK)
    all_coef = flat[:NRHS]
    all_nodes = flat[2 * NRHS : 2 * NRHS + 3]
    upward_sum = everyone[:, NRHS : 2 * NRHS].reshape(top_count, GROUP, NRHS, RANK).sum(axis=1)
    top_coef = jnp.transpose(upward_sum, (1, 0, 2)).reshape(NRHS, top_count * RANK)
    parent = myself // GROUP
    top_target = lax.dynamic_slice_in_dim(top_nodes, parent * RANK, RANK, 1)
    top_row = lax.dynamic_index_in_dim(top_mask, parent, 0, keepdims=False)
    top_select = jnp.repeat(top_row.astype(f32), RANK)[:, None]
    top_field = jnp.dot(top_coef, green(top_nodes, top_target) * top_select, precision=highest)
    mid_select = jnp.repeat(mid_mask[0].astype(f32), RANK)[:, None]
    mid_field = jnp.dot(all_coef, green(all_nodes, mid_nodes) * mid_select, precision=highest)
    mid_field = mid_field + jnp.dot(top_field, mid_transfer, precision=highest)
    leaf_down = jnp.dot(mid_field, leaf_transfer, precision=highest).reshape(NRHS, LEAF_DEV, RANK)

    window = jnp.concatenate([coef, coef_partner, coef_cross], axis=1)
    window = window.reshape(NRHS + 8, 3 * LEAF_DEV, RANK)
    far_local = phase_of(far_list) * LEAF_DEV + far_list % LEAF_DEV
    picked = jnp.take(window, far_local, axis=1)
    target_nodes = leaf_nodes.reshape(3, LEAF_DEV, RANK)
    coupling = green(picked[NRHS : NRHS + 3], target_nodes[:, :, None, :])
    field = jnp.einsum("rlfj,lfji->rli", picked[:NRHS], coupling, precision=highest) + leaf_down
    return final(near_out, field.reshape(NRHS, LEAF_DEV * RANK), leaf_basis)


def solution(mesh):
    in_specs = (
        P(None, "clus"),
        P(None, "clus"),
        P("clus"),
        P("clus", None, None),
        P(None, "clus"),
        P(None, "clus"),
        P(None, "clus"),
        P(None, "clus"),
        P(),
        P("clus", None),
        P("clus"),
        P("clus", None),
        P("clus", None),
        P(),
    )
    out_specs = P(None, "clus")
    return jax.shard_map(shards, mesh=mesh, in_specs=in_specs, out_specs=out_specs, check_vma=False)
```

```python
import functools
import math

import jax
import jax.numpy as jnp
from jax import lax
from jax.experimental import pallas as pl
from jax.experimental.pallas import tpu as pltpu
from jax.sharding import PartitionSpec as P

LEAF = 256
RANK = 64
NRHS = 32
LEAF_DEV = 32
NEAR_MAX = 27
FAR2 = 16
GROUP = 8

STEP = 4
LIST = 1024
FEAT = 64
UNROLL = 4

smoothing = 0.05
inv_four_pi = 1.0 / (4.0 * math.pi)
highest = lax.Precision.HIGHEST
bf16 = jnp.bfloat16
f32 = jnp.float32
NN = (((1,), (0,)), ((), ()))
NT = (((1,), (1,)), ((), ()))
SMEM = pl.BlockSpec(memory_space=pltpu.SMEM)
VMEM = pl.BlockSpec(memory_space=pltpu.VMEM)


def product(left, right, dims, precision=None):
    return lax.dot_general(left, right, dims, precision=precision, preferred_element_type=f32)


def source_rows(out, points):
    width = points.shape[1]
    out[0:3] = points
    out[3:4] = jnp.sum(points * points, axis=0, keepdims=True)
    out[4:5] = jnp.ones((1, width), f32)
    out[5:8] = jnp.zeros((3, width), f32)


def target_rows(out, points):
    width = points.shape[1]
    out[0:3] = points * -2.0
    out[3:4] = jnp.ones((1, width), f32)
    out[4:5] = jnp.sum(points * points, axis=0, keepdims=True) + smoothing * smoothing
    out[5:8] = jnp.zeros((3, width), f32)


def three(rows):
    first = rows.astype(bf16).astype(f32)
    rest = rows - first
    second = rest.astype(bf16).astype(f32)
    third = (rest - second).astype(bf16).astype(f32)
    return first, second, third


def source_features(rows):
    a, b, c = three(rows)
    return jnp.concatenate([a, a, b, a, c, b, b, c], axis=0)


def target_features(rows):
    a, b, c = three(rows)
    return jnp.concatenate([a, b, a, c, a, b, c, b], axis=0)


def two(values):
    high = values.astype(bf16)
    low = (values - high.astype(f32)).astype(bf16)
    return high, low


def upward_kernel(
    code_ref,
    charges_ref,
    points_ref,
    weights_ref,
    basis_ref,
    nodes_ref,
    transfer_ref,
    mid_nodes_ref,
    mid_transfer_ref,
    pack_ref,
    target_ref,
    coef_ref,
    node_target_ref,
    level_ref,
    list_ref,
    total,
    counts,
):
    step = pl.program_id(0)

    @pl.when(step == 0)
    def _():
        total[...] = jnp.zeros_like(total)
        counts[0] = 0

    charges = charges_ref[...]
    points = points_ref[...]
    pack_ref[0:NRHS] = charges * (weights_ref[...] * inv_four_pi)
    source_rows(pack_ref.at[NRHS : NRHS + 8], points)
    target_rows(target_ref, points)
    for leaf in range(STEP):
        own = charges[:, leaf * LEAF : (leaf + 1) * LEAF]
        coef = product(own, basis_ref[leaf], NT, highest)
        coef_ref[0:NRHS, leaf * RANK : (leaf + 1) * RANK] = coef
    source_rows(coef_ref.at[NRHS : NRHS + 8], nodes_ref[...])
    target_rows(node_target_ref, nodes_ref[...])
    total[...] += product(coef_ref[0:NRHS], transfer_ref[...], NT, highest)

    count = counts[0]
    for slot in range(STEP * NEAR_MAX):
        code = code_ref[step * (STEP * NEAR_MAX) + slot]
        shift = lax.shift_right_logical(code, 12) & 31
        place = lax.shift_right_logical(count, shift) & (LIST - 1)
        list_ref[lax.shift_left(lax.shift_right_logical(code, 17), 10) + place] = code
        count = count + lax.shift_left(1, shift)
    counts[0] = count

    @pl.when(step == pl.num_programs(0) - 1)
    def _():
        mid_coef = total[...]
        level_ref[0:NRHS] = mid_coef
        level_ref[NRHS : 2 * NRHS] = product(mid_coef, mid_transfer_ref[...], NT, highest)
        source_rows(level_ref.at[2 * NRHS : 2 * NRHS + 8], mid_nodes_ref[...])
        for phase in range(3):
            number = lax.shift_right_logical(count, 10 * phase) & (LIST - 1)
            for spare in range(8):
                list_ref[phase * LIST + number + spare] = LEAF_DEV * 64
            list_ref[phase * LIST + LIST - 1] = number


def upward(codes, charges, points, weights, basis, nodes, transfer, mid_nodes, mid_transfer):
    lanes = lambda rows, width: pl.BlockSpec((rows, width), lambda i: (0, i))
    fixed = lambda rows, width: pl.BlockSpec((rows, width), lambda i: (0, 0))
    wide, narrow = STEP * LEAF, STEP * RANK
    shape = jax.ShapeDtypeStruct
    return pl.pallas_call(
        upward_kernel,
        grid=(LEAF_DEV // STEP,),
        in_specs=[
            SMEM,
            lanes(NRHS, wide),
            lanes(3, wide),
            lanes(1, wide),
            pl.BlockSpec((STEP, RANK, LEAF), lambda i: (i, 0, 0)),
            lanes(3, narrow),
            lanes(RANK, narrow),
            fixed(3, RANK),
            fixed(RANK, RANK),
        ],
        out_specs=[
            lanes(NRHS + 8, wide),
            lanes(8, wide),
            lanes(NRHS + 8, narrow),
            lanes(8, narrow),
            fixed(2 * NRHS + 8, RANK),
            SMEM,
        ],
        out_shape=[
            shape((NRHS + 8, LEAF_DEV * LEAF), f32),
            shape((8, LEAF_DEV * LEAF), f32),
            shape((NRHS + 8, LEAF_DEV * RANK), f32),
            shape((8, LEAF_DEV * RANK), f32),
            shape((2 * NRHS + 8, RANK), f32),
            shape((4 * LIST,), jnp.int32),
        ],
        scratch_shapes=[pltpu.VMEM((NRHS, RANK), f32), pltpu.SMEM((1,), jnp.int32)],
        name="upward",
    )(codes, charges, points, weights, basis, nodes, transfer, mid_nodes, mid_transfer)


def near_kernel(phase, list_ref, pack_ref, target_ref, *refs):
    if phase == 0:
        (out_ref, source, target, sides, squares, highs, lows) = refs
        out_ref[...] = jnp.zeros_like(out_ref)
    else:
        (before_ref, out_ref, source, target, sides, squares, highs, lows) = refs
        out_ref[...] = before_ref[...]

    def prepare(leaf, _):
        start = pl.multiple_of(leaf * LEAF, LEAF)
        features = source_features(pack_ref[NRHS : NRHS + 8, pl.ds(start, LEAF)])
        source[leaf] = features.T.astype(bf16)
        target[leaf] = target_features(target_ref[:, pl.ds(start, LEAF)]).astype(bf16)
        high, low = two(pack_ref[0:NRHS, pl.ds(start, LEAF)])
        sides[leaf, 0:NRHS] = high
        sides[leaf, NRHS : 2 * NRHS] = low
        return 0

    lax.fori_loop(0, LEAF_DEV, prepare, 0)

    def item(index):
        code = list_ref[phase * LIST + index]
        return lax.shift_right_logical(code, 6) & 63, code & 63

    def distances(index, slot):
        to, of = item(index)
        squares[slot] = product(source[of], target[to], NN)

    def values(slot):
        for row in range(0, LEAF, 64):
            high, low = two(lax.rsqrt(squares[slot, row : row + 64]))
            highs[slot, row : row + 64] = high
            lows[slot, row : row + 64] = low

    def apply(index, slot):
        to, of = item(index)
        upper = product(sides[of], highs[slot], NN)
        lower = product(sides[of, 0:NRHS], lows[slot], NN)
        out_ref[to] += upper[0:NRHS] + upper[NRHS : 2 * NRHS] + lower

    distances(0, 0)
    distances(1, 1)
    values(0)

    def step(number, _):
        for part in range(UNROLL):
            index = number * UNROLL + part
            apply(index, part % 2)
            values((part + 1) % 2)
            distances(index + 2, part % 2)
        return 0

    length = list_ref[phase * LIST + LIST - 1]
    lax.fori_loop(0, lax.div(length + (UNROLL - 1), UNROLL), step, 0)


def near(phase, lists, pack, targets, before):
    operands = (lists, pack, targets) + (() if before is None else (before,))
    rows = LEAF_DEV + 1
    return pl.pallas_call(
        functools.partial(near_kernel, phase),
        in_specs=[SMEM] + [VMEM] * (len(operands) - 1),
        out_specs=VMEM,
        out_shape=jax.ShapeDtypeStruct((rows, NRHS, LEAF), f32),
        scratch_shapes=[
            pltpu.VMEM((LEAF_DEV, LEAF, FEAT), bf16),
            pltpu.VMEM((rows, FEAT, LEAF), bf16),
            pltpu.VMEM((LEAF_DEV, 2 * NRHS, LEAF), bf16),
            pltpu.VMEM((2, LEAF, LEAF), f32),
            pltpu.VMEM((2, LEAF, LEAF), bf16),
            pltpu.VMEM((2, LEAF, LEAF), bf16),
        ],
        compiler_params=pltpu.CompilerParams(vmem_limit_bytes=40 * 2**20),
        cost_estimate=pl.CostEstimate(flops=20_000_000_000, bytes_accessed=4_000_000, transcendentals=14_000_000),
        name="near" + str(phase),
    )(*operands)


def couple(coefs, rows, targets):
    squares = product(targets, source_features(rows).astype(bf16), NN)
    high, low = two(lax.rsqrt(squares))
    side, rest = two(coefs)
    both = product(jnp.concatenate([side, rest], axis=0), high, NT)
    return both[0:NRHS] + both[NRHS : 2 * NRHS] + product(side, low, NT)


def mid_kernel(
    mid_row_ref, top_row_ref, level_ref, top_nodes_ref, top_target_ref, mid_nodes_ref, mid_transfer_ref, transfer_ref, out_ref, rows, tops
):
    def features(nodes):
        target_rows(rows, nodes)
        return target_features(rows[...]).T.astype(bf16)

    source_rows(tops, top_nodes_ref[...])
    top_targets = features(top_target_ref[...])
    top_field = jnp.zeros((NRHS, RANK), f32)
    for first in range(0, top_nodes_ref.shape[1] // RANK, 4):
        coefs = []
        for top in range(first, first + 4):
            coef = level_ref[top * GROUP, NRHS : 2 * NRHS]
            for member in range(1, GROUP):
                coef = coef + level_ref[top * GROUP + member, NRHS : 2 * NRHS]
            coefs.append(coef * top_row_ref[top].astype(f32))
        picked = tops[:, first * RANK : (first + 4) * RANK]
        top_field = top_field + couple(jnp.concatenate(coefs, axis=1), picked, top_targets)
    mid_targets = features(mid_nodes_ref[...])

    def step(number, total):
        first = number * 4
        coefs = [level_ref[first + k, 0:NRHS] * mid_row_ref[first + k].astype(f32) for k in range(4)]
        picked = [level_ref[first + k, 2 * NRHS : 2 * NRHS + 8] for k in range(4)]
        return total + couple(jnp.concatenate(coefs, axis=1), jnp.concatenate(picked, axis=1), mid_targets)

    field = lax.fori_loop(0, level_ref.shape[0] // 4, step, jnp.zeros((NRHS, RANK), f32))
    field = field * inv_four_pi + product(top_field * inv_four_pi, mid_transfer_ref[...], NN, highest)
    out_ref[...] = product(field, transfer_ref[...], NN, highest)


def mid(mid_row, top_row, levels, top_nodes, top_target, mid_nodes, mid_transfer, transfer):
    return pl.pallas_call(
        mid_kernel,
        in_specs=[SMEM, SMEM] + [VMEM] * 6,
        out_specs=VMEM,
        out_shape=jax.ShapeDtypeStruct((NRHS, LEAF_DEV * RANK), f32),
        scratch_shapes=[pltpu.VMEM((8, RANK), f32), pltpu.VMEM((8, top_nodes.shape[1]), f32)],
        compiler_params=pltpu.CompilerParams(vmem_limit_bytes=40 * 2**20),
        name="mid",
    )(mid_row, top_row, levels, top_nodes, top_target, mid_nodes, mid_transfer, transfer)


def far_kernel(
    far_ref, own_ref, partner_ref, cross_ref, node_target_ref, down_ref, near_ref, basis_ref, out_ref, nodes_low, nodes_high, coef_low, coef_high
):
    quad = pl.program_id(0)
    lower = lax.broadcasted_iota(jnp.int32, (1, 2 * RANK), 1) < RANK

    @pl.when(quad == 0)
    def _():
        for phase, ref in enumerate((own_ref, partner_ref, cross_ref)):

            def prepare(pair, _):
                lanes = pl.ds(pl.multiple_of(pair * 2 * RANK, 2 * RANK), 2 * RANK)
                features = source_features(ref[NRHS : NRHS + 8, lanes])
                turned = jnp.concatenate([features, features], axis=0).T
                coef = ref[0:NRHS, lanes]
                swapped = pltpu.roll(coef, RANK, 1)
                for half in range(2):
                    leaf = phase * LEAF_DEV + 2 * pair + half
                    node = turned[half * RANK : (half + 1) * RANK]
                    nodes_low[leaf] = jnp.where(lower, node, 0.0).astype(bf16)
                    nodes_high[leaf] = jnp.where(lower, 0.0, node).astype(bf16)
                    left, right = (coef, swapped) if half == 0 else (swapped, coef)
                    for store, values in ((coef_low, jnp.where(lower, left, 0.0)), (coef_high, jnp.where(lower, 0.0, right))):
                        high, low = two(values)
                        store[leaf, 0:NRHS] = high
                        store[leaf, NRHS : 2 * NRHS] = low
                return 0

            lax.fori_loop(0, LEAF_DEV // 2, prepare, 0)

    block = lax.broadcasted_iota(jnp.int32, (1, 4 * RANK), 1) // RANK
    features = target_features(node_target_ref[...])
    weights = jnp.concatenate([jnp.where(block == k, features, 0.0) for k in range(4)], axis=0).astype(bf16)
    total = jnp.zeros((8 * NRHS, 4 * RANK), f32)
    extra = jnp.zeros((4 * NRHS, 4 * RANK), f32)
    for chunk in range(FAR2 // 4):
        leaves = [[far_ref[(quad * 4 + k) * FAR2 + chunk * 4 + f] for f in range(4)] for k in range(4)]
        parts = []
        for f in range(4):
            one = nodes_low[leaves[0][f]] + nodes_high[leaves[1][f]]
            other = nodes_low[leaves[2][f]] + nodes_high[leaves[3][f]]
            parts.append(jnp.concatenate([one, other], axis=1))
        squares = product(jnp.concatenate(parts, axis=0), weights, NN)
        high, low = two(lax.rsqrt(squares))
        sides = []
        for k in range(4):
            one = coef_low[leaves[k][0]] + coef_high[leaves[k][1]]
            other = coef_low[leaves[k][2]] + coef_high[leaves[k][3]]
            sides.append(jnp.concatenate([one, other], axis=1))
        total = total + product(jnp.concatenate(sides, axis=0), high, NN)
        extra = extra + product(jnp.concatenate([side[0:NRHS] for side in sides], axis=0), low, NN)
    field = jnp.zeros((NRHS, 4 * RANK), f32)
    for k in range(4):
        own = total[2 * k * NRHS : (2 * k + 1) * NRHS] + total[(2 * k + 1) * NRHS : (2 * k + 2) * NRHS]
        field = jnp.where(block == k, own + extra[k * NRHS : (k + 1) * NRHS], field)
    field = field * inv_four_pi + down_ref[...]
    for leaf in range(4):
        own = field[:, leaf * RANK : (leaf + 1) * RANK]
        high, low = two(own)
        basis, rest = two(basis_ref[leaf])
        both = product(jnp.concatenate([high, low], axis=0), basis, NN)
        far = both[0:NRHS] + both[NRHS : 2 * NRHS] + product(high, rest, NN)
        out_ref[:, leaf * LEAF : (leaf + 1) * LEAF] = far + near_ref[leaf]


def far(far_codes, own, partner, cross, node_targets, down, near_out, basis):
    leaves = 3 * LEAF_DEV
    return pl.pallas_call(
        far_kernel,
        grid=(LEAF_DEV // 4,),
        in_specs=[
            SMEM,
            VMEM,
            VMEM,
            VMEM,
            pl.BlockSpec((8, 4 * RANK), lambda i: (0, i)),
            pl.BlockSpec((NRHS, 4 * RANK), lambda i: (0, i)),
            pl.BlockSpec((4, NRHS, LEAF), lambda i: (i, 0, 0)),
            pl.BlockSpec((4, RANK, LEAF), lambda i: (i, 0, 0)),
        ],
        out_specs=pl.BlockSpec((NRHS, 4 * LEAF), lambda i: (0, i)),
        out_shape=jax.ShapeDtypeStruct((NRHS, LEAF_DEV * LEAF), f32),
        scratch_shapes=[pltpu.VMEM((leaves, RANK, 2 * RANK), bf16)] * 4,
        compiler_params=pltpu.CompilerParams(vmem_limit_bytes=40 * 2**20),
        name="far",
    )(far_codes, own, partner, cross, node_targets, down, near_out, basis)


def shards(
    charges,
    positions,
    quad_weights,
    leaf_basis,
    leaf_nodes,
    leaf_transfer,
    mid_nodes,
    mid_transfer,
    top_nodes,
    near_list,
    near_count,
    far_list,
    mid_mask,
    top_mask,
):
    devices = lax.axis_size("clus")
    myself = lax.axis_index("clus")
    partner = [(i, i ^ 1) for i in range(devices)]
    cross = [(i, (i + 1 if i % 2 else i - 1) % devices) for i in range(devices)]
    partner_step = jnp.where(myself % 2 == 0, 1, devices - 1)

    def phase_of(leaves):
        away = (leaves // LEAF_DEV - myself) % devices
        return jnp.where(away == 0, 0, jnp.where(away == partner_step, 1, 2))

    live = jnp.arange(NEAR_MAX)[None, :] < near_count[:, None]
    phase = jnp.where(live, phase_of(near_list), 3)
    leaf_row = jnp.arange(LEAF_DEV, dtype=jnp.int32)[:, None]
    codes = (phase << 17) | ((10 * phase) << 12) | (leaf_row << 6) | (near_list % LEAF_DEV)

    pack, targets, coef, node_targets, level, lists = upward(
        codes.reshape(-1).astype(jnp.int32),
        charges,
        positions,
        quad_weights.reshape(1, -1),
        leaf_basis,
        leaf_nodes,
        leaf_transfer,
        mid_nodes,
        mid_transfer,
    )
    pack_partner = lax.ppermute(pack, "clus", partner)
    coef_partner = lax.ppermute(coef, "clus", partner)
    pack_cross = lax.ppermute(pack, "clus", cross)
    coef_cross = lax.ppermute(coef, "clus", cross)
    everyone = lax.all_gather(level, "clus", axis=0, tiled=False)

    near_out = near(0, lists, pack, targets, None)
    near_out = near(1, lists, pack_partner, targets, near_out)
    near_out = near(2, lists, pack_cross, targets, near_out)

    parent = myself // GROUP
    top_target = lax.dynamic_slice_in_dim(top_nodes, parent * RANK, RANK, 1)
    top_row = lax.dynamic_index_in_dim(top_mask, parent, 0, keepdims=False)
    down = mid(mid_mask[0], top_row, everyone, top_nodes, top_target, mid_nodes, mid_transfer, leaf_transfer)
    far_codes = (phase_of(far_list) * LEAF_DEV + far_list % LEAF_DEV).reshape(-1).astype(jnp.int32)
    return far(far_codes, coef, coef_partner, coef_cross, node_targets, down, near_out, leaf_basis)


def solution(mesh):
    in_specs = (
        P(None, "clus"),
        P(None, "clus"),
        P("clus"),
        P("clus", None, None),
        P(None, "clus"),
        P(None, "clus"),
        P(None, "clus"),
        P(None, "clus"),
        P(),
        P("clus", None),
        P("clus"),
        P("clus", None),
        P("clus", None),
        P(),
    )
    out_specs = P(None, "clus")
    return jax.shard_map(shards, mesh=mesh, in_specs=in_specs, out_specs=out_specs, check_vma=False)
```

```python
import functools
import math

import jax
import jax.numpy as jnp
from jax import lax
from jax.experimental import pallas as pl
from jax.experimental.pallas import tpu as pltpu
from jax.sharding import PartitionSpec as P

LEAF = 256
RANK = 64
NRHS = 32
LEAF_DEV = 32
NEAR_MAX = 27
FAR2 = 16
GROUP = 8

STEP = 4
LIST = 1024
FEAT = 64
UNROLL = 16

smoothing = 0.05
inv_four_pi = 1.0 / (4.0 * math.pi)
highest = lax.Precision.HIGHEST
bf16 = jnp.bfloat16
f32 = jnp.float32
NN = (((1,), (0,)), ((), ()))
NT = (((1,), (1,)), ((), ()))
LIMIT = pltpu.CompilerParams(vmem_limit_bytes=56 * 2**20)
SMEM = pl.BlockSpec(memory_space=pltpu.SMEM)


def product(left, right, dims, precision=None):
    return lax.dot_general(left, right, dims, precision=precision, preferred_element_type=f32)


def source_rows(out, points):
    width = points.shape[1]
    out[0:3] = points
    out[3:4] = jnp.sum(points * points, axis=0, keepdims=True)
    out[4:5] = jnp.ones((1, width), f32)
    out[5:8] = jnp.zeros((3, width), f32)


def target_rows(out, points):
    width = points.shape[1]
    out[0:3] = points * -2.0
    out[3:4] = jnp.ones((1, width), f32)
    out[4:5] = jnp.sum(points * points, axis=0, keepdims=True) + smoothing * smoothing
    out[5:8] = jnp.zeros((3, width), f32)


def three(rows):
    first = rows.astype(bf16).astype(f32)
    rest = rows - first
    second = rest.astype(bf16).astype(f32)
    third = (rest - second).astype(bf16).astype(f32)
    return first, second, third


def source_features(rows):
    a, b, c = three(rows)
    return jnp.concatenate([a, a, b, a, c, b, b, c], axis=0)


def target_features(rows):
    a, b, c = three(rows)
    return jnp.concatenate([a, b, a, c, a, b, c, b], axis=0)


def two(values):
    high = values.astype(bf16)
    low = (values - high.astype(f32)).astype(bf16)
    return high, low


def fine(left, right, dims):
    rows = left.shape[0]
    high, low = two(left)
    near_high, near_low = two(right)
    both = product(jnp.concatenate([high, low], axis=0), near_high, dims)
    return both[0:rows] + both[rows : 2 * rows] + product(high, near_low, dims)


def whole(array):
    zeros = (0,) * array.ndim
    return pl.BlockSpec(array.shape, lambda i: zeros)


def upward_kernel(
    code_ref,
    add_ref,
    charges_ref,
    points_ref,
    weights_ref,
    basis_ref,
    nodes_ref,
    transfer_ref,
    mid_nodes_ref,
    mid_transfer_ref,
    pack_ref,
    target_ref,
    coef_ref,
    node_target_ref,
    level_ref,
    list_ref,
    total,
    mid_rows,
    counts,
):
    step = pl.program_id(0)

    @pl.when(step == 0)
    def _():
        total[...] = jnp.zeros_like(total)
        counts[0] = LIST << 16

    charges = charges_ref[...]
    points = points_ref[...]
    pack_ref[0:NRHS] = charges * (weights_ref[...] * inv_four_pi)
    source_rows(pack_ref.at[NRHS : NRHS + 8], points)
    target_rows(target_ref, points)
    coefs = [fine(charges[:, k * LEAF : (k + 1) * LEAF], basis_ref[k], NT) for k in range(STEP)]
    coef = jnp.concatenate(coefs, axis=1)
    coef_ref[0:NRHS] = coef
    source_rows(coef_ref.at[NRHS : NRHS + 8], nodes_ref[...])
    target_rows(node_target_ref, nodes_ref[...])
    total[...] += fine(coef, transfer_ref[...], NT)

    count = counts[0]
    for leaf in range(STEP):
        for slot in range(NEAR_MAX):
            code = code_ref[step * STEP + leaf, slot]
            list_ref[lax.shift_right_logical(count, lax.shift_right_logical(code, 16)) & 0xFFFF] = code
            count = count + add_ref[step * STEP + leaf, slot]
    counts[0] = count

    @pl.when(step == pl.num_programs(0) - 1)
    def _():
        mid_coef = total[...]
        top_coef = fine(mid_coef, mid_transfer_ref[...], NT)
        level_ref[0:NRHS] = jnp.concatenate([mid_coef, top_coef], axis=1)
        source_rows(mid_rows, mid_nodes_ref[...])
        level_ref[NRHS : NRHS + 8] = jnp.concatenate([mid_rows[...], jnp.zeros((8, RANK), f32)], axis=1)
        for phase in range(2):
            end = lax.shift_right_logical(count, 16 * phase) & 0xFFFF
            for spare in range(2 * UNROLL):
                list_ref[end + spare] = LEAF_DEV << 6
            list_ref[phase * LIST + LIST - 1] = end - phase * LIST


def upward(codes, adds, charges, points, weights, basis, nodes, transfer, mid_nodes, mid_transfer):
    lanes = lambda rows, width: pl.BlockSpec((rows, width), lambda i: (0, i))
    fixed = lambda rows, width: pl.BlockSpec((rows, width), lambda i: (0, 0))
    wide, narrow = STEP * LEAF, STEP * RANK
    shape = jax.ShapeDtypeStruct
    return pl.pallas_call(
        upward_kernel,
        grid=(LEAF_DEV // STEP,),
        in_specs=[
            SMEM,
            SMEM,
            lanes(NRHS, wide),
            lanes(3, wide),
            lanes(1, wide),
            pl.BlockSpec((STEP, RANK, LEAF), lambda i: (i, 0, 0)),
            lanes(3, narrow),
            lanes(RANK, narrow),
            fixed(3, RANK),
            fixed(RANK, RANK),
        ],
        out_specs=[
            lanes(NRHS + 8, wide),
            lanes(8, wide),
            lanes(NRHS + 8, narrow),
            lanes(8, narrow),
            fixed(NRHS + 8, 2 * RANK),
            SMEM,
        ],
        out_shape=[
            shape((NRHS + 8, LEAF_DEV * LEAF), f32),
            shape((8, LEAF_DEV * LEAF), f32),
            shape((NRHS + 8, LEAF_DEV * RANK), f32),
            shape((8, LEAF_DEV * RANK), f32),
            shape((NRHS + 8, 2 * RANK), f32),
            shape((2 * LIST,), jnp.int32),
        ],
        scratch_shapes=[pltpu.VMEM((NRHS, RANK), f32), pltpu.VMEM((8, RANK), f32), pltpu.SMEM((1,), jnp.int32)],
        compiler_params=LIMIT,
        name="upward",
    )(codes, adds, charges, points, weights, basis, nodes, transfer, mid_nodes, mid_transfer)


def near_kernel(phase, list_ref, *refs):
    sources = 1 + phase
    packs, target_ref = refs[0:sources], refs[sources]
    out_ref, source, target, sides, highs, lows = refs[-6:]
    out_ref[...] = jnp.zeros_like(out_ref) if phase == 0 else refs[sources + 1][...]

    def prepare(group, _):
        for leaf in [group * 4 + k for k in range(4)]:
            lanes = pl.ds(pl.multiple_of(leaf * LEAF, LEAF), LEAF)
            target[leaf] = target_features(target_ref[:, lanes]).astype(bf16)
            for number, pack_ref in enumerate(packs):
                features = source_features(pack_ref[NRHS : NRHS + 8, lanes])
                source[number * LEAF_DEV + leaf] = features.T.astype(bf16)
                high, low = two(pack_ref[0:NRHS, lanes])
                sides[number * LEAF_DEV + leaf, 0:NRHS] = high
                sides[number * LEAF_DEV + leaf, NRHS : 2 * NRHS] = low
        return 0

    lax.fori_loop(0, LEAF_DEV // 4, prepare, 0)

    def item(index):
        code = list_ref[phase * LIST + index]
        return lax.shift_right_logical(code, 6) & 63, code & 63

    def values(index, slot):
        to, of = item(index)
        squares = product(source[of], target[to], NN)
        for row in range(0, LEAF, 64):
            high, low = two(lax.rsqrt(squares[row : row + 64]))
            highs[slot, row : row + 64] = high
            lows[slot, row : row + 64] = low

    def apply(index, slot):
        to, of = item(index)
        upper = product(sides[of], highs[slot], NN)
        lower = product(sides[of, 0:NRHS], lows[slot], NN)
        return to, upper[0:NRHS] + upper[NRHS : 2 * NRHS] + lower

    for slot in range(UNROLL):
        values(slot, slot)

    def step(number, _):
        results = []
        for slot in range(UNROLL):
            index = number * UNROLL + slot
            results.append(apply(index, slot))
            values(index + UNROLL, slot)
        for to, result in results:
            out_ref[to] += result
        return 0

    length = list_ref[phase * LIST + LIST - 1]
    lax.fori_loop(0, lax.div(length + (UNROLL - 1), UNROLL), step, 0)


def near(phase, lists, packs, targets, before):
    operands = (*packs, targets) + (() if before is None else (before,))
    rows, sources = LEAF_DEV + 1, LEAF_DEV * len(packs)
    shape = jax.ShapeDtypeStruct((rows, NRHS, LEAF), f32)
    return pl.pallas_call(
        functools.partial(near_kernel, phase),
        grid=(1,),
        in_specs=[SMEM] + [whole(operand) for operand in operands],
        out_specs=whole(shape),
        out_shape=shape,
        scratch_shapes=[
            pltpu.VMEM((sources, LEAF, FEAT), bf16),
            pltpu.VMEM((rows, FEAT, LEAF), bf16),
            pltpu.VMEM((sources, 2 * NRHS, LEAF), bf16),
            pltpu.VMEM((UNROLL, LEAF, LEAF), bf16),
            pltpu.VMEM((UNROLL, LEAF, LEAF), bf16),
        ],
        compiler_params=LIMIT,
        cost_estimate=pl.CostEstimate(flops=20_000_000_000, bytes_accessed=4_000_000, transcendentals=14_000_000),
        name="near" + str(phase),
    )(lists, *operands)


def couple(groups, targets):
    kernels = []
    for _, rows in groups:
        kernels.append(product(targets, source_features(rows).astype(bf16), NN))
    total = jnp.zeros((2 * NRHS, RANK), f32)
    extra = jnp.zeros((NRHS, RANK), f32)
    for (coefs, _), squares in zip(groups, kernels):
        high, low = two(lax.rsqrt(squares))
        side, rest = two(coefs)
        total = total + product(jnp.concatenate([side, rest], axis=0), high, NT)
        extra = extra + product(side, low, NT)
    return total[0:NRHS] + total[NRHS : 2 * NRHS] + extra


def mid_kernel(
    mid_row_ref, top_row_ref, level_ref, top_nodes_ref, top_target_ref, mid_nodes_ref, mid_transfer_ref, transfer_ref, out_ref, rows, tops
):
    lower = lax.broadcasted_iota(jnp.int32, (1, 2 * RANK), 1) < RANK

    def features(nodes):
        target_rows(rows, nodes)
        return target_features(rows[...]).T.astype(bf16)

    def beside(left, right):
        return jnp.where(lower, left, pltpu.roll(right, RANK, 1))

    source_rows(tops, top_nodes_ref[...])
    top_targets = features(top_target_ref[...])
    groups = []
    for first in range(0, top_nodes_ref.shape[1] // RANK, 4):
        coefs = []
        for top in range(first, first + 4):
            coef = level_ref[top * GROUP, 0:NRHS]
            for member in range(1, GROUP):
                coef = coef + level_ref[top * GROUP + member, 0:NRHS]
            coefs.append(coef * top_row_ref[top].astype(f32))
        swapped = [pltpu.roll(coef, RANK, 1) for coef in coefs]
        side = [jnp.where(lower, swapped[k], coefs[k + 1]) for k in (0, 2)]
        groups.append((jnp.concatenate(side, axis=1), tops[:, first * RANK : (first + 4) * RANK]))
    top_field = couple(groups, top_targets)
    mid_targets = features(mid_nodes_ref[...])

    def step(number, total):
        groups = []
        for group in range(8):
            first = number * 32 + group * 4
            coefs = [level_ref[first + k, 0:NRHS] * mid_row_ref[0, first + k].astype(f32) for k in range(4)]
            picked = [level_ref[first + k, NRHS : NRHS + 8] for k in range(4)]
            side = [beside(coefs[0], coefs[1]), beside(coefs[2], coefs[3])]
            node = [beside(picked[0], picked[1]), beside(picked[2], picked[3])]
            groups.append((jnp.concatenate(side, axis=1), jnp.concatenate(node, axis=1)))
        return total + couple(groups, mid_targets)

    field = lax.fori_loop(0, level_ref.shape[0] // 32, step, jnp.zeros((NRHS, RANK), f32))
    field = field * inv_four_pi + fine(top_field * inv_four_pi, mid_transfer_ref[...], NN)
    out_ref[...] = fine(field, transfer_ref[...], NN)


def mid(mid_row, top_row, *operands):
    shape = jax.ShapeDtypeStruct((NRHS, LEAF_DEV * RANK), f32)
    return pl.pallas_call(
        mid_kernel,
        grid=(1,),
        in_specs=[SMEM, SMEM] + [whole(operand) for operand in operands],
        out_specs=whole(shape),
        out_shape=shape,
        scratch_shapes=[pltpu.VMEM((8, RANK), f32), pltpu.VMEM((8, operands[1].shape[1]), f32)],
        compiler_params=LIMIT,
        name="mid",
    )(mid_row, top_row, *operands)


def far_kernel(
    far_ref, own_ref, partner_ref, cross_ref, node_target_ref, down_ref, near_ref, basis_ref, out_ref, nodes_low, nodes_high, coef_low, coef_high
):
    quad = pl.program_id(0)
    lower = lax.broadcasted_iota(jnp.int32, (1, 2 * RANK), 1) < RANK

    @pl.when(quad == 0)
    def _():
        for phase, ref in enumerate((own_ref, partner_ref, cross_ref)):

            def prepare(group, _):
                for pair in [group * 4 + k for k in range(4)]:
                    lanes = pl.ds(pl.multiple_of(pair * 2 * RANK, 2 * RANK), 2 * RANK)
                    features = source_features(ref[NRHS : NRHS + 8, lanes])
                    turned = jnp.concatenate([features, features], axis=0).T
                    coef = ref[0:NRHS, lanes]
                    swapped = pltpu.roll(coef, RANK, 1)
                    for half in range(2):
                        leaf = phase * LEAF_DEV + 2 * pair + half
                        node = turned[half * RANK : (half + 1) * RANK]
                        nodes_low[leaf] = jnp.where(lower, node, 0.0).astype(bf16)
                        nodes_high[leaf] = jnp.where(lower, 0.0, node).astype(bf16)
                        left, right = (coef, swapped) if half == 0 else (swapped, coef)
                        for store, values in ((coef_low, jnp.where(lower, left, 0.0)), (coef_high, jnp.where(lower, 0.0, right))):
                            high, low = two(values)
                            store[leaf, 0:NRHS] = high
                            store[leaf, NRHS : 2 * NRHS] = low
                return 0

            lax.fori_loop(0, LEAF_DEV // 8, prepare, 0)

    block = lax.broadcasted_iota(jnp.int32, (1, 4 * RANK), 1) // RANK
    features = target_features(node_target_ref[...])
    weights = jnp.concatenate([jnp.where(block == k, features, 0.0) for k in range(4)], axis=0).astype(bf16)
    total = jnp.zeros((8 * NRHS, 4 * RANK), f32)
    extra = jnp.zeros((4 * NRHS, 4 * RANK), f32)
    chunks = []
    for chunk in range(FAR2 // 4):
        leaves = [[far_ref[quad * 4 + k, chunk * 4 + f] for f in range(4)] for k in range(4)]
        parts = []
        for f in range(4):
            one = nodes_low[leaves[0][f]] + nodes_high[leaves[1][f]]
            other = nodes_low[leaves[2][f]] + nodes_high[leaves[3][f]]
            parts.append(jnp.concatenate([one, other], axis=1))
        chunks.append((leaves, product(jnp.concatenate(parts, axis=0), weights, NN)))
    for leaves, squares in chunks:
        high, low = two(lax.rsqrt(squares))
        sides = []
        for k in range(4):
            one = coef_low[leaves[k][0]] + coef_high[leaves[k][1]]
            other = coef_low[leaves[k][2]] + coef_high[leaves[k][3]]
            sides.append(jnp.concatenate([one, other], axis=1))
        total = total + product(jnp.concatenate(sides, axis=0), high, NN)
        extra = extra + product(jnp.concatenate([side[0:NRHS] for side in sides], axis=0), low, NN)
    field = jnp.zeros((NRHS, 4 * RANK), f32)
    for k in range(4):
        own = total[2 * k * NRHS : (2 * k + 1) * NRHS] + total[(2 * k + 1) * NRHS : (2 * k + 2) * NRHS]
        field = jnp.where(block == k, own + extra[k * NRHS : (k + 1) * NRHS], field)
    field = field * inv_four_pi + down_ref[...]
    for leaf in range(4):
        far = fine(field[:, leaf * RANK : (leaf + 1) * RANK], basis_ref[leaf], NN)
        out_ref[:, leaf * LEAF : (leaf + 1) * LEAF] = far + near_ref[leaf]


def far(far_codes, own, partner, cross, node_targets, down, near_out, basis):
    leaves = 3 * LEAF_DEV
    return pl.pallas_call(
        far_kernel,
        grid=(LEAF_DEV // 4,),
        in_specs=[
            SMEM,
            whole(own),
            whole(partner),
            whole(cross),
            pl.BlockSpec((8, 4 * RANK), lambda i: (0, i)),
            pl.BlockSpec((NRHS, 4 * RANK), lambda i: (0, i)),
            pl.BlockSpec((4, NRHS, LEAF), lambda i: (i, 0, 0)),
            pl.BlockSpec((4, RANK, LEAF), lambda i: (i, 0, 0)),
        ],
        out_specs=pl.BlockSpec((NRHS, 4 * LEAF), lambda i: (0, i)),
        out_shape=jax.ShapeDtypeStruct((NRHS, LEAF_DEV * LEAF), f32),
        scratch_shapes=[pltpu.VMEM((leaves, RANK, 2 * RANK), bf16)] * 4,
        compiler_params=LIMIT,
        name="far",
    )(far_codes, own, partner, cross, node_targets, down, near_out, basis)


def shards(
    charges,
    positions,
    quad_weights,
    leaf_basis,
    leaf_nodes,
    leaf_transfer,
    mid_nodes,
    mid_transfer,
    top_nodes,
    near_list,
    near_count,
    far_list,
    mid_mask,
    top_mask,
):
    devices = lax.axis_size("clus")
    myself = lax.axis_index("clus")
    partner = [(i, i ^ 1) for i in range(devices)]
    cross = [(i, (i + 1 if i % 2 else i - 1) % devices) for i in range(devices)]
    partner_step = jnp.where(myself % 2 == 0, 1, devices - 1)

    def away(leaves):
        return (leaves // LEAF_DEV - myself) % devices

    def place(leaves):
        steps = away(leaves)
        return jnp.where(steps == 0, 0, jnp.where(steps == partner_step, LEAF_DEV, 2 * LEAF_DEV)) + leaves % LEAF_DEV

    live = jnp.arange(NEAR_MAX)[None, :] < near_count[:, None]
    other = away(near_list) != 0
    leaf_row = jnp.arange(LEAF_DEV, dtype=jnp.int32)[:, None]
    source = place(near_list) - jnp.where(other, LEAF_DEV, 0)
    codes = (jnp.where(other, 16, 0) << 16) | (leaf_row << 6) | source
    adds = jnp.where(live, jnp.where(other, 1 << 16, 1), 0)

    pack, targets, coef, node_targets, level, lists = upward(
        codes.astype(jnp.int32),
        adds.astype(jnp.int32),
        charges,
        positions,
        quad_weights.reshape(1, -1),
        leaf_basis,
        leaf_nodes,
        leaf_transfer,
        mid_nodes,
        mid_transfer,
    )
    everyone = lax.all_gather(level, "clus", axis=0, tiled=False)
    pack_partner = lax.ppermute(pack, "clus", partner)
    pack_cross = lax.ppermute(pack, "clus", cross)
    coef_partner = lax.ppermute(coef, "clus", partner)
    coef_cross = lax.ppermute(coef, "clus", cross)

    near_out = near(0, lists, (pack,), targets, None)
    near_out = near(1, lists, (pack_partner, pack_cross), targets, near_out)

    parent = myself // GROUP
    top_target = lax.dynamic_slice_in_dim(top_nodes, parent * RANK, RANK, 1)
    top_row = lax.dynamic_index_in_dim(top_mask, parent, 0, keepdims=False)
    down = mid(mid_mask, top_row, everyone, top_nodes, top_target, mid_nodes, mid_transfer, leaf_transfer)
    far_codes = place(far_list).astype(jnp.int32)
    return far(far_codes, coef, coef_partner, coef_cross, node_targets, down, near_out, leaf_basis)


def solution(mesh):
    in_specs = (
        P(None, "clus"),
        P(None, "clus"),
        P("clus"),
        P("clus", None, None),
        P(None, "clus"),
        P(None, "clus"),
        P(None, "clus"),
        P(None, "clus"),
        P(),
        P("clus", None),
        P("clus"),
        P("clus", None),
        P("clus", None),
        P(),
    )
    out_specs = P(None, "clus")
    return jax.shard_map(shards, mesh=mesh, in_specs=in_specs, out_specs=out_specs, check_vma=False)
```

```python
import functools
import math

import jax
import jax.numpy as jnp
from jax import lax
from jax.experimental import pallas as pl
from jax.experimental.pallas import tpu as pltpu
from jax.sharding import PartitionSpec as P

LEAF = 256
RANK = 64
NRHS = 32
LEAF_DEV = 32
NEAR_MAX = 27
FAR2 = 16
GROUP = 8

STEP = 4
LIST = 1024
FEAT = 64
WIDE = STEP * LEAF
PACK = STEP * (LEAF + RANK)
UNROLL = 16

smoothing = 0.05
inv_four_pi = 1.0 / (4.0 * math.pi)
highest = lax.Precision.HIGHEST
bf16 = jnp.bfloat16
f32 = jnp.float32
NN = (((1,), (0,)), ((), ()))
NT = (((1,), (1,)), ((), ()))
LIMIT = pltpu.CompilerParams(vmem_limit_bytes=56 * 2**20)
SMEM = pl.BlockSpec(memory_space=pltpu.SMEM)


def product(left, right, dims, precision=None):
    return lax.dot_general(left, right, dims, precision=precision, preferred_element_type=f32)


def source_rows(out, points):
    width = points.shape[1]
    out[0:3] = points
    out[3:4] = jnp.sum(points * points, axis=0, keepdims=True)
    out[4:5] = jnp.ones((1, width), f32)
    out[5:8] = jnp.zeros((3, width), f32)


def target_rows(out, points):
    width = points.shape[1]
    out[0:3] = points * -2.0
    out[3:4] = jnp.ones((1, width), f32)
    out[4:5] = jnp.sum(points * points, axis=0, keepdims=True) + smoothing * smoothing
    out[5:8] = jnp.zeros((3, width), f32)


def three(rows):
    first = rows.astype(bf16).astype(f32)
    rest = rows - first
    second = rest.astype(bf16).astype(f32)
    third = (rest - second).astype(bf16).astype(f32)
    return first, second, third


def source_features(rows):
    a, b, c = three(rows)
    return jnp.concatenate([a, a, b, a, c, b, b, c], axis=0)


def target_features(rows):
    a, b, c = three(rows)
    return jnp.concatenate([a, b, a, c, a, b, c, b], axis=0)


def two(values):
    high = values.astype(bf16)
    low = (values - high.astype(f32)).astype(bf16)
    return high, low


def fine(left, right, dims):
    rows = left.shape[0]
    high, low = two(left)
    near_high, near_low = two(right)
    both = product(jnp.concatenate([high, low], axis=0), near_high, dims)
    return both[0:rows] + both[rows : 2 * rows] + product(high, near_low, dims)


def whole(array):
    zeros = (0,) * array.ndim
    return pl.BlockSpec(array.shape, lambda i: zeros)


def upward_kernel(
    charges_ref,
    points_ref,
    weights_ref,
    basis_ref,
    nodes_ref,
    transfer_ref,
    mid_nodes_ref,
    mid_transfer_ref,
    pack_ref,
    target_ref,
    node_target_ref,
    level_ref,
    total,
    mid_rows,
):
    step = pl.program_id(0)

    @pl.when(step == 0)
    def _():
        total[...] = jnp.zeros_like(total)

    charges = charges_ref[...]
    points = points_ref[...]
    pack_ref[0:NRHS, 0:WIDE] = charges * (weights_ref[...] * inv_four_pi)
    source_rows(pack_ref.at[NRHS : NRHS + 8, 0:WIDE], points)
    target_rows(target_ref, points)
    coefs = [fine(charges[:, k * LEAF : (k + 1) * LEAF], basis_ref[k], NT) for k in range(STEP)]
    coef = jnp.concatenate(coefs, axis=1)
    pack_ref[0:NRHS, WIDE:PACK] = coef
    source_rows(pack_ref.at[NRHS : NRHS + 8, WIDE:PACK], nodes_ref[...])
    target_rows(node_target_ref, nodes_ref[...])
    total[...] += fine(coef, transfer_ref[...], NT)

    @pl.when(step == pl.num_programs(0) - 1)
    def _():
        mid_coef = total[...]
        top_coef = fine(mid_coef, mid_transfer_ref[...], NT)
        level_ref[0:NRHS] = jnp.concatenate([mid_coef, top_coef], axis=1)
        source_rows(mid_rows, mid_nodes_ref[...])
        level_ref[NRHS : NRHS + 8] = jnp.concatenate([mid_rows[...], jnp.zeros((8, RANK), f32)], axis=1)


def upward(charges, points, weights, basis, nodes, transfer, mid_nodes, mid_transfer):
    lanes = lambda rows, width: pl.BlockSpec((rows, width), lambda i: (0, i))
    fixed = lambda rows, width: pl.BlockSpec((rows, width), lambda i: (0, 0))
    narrow, steps = STEP * RANK, LEAF_DEV // STEP
    shape = jax.ShapeDtypeStruct
    return pl.pallas_call(
        upward_kernel,
        grid=(steps,),
        in_specs=[
            lanes(NRHS, WIDE),
            lanes(3, WIDE),
            lanes(1, WIDE),
            pl.BlockSpec((STEP, RANK, LEAF), lambda i: (i, 0, 0)),
            lanes(3, narrow),
            lanes(RANK, narrow),
            fixed(3, RANK),
            fixed(RANK, RANK),
        ],
        out_specs=[lanes(NRHS + 8, PACK), lanes(8, WIDE), lanes(8, narrow), fixed(NRHS + 8, 2 * RANK)],
        out_shape=[
            shape((NRHS + 8, steps * PACK), f32),
            shape((8, LEAF_DEV * LEAF), f32),
            shape((8, LEAF_DEV * RANK), f32),
            shape((NRHS + 8, 2 * RANK), f32),
        ],
        scratch_shapes=[pltpu.VMEM((NRHS, RANK), f32), pltpu.VMEM((8, RANK), f32)],
        compiler_params=LIMIT,
        name="upward",
    )(charges, points, weights, basis, nodes, transfer, mid_nodes, mid_transfer)


def lists_kernel(devices, self_ref, near_ref, count_ref, far_list_ref, list_ref, far_ref):
    myself = self_ref[0]
    partner_step = jnp.where(myself % 2 == 0, 1, devices - 1)

    def place(leaves):
        steps = lax.shift_right_logical(leaves, 5) - myself
        steps = jnp.where(steps < 0, steps + devices, steps)
        return steps == 0, jnp.where(steps == partner_step, 0, LEAF_DEV) + (leaves & (LEAF_DEV - 1))

    own, other = place(far_list_ref[...])
    far_ref[...] = jnp.where(own, far_list_ref[...] & (LEAF_DEV - 1), other + LEAF_DEV)

    leaves = near_ref[...]
    own, other = place(leaves)
    row = lax.broadcasted_iota(jnp.int32, leaves.shape, 0)
    code = (lax.shift_left(row, 6) | jnp.where(own, leaves & (LEAF_DEV - 1), other)).astype(f32)
    square = (LEAF_DEV, LEAF_DEV)
    up, across = lax.broadcasted_iota(jnp.int32, square, 0), lax.broadcasted_iota(jnp.int32, square, 1)
    counts = jnp.sum(jnp.where(up == across, jnp.broadcast_to(count_ref[...], square), 0).astype(f32), axis=1, keepdims=True)
    live = lax.broadcasted_iota(jnp.int32, leaves.shape, 1).astype(f32) < counts
    slots = (NEAR_MAX, NEAR_MAX)
    earlier_slot = lax.broadcasted_iota(jnp.int32, slots, 0) < lax.broadcasted_iota(jnp.int32, slots, 1)
    earlier_slot = jnp.where(earlier_slot, 1.0, 0.0).astype(bf16)
    earlier_row = jnp.where(across < up, 1.0, 0.0).astype(bf16)
    for phase in range(2):
        chosen = jnp.where(live, jnp.where(own, 1.0, 0.0), 0.0)
        if phase == 1:
            chosen = jnp.where(live, 1.0 - chosen, 0.0)
        mark = chosen.astype(bf16)
        before = jnp.sum(product(earlier_row, mark, NN), axis=1, keepdims=True)
        place_of = jnp.where(chosen > 0.0, before + product(mark, earlier_slot, NN), -1.0)
        length = jnp.sum(jnp.sum(chosen, axis=1, keepdims=True), axis=0, keepdims=True)
        for first in range(0, LIST, 256):
            lane = lax.broadcasted_iota(jnp.int32, (1, 256), 1) + first
            spot = lane.astype(f32)
            total = jnp.zeros((LEAF_DEV, 256), f32)
            for slot in range(NEAR_MAX):
                total = total + jnp.where(place_of[:, slot : slot + 1] == spot, code[:, slot : slot + 1], 0.0)
            words = jnp.sum(total, axis=0, keepdims=True)
            words = jnp.where(spot < length, words, float(LEAF_DEV << 6))
            words = jnp.where(lane == LIST - 1, length, words)
            list_ref[phase : phase + 1, first : first + 256] = words.astype(jnp.int32)


def lists(devices, myself, near_list, near_count, far_list):
    operands = (near_list, near_count.reshape(1, -1), far_list)
    shapes = [jax.ShapeDtypeStruct((2, LIST), jnp.int32), jax.ShapeDtypeStruct(far_list.shape, jnp.int32)]
    return pl.pallas_call(
        functools.partial(lists_kernel, devices),
        grid=(1,),
        in_specs=[SMEM] + [whole(operand) for operand in operands],
        out_specs=[whole(shape) for shape in shapes],
        out_shape=shapes,
        compiler_params=LIMIT,
        name="lists",
    )(myself, *operands)


def near_kernel(phase, list_ref, *refs):
    sources = 1 + phase
    packs, target_ref = refs[0:sources], refs[sources]
    out_ref, source, target, sides, highs, lows = refs[-6:]
    out_ref[...] = jnp.zeros_like(out_ref) if phase == 0 else refs[sources + 1][...]

    def prepare(group, _):
        for leaf in [group * STEP + k for k in range(STEP)]:
            lanes = pl.ds(pl.multiple_of(leaf * LEAF, LEAF), LEAF)
            packed = pl.ds(pl.multiple_of(group * PACK + (leaf - group * STEP) * LEAF, LEAF), LEAF)
            target[leaf] = target_features(target_ref[:, lanes]).astype(bf16)
            for number, pack_ref in enumerate(packs):
                features = source_features(pack_ref[NRHS : NRHS + 8, packed])
                source[number * LEAF_DEV + leaf] = features.T.astype(bf16)
                high, low = two(pack_ref[0:NRHS, packed])
                sides[number * LEAF_DEV + leaf, 0:NRHS] = high
                sides[number * LEAF_DEV + leaf, NRHS : 2 * NRHS] = low
        return 0

    lax.fori_loop(0, LEAF_DEV // STEP, prepare, 0)

    def item(index):
        code = list_ref[phase, index]
        return lax.shift_right_logical(code, 6) & 63, code & 63

    def values(index, slot):
        to, of = item(index)
        squares = product(source[of], target[to], NN)
        for row in range(0, LEAF, 64):
            high, low = two(lax.rsqrt(squares[row : row + 64]))
            highs[slot, row : row + 64] = high
            lows[slot, row : row + 64] = low

    def apply(index, slot):
        to, of = item(index)
        upper = product(sides[of], highs[slot], NN)
        lower = product(sides[of, 0:NRHS], lows[slot], NN)
        return to, upper[0:NRHS] + upper[NRHS : 2 * NRHS] + lower

    for slot in range(UNROLL):
        values(slot, slot)

    def step(number, _):
        results = []
        for slot in range(UNROLL):
            index = number * UNROLL + slot
            results.append(apply(index, slot))
            values(index + UNROLL, slot)
        for to, result in results:
            out_ref[to] += result
        return 0

    length = list_ref[phase, LIST - 1]
    lax.fori_loop(0, lax.div(length + (UNROLL - 1), UNROLL), step, 0)


def near(phase, items, packs, targets, before):
    operands = (*packs, targets) + (() if before is None else (before,))
    rows, sources = LEAF_DEV + 1, LEAF_DEV * len(packs)
    shape = jax.ShapeDtypeStruct((rows, NRHS, LEAF), f32)
    return pl.pallas_call(
        functools.partial(near_kernel, phase),
        grid=(1,),
        in_specs=[SMEM] + [whole(operand) for operand in operands],
        out_specs=whole(shape),
        out_shape=shape,
        scratch_shapes=[
            pltpu.VMEM((sources, LEAF, FEAT), bf16),
            pltpu.VMEM((rows, FEAT, LEAF), bf16),
            pltpu.VMEM((sources, 2 * NRHS, LEAF), bf16),
            pltpu.VMEM((UNROLL, LEAF, LEAF), bf16),
            pltpu.VMEM((UNROLL, LEAF, LEAF), bf16),
        ],
        compiler_params=LIMIT,
        cost_estimate=pl.CostEstimate(flops=20_000_000_000, bytes_accessed=4_000_000, transcendentals=14_000_000),
        name="near" + str(phase),
    )(items, *operands)


def couple(groups, targets):
    kernels = []
    for _, rows in groups:
        kernels.append(product(targets, source_features(rows).astype(bf16), NN))
    total = jnp.zeros((2 * NRHS, RANK), f32)
    extra = jnp.zeros((NRHS, RANK), f32)
    for (coefs, _), squares in zip(groups, kernels):
        high, low = two(lax.rsqrt(squares))
        side, rest = two(coefs)
        total = total + product(jnp.concatenate([side, rest], axis=0), high, NT)
        extra = extra + product(side, low, NT)
    return total[0:NRHS] + total[NRHS : 2 * NRHS] + extra


def down_kernel(
    self_ref,
    mid_row_ref,
    top_mask_ref,
    level_ref,
    top_nodes_ref,
    mid_nodes_ref,
    mid_transfer_ref,
    transfer_ref,
    field_ref,
    near_ref,
    basis_ref,
    out_ref,
    rows,
    tops,
    down,
):
    @pl.when(pl.program_id(0) == 0)
    def _():
        down[...] = mid_field(
            self_ref, mid_row_ref, top_mask_ref, level_ref, top_nodes_ref, mid_nodes_ref, mid_transfer_ref, transfer_ref, rows, tops
        )

    lanes = pl.ds(pl.multiple_of(pl.program_id(0) * (STEP * RANK), STEP * RANK), STEP * RANK)
    field = field_ref[...] + down[:, lanes]
    for leaf in range(STEP):
        far = fine(field[:, leaf * RANK : (leaf + 1) * RANK], basis_ref[leaf], NN)
        out_ref[:, leaf * LEAF : (leaf + 1) * LEAF] = far + near_ref[leaf]


def mid_field(self_ref, mid_row_ref, top_mask_ref, level_ref, top_nodes_ref, mid_nodes_ref, mid_transfer_ref, transfer_ref, rows, tops):
    parent = self_ref[1]
    lower = lax.broadcasted_iota(jnp.int32, (1, 2 * RANK), 1) < RANK

    def features(nodes):
        target_rows(rows, nodes)
        return target_features(rows[...]).T.astype(bf16)

    def beside(left, right):
        return jnp.where(lower, left, pltpu.roll(right, RANK, 1))

    source_rows(tops, top_nodes_ref[...])
    own = jnp.zeros((3, RANK), f32)
    for top in range(top_nodes_ref.shape[1] // RANK):
        own = jnp.where(parent == top, top_nodes_ref[:, top * RANK : (top + 1) * RANK], own)
    top_targets = features(own)
    groups = []
    for first in range(0, top_nodes_ref.shape[1] // RANK, 4):
        coefs = []
        for top in range(first, first + 4):
            coef = level_ref[top * GROUP, 0:NRHS]
            for member in range(1, GROUP):
                coef = coef + level_ref[top * GROUP + member, 0:NRHS]
            coefs.append(coef * top_mask_ref[parent, top].astype(f32))
        swapped = [pltpu.roll(coef, RANK, 1) for coef in coefs]
        side = [jnp.where(lower, swapped[k], coefs[k + 1]) for k in (0, 2)]
        groups.append((jnp.concatenate(side, axis=1), tops[:, first * RANK : (first + 4) * RANK]))
    top_field = couple(groups, top_targets)
    mid_targets = features(mid_nodes_ref[...])

    def step(number, total):
        groups = []
        for group in range(8):
            first = number * 32 + group * 4
            coefs = [level_ref[first + k, 0:NRHS] * mid_row_ref[0, first + k].astype(f32) for k in range(4)]
            picked = [level_ref[first + k, NRHS : NRHS + 8] for k in range(4)]
            side = [beside(coefs[0], coefs[1]), beside(coefs[2], coefs[3])]
            node = [beside(picked[0], picked[1]), beside(picked[2], picked[3])]
            groups.append((jnp.concatenate(side, axis=1), jnp.concatenate(node, axis=1)))
        return total + couple(groups, mid_targets)

    field = lax.fori_loop(0, level_ref.shape[0] // 32, step, jnp.zeros((NRHS, RANK), f32))
    field = field * inv_four_pi + fine(top_field * inv_four_pi, mid_transfer_ref[...], NN)
    return fine(field, transfer_ref[...], NN)


def downward(self_parent, mid_row, top_mask, everyone, top_nodes, mid_nodes, mid_transfer, transfer, field, near_out, basis):
    fixed = (everyone, top_nodes, mid_nodes, mid_transfer, transfer)
    return pl.pallas_call(
        down_kernel,
        grid=(LEAF_DEV // STEP,),
        in_specs=[SMEM, SMEM, SMEM]
        + [whole(operand) for operand in fixed]
        + [
            pl.BlockSpec((NRHS, STEP * RANK), lambda i: (0, i)),
            pl.BlockSpec((STEP, NRHS, LEAF), lambda i: (i, 0, 0)),
            pl.BlockSpec((STEP, RANK, LEAF), lambda i: (i, 0, 0)),
        ],
        out_specs=pl.BlockSpec((NRHS, STEP * LEAF), lambda i: (0, i)),
        out_shape=jax.ShapeDtypeStruct((NRHS, LEAF_DEV * LEAF), f32),
        scratch_shapes=[
            pltpu.VMEM((8, RANK), f32),
            pltpu.VMEM((8, top_nodes.shape[1]), f32),
            pltpu.VMEM((NRHS, LEAF_DEV * RANK), f32),
        ],
        compiler_params=LIMIT,
        name="downward",
    )(self_parent, mid_row, top_mask, *fixed, field, near_out, basis)


def far_kernel(
    far_ref, own_ref, partner_ref, cross_ref, node_target_ref, out_ref, nodes_low, nodes_high, coef_low, coef_high
):
    quad = pl.program_id(0)
    lower = lax.broadcasted_iota(jnp.int32, (1, 2 * RANK), 1) < RANK

    @pl.when(quad == 0)
    def _():
        for phase, ref in enumerate((own_ref, partner_ref, cross_ref)):

            def prepare(group, _):
                for k in range(4):
                    pair = group * 4 + k
                    start = (group * 2 + k // 2) * PACK + WIDE + k % 2 * (2 * RANK)
                    lanes = pl.ds(pl.multiple_of(start, 2 * RANK), 2 * RANK)
                    features = source_features(ref[NRHS : NRHS + 8, lanes])
                    turned = jnp.concatenate([features, features], axis=0).T
                    coef = ref[0:NRHS, lanes]
                    swapped = pltpu.roll(coef, RANK, 1)
                    for half in range(2):
                        leaf = phase * LEAF_DEV + 2 * pair + half
                        node = turned[half * RANK : (half + 1) * RANK]
                        nodes_low[leaf] = jnp.where(lower, node, 0.0).astype(bf16)
                        nodes_high[leaf] = jnp.where(lower, 0.0, node).astype(bf16)
                        left, right = (coef, swapped) if half == 0 else (swapped, coef)
                        for store, values in ((coef_low, jnp.where(lower, left, 0.0)), (coef_high, jnp.where(lower, 0.0, right))):
                            high, low = two(values)
                            store[leaf, 0:NRHS] = high
                            store[leaf, NRHS : 2 * NRHS] = low
                return 0

            lax.fori_loop(0, LEAF_DEV // 8, prepare, 0)

    block = lax.broadcasted_iota(jnp.int32, (1, 4 * RANK), 1) // RANK
    features = target_features(node_target_ref[...])
    weights = jnp.concatenate([jnp.where(block == k, features, 0.0) for k in range(4)], axis=0).astype(bf16)
    total = jnp.zeros((8 * NRHS, 4 * RANK), f32)
    extra = jnp.zeros((4 * NRHS, 4 * RANK), f32)
    chunks = []
    for chunk in range(FAR2 // 4):
        leaves = [[far_ref[quad * 4 + k, chunk * 4 + f] for f in range(4)] for k in range(4)]
        parts = []
        for f in range(4):
            one = nodes_low[leaves[0][f]] + nodes_high[leaves[1][f]]
            other = nodes_low[leaves[2][f]] + nodes_high[leaves[3][f]]
            parts.append(jnp.concatenate([one, other], axis=1))
        chunks.append((leaves, product(jnp.concatenate(parts, axis=0), weights, NN)))
    for leaves, squares in chunks:
        high, low = two(lax.rsqrt(squares))
        sides = []
        for k in range(4):
            one = coef_low[leaves[k][0]] + coef_high[leaves[k][1]]
            other = coef_low[leaves[k][2]] + coef_high[leaves[k][3]]
            sides.append(jnp.concatenate([one, other], axis=1))
        total = total + product(jnp.concatenate(sides, axis=0), high, NN)
        extra = extra + product(jnp.concatenate([side[0:NRHS] for side in sides], axis=0), low, NN)
    field = jnp.zeros((NRHS, 4 * RANK), f32)
    for k in range(4):
        own = total[2 * k * NRHS : (2 * k + 1) * NRHS] + total[(2 * k + 1) * NRHS : (2 * k + 2) * NRHS]
        field = jnp.where(block == k, own + extra[k * NRHS : (k + 1) * NRHS], field)
    out_ref[...] = field * inv_four_pi


def far(far_codes, own, partner, cross, node_targets):
    leaves = 3 * LEAF_DEV
    return pl.pallas_call(
        far_kernel,
        grid=(LEAF_DEV // 4,),
        in_specs=[SMEM, whole(own), whole(partner), whole(cross), pl.BlockSpec((8, 4 * RANK), lambda i: (0, i))],
        out_specs=pl.BlockSpec((NRHS, 4 * RANK), lambda i: (0, i)),
        out_shape=jax.ShapeDtypeStruct((NRHS, LEAF_DEV * RANK), f32),
        scratch_shapes=[pltpu.VMEM((leaves, RANK, 2 * RANK), bf16)] * 4,
        compiler_params=LIMIT,
        cost_estimate=pl.CostEstimate(flops=10_000_000_000, bytes_accessed=4_000_000, transcendentals=2_000_000),
        name="far",
    )(far_codes, own, partner, cross, node_targets)


def shards(
    charges,
    positions,
    quad_weights,
    leaf_basis,
    leaf_nodes,
    leaf_transfer,
    mid_nodes,
    mid_transfer,
    top_nodes,
    near_list,
    near_count,
    far_list,
    mid_mask,
    top_mask,
):
    devices = lax.axis_size("clus")
    myself = lax.axis_index("clus")
    partner = [(i, i ^ 1) for i in range(devices)]
    cross = [(i, (i + 1 if i % 2 else i - 1) % devices) for i in range(devices)]
    pack, targets, node_targets, level = upward(
        charges, positions, quad_weights.reshape(1, -1), leaf_basis, leaf_nodes, leaf_transfer, mid_nodes, mid_transfer
    )
    everyone = lax.all_gather(level, "clus", axis=0, tiled=False)
    pack_partner = lax.ppermute(pack, "clus", partner)
    pack_cross = lax.ppermute(pack, "clus", cross)

    self_parent = jnp.stack([myself, myself // GROUP]).astype(jnp.int32)
    items, far_codes = lists(devices, self_parent, near_list, near_count, far_list)
    near_out = near(0, items, (pack,), targets, None)
    near_out = near(1, items, (pack_partner, pack_cross), targets, near_out)
    field = far(far_codes, pack, pack_partner, pack_cross, node_targets)
    return downward(
        self_parent, mid_mask, top_mask, everyone, top_nodes, mid_nodes, mid_transfer, leaf_transfer, field, near_out, leaf_basis
    )


def solution(mesh):
    in_specs = (
        P(None, "clus"),
        P(None, "clus"),
        P("clus"),
        P("clus", None, None),
        P(None, "clus"),
        P(None, "clus"),
        P(None, "clus"),
        P(None, "clus"),
        P(),
        P("clus", None),
        P("clus"),
        P("clus", None),
        P("clus", None),
        P(),
    )
    out_specs = P(None, "clus")
    return jax.shard_map(shards, mesh=mesh, in_specs=in_specs, out_specs=out_specs, check_vma=False)
```

```python
import functools
import math

import jax
import jax.numpy as jnp
from jax import lax
from jax.experimental import pallas as pl
from jax.experimental.pallas import tpu as pltpu
from jax.sharding import PartitionSpec as P

LEAF = 256
RANK = 64
NRHS = 32
LEAF_DEV = 32
NEAR_MAX = 27
FAR2 = 16
GROUP = 8

STEP = 4
LIST = 1024
FEAT = 64
WIDE = STEP * LEAF
PACK = STEP * (LEAF + RANK)
GROUPS = 4
UNROLL = 16

smoothing = 0.05
inv_four_pi = 1.0 / (4.0 * math.pi)
highest = lax.Precision.HIGHEST
bf16 = jnp.bfloat16
f32 = jnp.float32
NN = (((1,), (0,)), ((), ()))
NT = (((1,), (1,)), ((), ()))
LIMIT = pltpu.CompilerParams(vmem_limit_bytes=56 * 2**20)
SMEM = pl.BlockSpec(memory_space=pltpu.SMEM)


def product(left, right, dims, precision=None):
    return lax.dot_general(left, right, dims, precision=precision, preferred_element_type=f32)


def source_rows(out, points):
    width = points.shape[1]
    out[0:3] = points
    out[3:4] = jnp.sum(points * points, axis=0, keepdims=True)
    out[4:5] = jnp.ones((1, width), f32)
    out[5:8] = jnp.zeros((3, width), f32)


def target_rows(out, points):
    width = points.shape[1]
    out[0:3] = points * -2.0
    out[3:4] = jnp.ones((1, width), f32)
    out[4:5] = jnp.sum(points * points, axis=0, keepdims=True) + smoothing * smoothing
    out[5:8] = jnp.zeros((3, width), f32)


def three(rows):
    first = rows.astype(bf16).astype(f32)
    rest = rows - first
    second = rest.astype(bf16).astype(f32)
    third = (rest - second).astype(bf16).astype(f32)
    return first, second, third


def source_features(rows):
    a, b, c = three(rows)
    return jnp.concatenate([a, a, b, a, c, b, b, c], axis=0)


def target_features(rows):
    a, b, c = three(rows)
    return jnp.concatenate([a, b, a, c, a, b, c, b], axis=0)


def two(values):
    high = values.astype(bf16)
    low = (values - high.astype(f32)).astype(bf16)
    return high, low


def fine(left, right, dims):
    rows = left.shape[0]
    high, low = two(left)
    near_high, near_low = two(right)
    both = product(jnp.concatenate([high, low], axis=0), near_high, dims)
    return both[0:rows] + both[rows : 2 * rows] + product(high, near_low, dims)


def whole(array):
    zeros = (0,) * array.ndim
    return pl.BlockSpec(array.shape, lambda i: zeros)


def upward_kernel(
    charges_ref,
    points_ref,
    weights_ref,
    basis_ref,
    nodes_ref,
    transfer_ref,
    mid_nodes_ref,
    mid_transfer_ref,
    pack_ref,
    target_ref,
    node_target_ref,
    level_ref,
    total,
    mid_rows,
):
    step = pl.program_id(0)

    @pl.when(step == 0)
    def _():
        total[...] = jnp.zeros_like(total)

    for group in range(GROUPS):
        wide = slice(group * WIDE, (group + 1) * WIDE)
        narrow = slice(group * STEP * RANK, (group + 1) * STEP * RANK)
        first = group * PACK
        charges = charges_ref[:, wide]
        pack_ref[0:NRHS, first : first + WIDE] = charges * (weights_ref[:, wide] * inv_four_pi)
        source_rows(pack_ref.at[NRHS : NRHS + 8, first : first + WIDE], points_ref[:, wide])
        target_rows(target_ref.at[:, wide], points_ref[:, wide])
        coefs = []
        for k in range(STEP):
            coefs.append(fine(charges[:, k * LEAF : (k + 1) * LEAF], basis_ref[group * STEP + k], NT))
        coef = jnp.concatenate(coefs, axis=1)
        pack_ref[0:NRHS, first + WIDE : first + PACK] = coef
        source_rows(pack_ref.at[NRHS : NRHS + 8, first + WIDE : first + PACK], nodes_ref[:, narrow])
        target_rows(node_target_ref.at[:, narrow], nodes_ref[:, narrow])
        total[...] += fine(coef, transfer_ref[:, narrow], NT)

    @pl.when(step == pl.num_programs(0) - 1)
    def _():
        mid_coef = total[...]
        top_coef = fine(mid_coef, mid_transfer_ref[...], NT)
        level_ref[0:NRHS] = jnp.concatenate([mid_coef, top_coef], axis=1)
        source_rows(mid_rows, mid_nodes_ref[...])
        level_ref[NRHS : NRHS + 8] = jnp.concatenate([mid_rows[...], jnp.zeros((8, RANK), f32)], axis=1)


def upward(charges, points, weights, basis, nodes, transfer, mid_nodes, mid_transfer):
    lanes = lambda rows, width: pl.BlockSpec((rows, width), lambda i: (0, i))
    fixed = lambda rows, width: pl.BlockSpec((rows, width), lambda i: (0, 0))
    wide, narrow, steps = GROUPS * WIDE, GROUPS * STEP * RANK, LEAF_DEV // (GROUPS * STEP)
    shape = jax.ShapeDtypeStruct
    return pl.pallas_call(
        upward_kernel,
        grid=(steps,),
        in_specs=[
            lanes(NRHS, wide),
            lanes(3, wide),
            lanes(1, wide),
            pl.BlockSpec((GROUPS * STEP, RANK, LEAF), lambda i: (i, 0, 0)),
            lanes(3, narrow),
            lanes(RANK, narrow),
            fixed(3, RANK),
            fixed(RANK, RANK),
        ],
        out_specs=[lanes(NRHS + 8, GROUPS * PACK), lanes(8, wide), lanes(8, narrow), fixed(NRHS + 8, 2 * RANK)],
        out_shape=[
            shape((NRHS + 8, steps * GROUPS * PACK), f32),
            shape((8, LEAF_DEV * LEAF), f32),
            shape((8, LEAF_DEV * RANK), f32),
            shape((NRHS + 8, 2 * RANK), f32),
        ],
        scratch_shapes=[pltpu.VMEM((NRHS, RANK), f32), pltpu.VMEM((8, RANK), f32)],
        compiler_params=LIMIT,
        name="upward",
    )(charges, points, weights, basis, nodes, transfer, mid_nodes, mid_transfer)


def lists_kernel(devices, self_ref, near_ref, count_ref, far_list_ref, list_ref, far_ref):
    myself = self_ref[0]
    partner_step = jnp.where(myself % 2 == 0, 1, devices - 1)

    def place(leaves):
        steps = lax.shift_right_logical(leaves, 5) - myself
        steps = jnp.where(steps < 0, steps + devices, steps)
        return steps == 0, jnp.where(steps == partner_step, 0, LEAF_DEV) + (leaves & (LEAF_DEV - 1))

    own, other = place(far_list_ref[...])
    far_ref[...] = jnp.where(own, far_list_ref[...] & (LEAF_DEV - 1), other + LEAF_DEV)

    leaves = near_ref[...]
    own, other = place(leaves)
    row = lax.broadcasted_iota(jnp.int32, leaves.shape, 0)
    code = (lax.shift_left(row, 6) | jnp.where(own, leaves & (LEAF_DEV - 1), other)).astype(f32)
    square = (LEAF_DEV, LEAF_DEV)
    up, across = lax.broadcasted_iota(jnp.int32, square, 0), lax.broadcasted_iota(jnp.int32, square, 1)
    counts = jnp.sum(jnp.where(up == across, jnp.broadcast_to(count_ref[...], square), 0).astype(f32), axis=1, keepdims=True)
    live = lax.broadcasted_iota(jnp.int32, leaves.shape, 1).astype(f32) < counts
    slots = (NEAR_MAX, NEAR_MAX)
    earlier_slot = lax.broadcasted_iota(jnp.int32, slots, 0) < lax.broadcasted_iota(jnp.int32, slots, 1)
    earlier_slot = jnp.where(earlier_slot, 1.0, 0.0).astype(bf16)
    earlier_row = jnp.where(across < up, 1.0, 0.0).astype(bf16)
    for phase in range(2):
        chosen = jnp.where(live, jnp.where(own, 1.0, 0.0), 0.0)
        if phase == 1:
            chosen = jnp.where(live, 1.0 - chosen, 0.0)
        mark = chosen.astype(bf16)
        before = jnp.sum(product(earlier_row, mark, NN), axis=1, keepdims=True)
        place_of = jnp.where(chosen > 0.0, before + product(mark, earlier_slot, NN), -1.0)
        length = jnp.sum(jnp.sum(chosen, axis=1, keepdims=True), axis=0, keepdims=True)
        for first in range(0, LIST, 256):
            lane = lax.broadcasted_iota(jnp.int32, (1, 256), 1) + first
            spot = lane.astype(f32)
            total = jnp.zeros((LEAF_DEV, 256), f32)
            for slot in range(NEAR_MAX):
                total = total + jnp.where(place_of[:, slot : slot + 1] == spot, code[:, slot : slot + 1], 0.0)
            words = jnp.sum(total, axis=0, keepdims=True)
            words = jnp.where(spot < length, words, float(LEAF_DEV << 6))
            words = jnp.where(lane == LIST - 1, length, words)
            list_ref[phase : phase + 1, first : first + 256] = words.astype(jnp.int32)


def lists(devices, myself, near_list, near_count, far_list):
    operands = (near_list, near_count.reshape(1, -1), far_list)
    shapes = [jax.ShapeDtypeStruct((2, LIST), jnp.int32), jax.ShapeDtypeStruct(far_list.shape, jnp.int32)]
    return pl.pallas_call(
        functools.partial(lists_kernel, devices),
        grid=(1,),
        in_specs=[SMEM] + [whole(operand) for operand in operands],
        out_specs=[whole(shape) for shape in shapes],
        out_shape=shapes,
        compiler_params=LIMIT,
        name="lists",
    )(myself, *operands)


def far_field(far_ref, packs, node_target_ref, field_ref, nodes_low, nodes_high, coef_low, coef_high):
    lower = lax.broadcasted_iota(jnp.int32, (1, 2 * RANK), 1) < RANK

    for phase, ref in enumerate(packs):

        def prepare(group, _):
            for k in range(4):
                pair = group * 4 + k
                start = (group * 2 + k // 2) * PACK + WIDE + k % 2 * (2 * RANK)
                lanes = pl.ds(pl.multiple_of(start, 2 * RANK), 2 * RANK)
                features = source_features(ref[NRHS : NRHS + 8, lanes])
                turned = jnp.concatenate([features, features], axis=0).T
                coef = ref[0:NRHS, lanes]
                swapped = pltpu.roll(coef, RANK, 1)
                for half in range(2):
                    leaf = phase * LEAF_DEV + 2 * pair + half
                    node = turned[half * RANK : (half + 1) * RANK]
                    nodes_low[leaf] = jnp.where(lower, node, 0.0).astype(bf16)
                    nodes_high[leaf] = jnp.where(lower, 0.0, node).astype(bf16)
                    left, right = (coef, swapped) if half == 0 else (swapped, coef)
                    for store, values in ((coef_low, jnp.where(lower, left, 0.0)), (coef_high, jnp.where(lower, 0.0, right))):
                        high, low = two(values)
                        store[leaf, 0:NRHS] = high
                        store[leaf, NRHS : 2 * NRHS] = low
            return 0

        lax.fori_loop(0, LEAF_DEV // 8, prepare, 0)

    def fields(quad, _):
        lanes = pl.ds(pl.multiple_of(quad * 4 * RANK, 4 * RANK), 4 * RANK)
        block = lax.broadcasted_iota(jnp.int32, (1, 4 * RANK), 1) // RANK
        features = target_features(node_target_ref[:, lanes])
        weights = jnp.concatenate([jnp.where(block == k, features, 0.0) for k in range(4)], axis=0).astype(bf16)
        total = jnp.zeros((8 * NRHS, 4 * RANK), f32)
        extra = jnp.zeros((4 * NRHS, 4 * RANK), f32)
        chunks = []
        for chunk in range(FAR2 // 4):
            leaves = [[far_ref[quad * 4 + k, chunk * 4 + f] for f in range(4)] for k in range(4)]
            parts = []
            for f in range(4):
                one = nodes_low[leaves[0][f]] + nodes_high[leaves[1][f]]
                other = nodes_low[leaves[2][f]] + nodes_high[leaves[3][f]]
                parts.append(jnp.concatenate([one, other], axis=1))
            chunks.append((leaves, product(jnp.concatenate(parts, axis=0), weights, NN)))
        for leaves, squares in chunks:
            high, low = two(lax.rsqrt(squares))
            sides = []
            for k in range(4):
                one = coef_low[leaves[k][0]] + coef_high[leaves[k][1]]
                other = coef_low[leaves[k][2]] + coef_high[leaves[k][3]]
                sides.append(jnp.concatenate([one, other], axis=1))
            total = total + product(jnp.concatenate(sides, axis=0), high, NN)
            extra = extra + product(jnp.concatenate([side[0:NRHS] for side in sides], axis=0), low, NN)
        field = jnp.zeros((NRHS, 4 * RANK), f32)
        for k in range(4):
            own = total[2 * k * NRHS : (2 * k + 1) * NRHS] + total[(2 * k + 1) * NRHS : (2 * k + 2) * NRHS]
            field = jnp.where(block == k, own + extra[k * NRHS : (k + 1) * NRHS], field)
        field_ref[:, lanes] = field * inv_four_pi
        return 0

    lax.fori_loop(0, LEAF_DEV // 4, fields, 0)


def near_kernel(phase, list_ref, *refs):
    if phase == 0:
        (pack_ref, target_ref, out_ref, source, target, sides, highs, lows) = refs
        packs = (pack_ref,)
        out_ref[...] = jnp.zeros_like(out_ref)
    else:
        (far_ref, *packs, target_ref, node_target_ref, before_ref, out_ref, field_ref) = refs[:9]
        (source, target, sides, highs, lows, *far_parts) = refs[9:]
        out_ref[...] = before_ref[...]
        far_field(far_ref, packs, node_target_ref, field_ref, *far_parts)
        packs = packs[1:]

    def prepare(group, _):
        for leaf in [group * STEP + k for k in range(STEP)]:
            lanes = pl.ds(pl.multiple_of(leaf * LEAF, LEAF), LEAF)
            packed = pl.ds(pl.multiple_of(group * PACK + (leaf - group * STEP) * LEAF, LEAF), LEAF)
            target[leaf] = target_features(target_ref[:, lanes]).astype(bf16)
            for number, pack_ref in enumerate(packs):
                features = source_features(pack_ref[NRHS : NRHS + 8, packed])
                source[number * LEAF_DEV + leaf] = features.T.astype(bf16)
                high, low = two(pack_ref[0:NRHS, packed])
                sides[number * LEAF_DEV + leaf, 0:NRHS] = high
                sides[number * LEAF_DEV + leaf, NRHS : 2 * NRHS] = low
        return 0

    lax.fori_loop(0, LEAF_DEV // STEP, prepare, 0)

    def item(index):
        code = list_ref[phase, index]
        return lax.shift_right_logical(code, 6) & 63, code & 63

    def values(index, slot):
        to, of = item(index)
        squares = product(source[of], target[to], NN)
        for row in range(0, LEAF, 64):
            high, low = two(lax.rsqrt(squares[row : row + 64]))
            highs[slot, row : row + 64] = high
            lows[slot, row : row + 64] = low

    def apply(index, slot):
        to, of = item(index)
        upper = product(sides[of], highs[slot], NN)
        lower = product(sides[of, 0:NRHS], lows[slot], NN)
        return to, upper[0:NRHS] + upper[NRHS : 2 * NRHS] + lower

    for slot in range(UNROLL):
        values(slot, slot)

    def step(number, _):
        results = []
        for slot in range(UNROLL):
            index = number * UNROLL + slot
            results.append(apply(index, slot))
            values(index + UNROLL, slot)
        for to, result in results:
            out_ref[to] += result
        return 0

    length = list_ref[phase, LIST - 1]
    lax.fori_loop(0, lax.div(length + (UNROLL - 1), UNROLL), step, 0)


def near(phase, smem, operands):
    rows, sources = LEAF_DEV + 1, LEAF_DEV * (1 + phase)
    shapes = [jax.ShapeDtypeStruct((rows, NRHS, LEAF), f32)]
    parts = []
    if phase == 1:
        shapes.append(jax.ShapeDtypeStruct((NRHS, LEAF_DEV * RANK), f32))
        parts = [pltpu.VMEM((3 * LEAF_DEV, RANK, 2 * RANK), bf16)] * 4
    return pl.pallas_call(
        functools.partial(near_kernel, phase),
        grid=(1,),
        in_specs=[SMEM] * len(smem) + [whole(operand) for operand in operands],
        out_specs=[whole(shape) for shape in shapes],
        out_shape=shapes,
        scratch_shapes=[
            pltpu.VMEM((sources, LEAF, FEAT), bf16),
            pltpu.VMEM((rows, FEAT, LEAF), bf16),
            pltpu.VMEM((sources, 2 * NRHS, LEAF), bf16),
            pltpu.VMEM((UNROLL, LEAF, LEAF), bf16),
            pltpu.VMEM((UNROLL, LEAF, LEAF), bf16),
            *parts,
        ],
        compiler_params=LIMIT,
        cost_estimate=pl.CostEstimate(flops=20_000_000_000, bytes_accessed=4_000_000, transcendentals=14_000_000),
        name="near" + str(phase),
    )(*smem, *operands)


def couple(groups, targets):
    kernels = []
    for _, rows in groups:
        kernels.append(product(targets, source_features(rows).astype(bf16), NN))
    total = jnp.zeros((2 * NRHS, RANK), f32)
    extra = jnp.zeros((NRHS, RANK), f32)
    for (coefs, _), squares in zip(groups, kernels):
        high, low = two(lax.rsqrt(squares))
        side, rest = two(coefs)
        total = total + product(jnp.concatenate([side, rest], axis=0), high, NT)
        extra = extra + product(side, low, NT)
    return total[0:NRHS] + total[NRHS : 2 * NRHS] + extra


def down_kernel(
    self_ref,
    mid_row_ref,
    top_mask_ref,
    level_ref,
    top_nodes_ref,
    mid_nodes_ref,
    mid_transfer_ref,
    transfer_ref,
    field_ref,
    near_ref,
    basis_ref,
    out_ref,
    rows,
    tops,
    down,
):
    @pl.when(pl.program_id(0) == 0)
    def _():
        down[...] = mid_field(
            self_ref, mid_row_ref, top_mask_ref, level_ref, top_nodes_ref, mid_nodes_ref, mid_transfer_ref, transfer_ref, rows, tops
        )

    leaves = GROUPS * STEP
    lanes = pl.ds(pl.multiple_of(pl.program_id(0) * (leaves * RANK), leaves * RANK), leaves * RANK)
    field = field_ref[...] + down[:, lanes]
    for leaf in range(leaves):
        far = fine(field[:, leaf * RANK : (leaf + 1) * RANK], basis_ref[leaf], NN)
        out_ref[:, leaf * LEAF : (leaf + 1) * LEAF] = far + near_ref[leaf]


def mid_field(self_ref, mid_row_ref, top_mask_ref, level_ref, top_nodes_ref, mid_nodes_ref, mid_transfer_ref, transfer_ref, rows, tops):
    parent = self_ref[1]
    lower = lax.broadcasted_iota(jnp.int32, (1, 2 * RANK), 1) < RANK

    def features(nodes):
        target_rows(rows, nodes)
        return target_features(rows[...]).T.astype(bf16)

    def beside(left, right):
        return jnp.where(lower, left, pltpu.roll(right, RANK, 1))

    source_rows(tops, top_nodes_ref[...])
    own = jnp.zeros((3, RANK), f32)
    for top in range(top_nodes_ref.shape[1] // RANK):
        own = jnp.where(parent == top, top_nodes_ref[:, top * RANK : (top + 1) * RANK], own)
    top_targets = features(own)
    groups = []
    for first in range(0, top_nodes_ref.shape[1] // RANK, 4):
        coefs = []
        for top in range(first, first + 4):
            coef = level_ref[top * GROUP, 0:NRHS]
            for member in range(1, GROUP):
                coef = coef + level_ref[top * GROUP + member, 0:NRHS]
            coefs.append(coef * top_mask_ref[parent, top].astype(f32))
        swapped = [pltpu.roll(coef, RANK, 1) for coef in coefs]
        side = [jnp.where(lower, swapped[k], coefs[k + 1]) for k in (0, 2)]
        groups.append((jnp.concatenate(side, axis=1), tops[:, first * RANK : (first + 4) * RANK]))
    top_field = couple(groups, top_targets)
    mid_targets = features(mid_nodes_ref[...])

    def step(number, total):
        groups = []
        for group in range(8):
            first = number * 32 + group * 4
            coefs = [level_ref[first + k, 0:NRHS] * mid_row_ref[0, first + k].astype(f32) for k in range(4)]
            picked = [level_ref[first + k, NRHS : NRHS + 8] for k in range(4)]
            side = [beside(coefs[0], coefs[1]), beside(coefs[2], coefs[3])]
            node = [beside(picked[0], picked[1]), beside(picked[2], picked[3])]
            groups.append((jnp.concatenate(side, axis=1), jnp.concatenate(node, axis=1)))
        return total + couple(groups, mid_targets)

    field = lax.fori_loop(0, level_ref.shape[0] // 32, step, jnp.zeros((NRHS, RANK), f32))
    field = field * inv_four_pi + fine(top_field * inv_four_pi, mid_transfer_ref[...], NN)
    return fine(field, transfer_ref[...], NN)


def downward(self_parent, mid_row, top_mask, everyone, top_nodes, mid_nodes, mid_transfer, transfer, field, near_out, basis):
    leaves = GROUPS * STEP
    fixed = (everyone, top_nodes, mid_nodes, mid_transfer, transfer)
    return pl.pallas_call(
        down_kernel,
        grid=(LEAF_DEV // leaves,),
        in_specs=[SMEM, SMEM, SMEM]
        + [whole(operand) for operand in fixed]
        + [
            pl.BlockSpec((NRHS, leaves * RANK), lambda i: (0, i)),
            pl.BlockSpec((leaves, NRHS, LEAF), lambda i: (i, 0, 0)),
            pl.BlockSpec((leaves, RANK, LEAF), lambda i: (i, 0, 0)),
        ],
        out_specs=pl.BlockSpec((NRHS, leaves * LEAF), lambda i: (0, i)),
        out_shape=jax.ShapeDtypeStruct((NRHS, LEAF_DEV * LEAF), f32),
        scratch_shapes=[
            pltpu.VMEM((8, RANK), f32),
            pltpu.VMEM((8, top_nodes.shape[1]), f32),
            pltpu.VMEM((NRHS, LEAF_DEV * RANK), f32),
        ],
        compiler_params=LIMIT,
        name="downward",
    )(self_parent, mid_row, top_mask, *fixed, field, near_out, basis)


def shards(
    charges,
    positions,
    quad_weights,
    leaf_basis,
    leaf_nodes,
    leaf_transfer,
    mid_nodes,
    mid_transfer,
    top_nodes,
    near_list,
    near_count,
    far_list,
    mid_mask,
    top_mask,
):
    devices = lax.axis_size("clus")
    myself = lax.axis_index("clus")
    partner = [(i, i ^ 1) for i in range(devices)]
    cross = [(i, (i + 1 if i % 2 else i - 1) % devices) for i in range(devices)]
    pack, targets, node_targets, level = upward(
        charges, positions, quad_weights.reshape(1, -1), leaf_basis, leaf_nodes, leaf_transfer, mid_nodes, mid_transfer
    )
    everyone = lax.all_gather(level, "clus", axis=0, tiled=False)
    pack_partner = lax.ppermute(pack, "clus", partner)
    pack_cross = lax.ppermute(pack, "clus", cross)

    self_parent = jnp.stack([myself, myself // GROUP]).astype(jnp.int32)
    items, far_codes = lists(devices, self_parent, near_list, near_count, far_list)
    (near_out,) = near(0, (items,), (pack, targets))
    near_out, field = near(1, (items, far_codes), (pack, pack_partner, pack_cross, targets, node_targets, near_out))
    return downward(
        self_parent, mid_mask, top_mask, everyone, top_nodes, mid_nodes, mid_transfer, leaf_transfer, field, near_out, leaf_basis
    )


def solution(mesh):
    in_specs = (
        P(None, "clus"),
        P(None, "clus"),
        P("clus"),
        P("clus", None, None),
        P(None, "clus"),
        P(None, "clus"),
        P(None, "clus"),
        P(None, "clus"),
        P(),
        P("clus", None),
        P("clus"),
        P("clus", None),
        P("clus", None),
        P(),
    )
    out_specs = P(None, "clus")
    return jax.shard_map(shards, mesh=mesh, in_specs=in_specs, out_specs=out_specs, check_vma=False)
```

```python
import functools
import math

import jax
import jax.numpy as jnp
from jax import lax
from jax.experimental import pallas as pl
from jax.experimental.pallas import tpu as pltpu
from jax.sharding import PartitionSpec as P

LEAF = 256
RANK = 64
NRHS = 32
LEAF_DEV = 32
NEAR_MAX = 27
FAR2 = 16
GROUP = 8

STEP = 4
LIST = 1024
FEAT = 64
WIDE = STEP * LEAF
PACK = STEP * (LEAF + RANK)
GROUPS = 4
UNROLL = 16

smoothing = 0.05
inv_four_pi = 1.0 / (4.0 * math.pi)
highest = lax.Precision.HIGHEST
bf16 = jnp.bfloat16
f32 = jnp.float32
NN = (((1,), (0,)), ((), ()))
NT = (((1,), (1,)), ((), ()))
LIMIT = pltpu.CompilerParams(vmem_limit_bytes=63 * 2**20)
SMEM = pl.BlockSpec(memory_space=pltpu.SMEM)


def product(left, right, dims, precision=None):
    return lax.dot_general(left, right, dims, precision=precision, preferred_element_type=f32)


def source_rows(out, points):
    width = points.shape[1]
    out[0:3] = points
    out[3:4] = jnp.sum(points * points, axis=0, keepdims=True)
    out[4:5] = jnp.ones((1, width), f32)
    out[5:8] = jnp.zeros((3, width), f32)


def target_rows(out, points):
    width = points.shape[1]
    out[0:3] = points * -2.0
    out[3:4] = jnp.ones((1, width), f32)
    out[4:5] = jnp.sum(points * points, axis=0, keepdims=True) + smoothing * smoothing
    out[5:8] = jnp.zeros((3, width), f32)


def three(rows):
    first = rows.astype(bf16).astype(f32)
    rest = rows - first
    second = rest.astype(bf16).astype(f32)
    third = (rest - second).astype(bf16).astype(f32)
    return first, second, third


def source_features(rows):
    a, b, c = three(rows)
    return jnp.concatenate([a, a, b, a, c, b, b, c], axis=0)


def target_features(rows):
    a, b, c = three(rows)
    return jnp.concatenate([a, b, a, c, a, b, c, b], axis=0)


def two(values):
    high = values.astype(bf16)
    low = (values - high.astype(f32)).astype(bf16)
    return high, low


def fine(left, right, dims):
    rows = left.shape[0]
    high, low = two(left)
    near_high, near_low = two(right)
    both = product(jnp.concatenate([high, low], axis=0), near_high, dims)
    return both[0:rows] + both[rows : 2 * rows] + product(high, near_low, dims)


def whole(array):
    zeros = (0,) * array.ndim
    return pl.BlockSpec(array.shape, lambda i: zeros)


def upward_kernel(
    charges_ref,
    points_ref,
    weights_ref,
    basis_ref,
    nodes_ref,
    transfer_ref,
    mid_nodes_ref,
    mid_transfer_ref,
    pack_ref,
    target_ref,
    node_target_ref,
    level_ref,
    total,
    mid_rows,
):
    step = pl.program_id(0)

    @pl.when(step == 0)
    def _():
        total[...] = jnp.zeros_like(total)

    for group in range(GROUPS):
        wide = slice(group * WIDE, (group + 1) * WIDE)
        narrow = slice(group * STEP * RANK, (group + 1) * STEP * RANK)
        first = group * PACK
        charges = charges_ref[:, wide]
        pack_ref[0:NRHS, first : first + WIDE] = charges * (weights_ref[:, wide] * inv_four_pi)
        source_rows(pack_ref.at[NRHS : NRHS + 8, first : first + WIDE], points_ref[:, wide])
        target_rows(target_ref.at[:, wide], points_ref[:, wide])
        coefs = []
        for k in range(STEP):
            coefs.append(fine(charges[:, k * LEAF : (k + 1) * LEAF], basis_ref[group * STEP + k], NT))
        coef = jnp.concatenate(coefs, axis=1)
        pack_ref[0:NRHS, first + WIDE : first + PACK] = coef
        source_rows(pack_ref.at[NRHS : NRHS + 8, first + WIDE : first + PACK], nodes_ref[:, narrow])
        target_rows(node_target_ref.at[:, narrow], nodes_ref[:, narrow])
        total[...] += fine(coef, transfer_ref[:, narrow], NT)

    @pl.when(step == pl.num_programs(0) - 1)
    def _():
        mid_coef = total[...]
        top_coef = fine(mid_coef, mid_transfer_ref[...], NT)
        level_ref[0:NRHS] = jnp.concatenate([mid_coef, top_coef], axis=1)
        source_rows(mid_rows, mid_nodes_ref[...])
        level_ref[NRHS : NRHS + 8] = jnp.concatenate([mid_rows[...], jnp.zeros((8, RANK), f32)], axis=1)


def upward(charges, points, weights, basis, nodes, transfer, mid_nodes, mid_transfer):
    lanes = lambda rows, width: pl.BlockSpec((rows, width), lambda i: (0, i))
    fixed = lambda rows, width: pl.BlockSpec((rows, width), lambda i: (0, 0))
    wide, narrow, steps = GROUPS * WIDE, GROUPS * STEP * RANK, LEAF_DEV // (GROUPS * STEP)
    shape = jax.ShapeDtypeStruct
    return pl.pallas_call(
        upward_kernel,
        grid=(steps,),
        in_specs=[
            lanes(NRHS, wide),
            lanes(3, wide),
            lanes(1, wide),
            pl.BlockSpec((GROUPS * STEP, RANK, LEAF), lambda i: (i, 0, 0)),
            lanes(3, narrow),
            lanes(RANK, narrow),
            fixed(3, RANK),
            fixed(RANK, RANK),
        ],
        out_specs=[lanes(NRHS + 8, GROUPS * PACK), lanes(8, wide), lanes(8, narrow), fixed(NRHS + 8, 2 * RANK)],
        out_shape=[
            shape((NRHS + 8, steps * GROUPS * PACK), f32),
            shape((8, LEAF_DEV * LEAF), f32),
            shape((8, LEAF_DEV * RANK), f32),
            shape((NRHS + 8, 2 * RANK), f32),
        ],
        scratch_shapes=[pltpu.VMEM((NRHS, RANK), f32), pltpu.VMEM((8, RANK), f32)],
        compiler_params=LIMIT,
        name="upward",
    )(charges, points, weights, basis, nodes, transfer, mid_nodes, mid_transfer)


def lists_kernel(devices, near_ref, count_ref, far_list_ref, list_ref, far_ref):
    myself = lax.axis_index("clus")
    partner_step = jnp.where(myself % 2 == 0, 1, devices - 1)

    def place(leaves):
        steps = lax.shift_right_logical(leaves, 5) - myself
        steps = jnp.where(steps < 0, steps + devices, steps)
        return steps == 0, jnp.where(steps == partner_step, 0, LEAF_DEV) + (leaves & (LEAF_DEV - 1))

    own, other = place(far_list_ref[...])
    far_ref[...] = jnp.where(own, far_list_ref[...] & (LEAF_DEV - 1), other + LEAF_DEV)

    leaves = near_ref[...]
    own, other = place(leaves)
    row = lax.broadcasted_iota(jnp.int32, leaves.shape, 0)
    code = (lax.shift_left(row, 6) | jnp.where(own, leaves & (LEAF_DEV - 1), other)).astype(f32)
    square = (LEAF_DEV, LEAF_DEV)
    up, across = lax.broadcasted_iota(jnp.int32, square, 0), lax.broadcasted_iota(jnp.int32, square, 1)
    counts = jnp.sum(jnp.where(up == across, jnp.broadcast_to(count_ref[...], square), 0).astype(f32), axis=1, keepdims=True)
    live = lax.broadcasted_iota(jnp.int32, leaves.shape, 1).astype(f32) < counts
    slots = (NEAR_MAX, NEAR_MAX)
    earlier_slot = lax.broadcasted_iota(jnp.int32, slots, 0) < lax.broadcasted_iota(jnp.int32, slots, 1)
    earlier_slot = jnp.where(earlier_slot, 1.0, 0.0).astype(bf16)
    earlier_row = jnp.where(across < up, 1.0, 0.0).astype(bf16)
    mine = jnp.where(live, jnp.where(own, 1.0, 0.0), 0.0)
    marks = (mine, jnp.where(live, 1.0 - mine, 0.0))
    places, lengths = [], []
    for chosen in marks:
        mark = chosen.astype(bf16)
        before = jnp.sum(product(earlier_row, mark, NN), axis=1, keepdims=True)
        places.append(before + product(mark, earlier_slot, NN))
        lengths.append(jnp.sum(jnp.sum(chosen, axis=1, keepdims=True), axis=0, keepdims=True))
    spots = jnp.where(marks[0] > 0.0, places[0], jnp.where(marks[1] > 0.0, LIST - 1.0 - places[1], -1.0))
    for first in range(0, LIST, 256):
        spot = (lax.broadcasted_iota(jnp.int32, (1, 256), 1) + first).astype(f32)
        total = jnp.zeros((LEAF_DEV, 256), f32)
        for slot in range(NEAR_MAX):
            total = total + jnp.where(spots[:, slot : slot + 1] == spot, code[:, slot : slot + 1], 0.0)
        words = jnp.sum(total, axis=0, keepdims=True)
        filled = jnp.where(spot < lengths[0], 1.0, jnp.where(spot > LIST - 1.0 - lengths[1], 1.0, 0.0))
        words = jnp.where(filled > 0.0, words, float(LEAF_DEV << 6))
        list_ref[0:1, first : first + 256] = words.astype(jnp.int32)
    lane = lax.broadcasted_iota(jnp.int32, (1, LIST), 1)
    list_ref[1:2] = jnp.where(lane == 0, lengths[0], lengths[1]).astype(jnp.int32)


def lists(devices, near_list, near_count, far_list):
    operands = (near_list, near_count.reshape(1, -1), far_list)
    shapes = [jax.ShapeDtypeStruct((2, LIST), jnp.int32), jax.ShapeDtypeStruct(far_list.shape, jnp.int32)]
    return pl.pallas_call(
        functools.partial(lists_kernel, devices),
        grid=(1,),
        in_specs=[whole(operand) for operand in operands],
        out_specs=[whole(shape) for shape in shapes],
        out_shape=shapes,
        compiler_params=LIMIT,
        name="lists",
    )(*operands)


def far_field(far_ref, packs, node_target_ref, field_ref, highs, lows, nodes_low, nodes_high, coef_low, coef_high):
    lower = lax.broadcasted_iota(jnp.int32, (1, 2 * RANK), 1) < RANK

    for phase, ref in enumerate(packs):

        def prepare(group, _):
            for k in range(4):
                pair = group * 4 + k
                start = (group * 2 + k // 2) * PACK + WIDE + k % 2 * (2 * RANK)
                lanes = pl.ds(pl.multiple_of(start, 2 * RANK), 2 * RANK)
                features = source_features(ref[NRHS : NRHS + 8, lanes])
                turned = jnp.concatenate([features, features], axis=0).T
                coef = ref[0:NRHS, lanes]
                swapped = pltpu.roll(coef, RANK, 1)
                for half in range(2):
                    leaf = phase * LEAF_DEV + 2 * pair + half
                    node = turned[half * RANK : (half + 1) * RANK]
                    nodes_low[leaf] = jnp.where(lower, node, 0.0).astype(bf16)
                    nodes_high[leaf] = jnp.where(lower, 0.0, node).astype(bf16)
                    left, right = (coef, swapped) if half == 0 else (swapped, coef)
                    for store, values in ((coef_low, jnp.where(lower, left, 0.0)), (coef_high, jnp.where(lower, 0.0, right))):
                        high, low = two(values)
                        store[leaf, 0:NRHS] = high
                        store[leaf, NRHS : 2 * NRHS] = low
            return 0

        lax.fori_loop(0, LEAF_DEV // 8, prepare, 0)

    block = lax.broadcasted_iota(jnp.int32, (1, 4 * RANK), 1) // RANK

    def span(quad):
        return pl.ds(pl.multiple_of(quad * 4 * RANK, 4 * RANK), 4 * RANK)

    def sources(quad, chunk):
        return [[far_ref[chunk * 4 + f, quad * 4 + k] for f in range(4)] for k in range(4)]

    def weights(quad):
        features = target_features(node_target_ref[:, span(quad)])
        return jnp.concatenate([jnp.where(block == k, features, 0.0) for k in range(4)], axis=0).astype(bf16)

    def values(quad, chunk, targets):
        leaves = sources(quad, chunk)
        parts = []
        for f in range(4):
            one = nodes_low[leaves[0][f]] + nodes_high[leaves[1][f]]
            other = nodes_low[leaves[2][f]] + nodes_high[leaves[3][f]]
            parts.append(jnp.concatenate([one, other], axis=1))
        squares = product(jnp.concatenate(parts, axis=0), targets, NN)
        for row in range(0, LEAF, 64):
            high, low = two(lax.rsqrt(squares[row : row + 64]))
            highs[chunk, row : row + 64] = high
            lows[chunk, row : row + 64] = low

    def apply(quad, chunk):
        leaves = sources(quad, chunk)
        sides = []
        for k in range(4):
            one = coef_low[leaves[k][0]] + coef_high[leaves[k][1]]
            other = coef_low[leaves[k][2]] + coef_high[leaves[k][3]]
            sides.append(jnp.concatenate([one, other], axis=1))
        upper = product(jnp.concatenate(sides, axis=0), highs[chunk], NN)
        lower = product(jnp.concatenate([side[0:NRHS] for side in sides], axis=0), lows[chunk], NN)
        field = jnp.zeros((NRHS, 4 * RANK), f32)
        for k in range(4):
            own = upper[2 * k * NRHS : (2 * k + 1) * NRHS] + upper[(2 * k + 1) * NRHS : (2 * k + 2) * NRHS]
            field = jnp.where(block == k, own + lower[k * NRHS : (k + 1) * NRHS], field)
        return field

    chunks = FAR2 // 4
    first = weights(0)
    for chunk in range(chunks):
        values(0, chunk, first)

    def fields(quad, _):
        later = jnp.minimum(quad + 1, LEAF_DEV // 4 - 1)
        targets = weights(later)
        field = jnp.zeros((NRHS, 4 * RANK), f32)
        for chunk in range(chunks):
            field = field + apply(quad, chunk)
            values(later, chunk, targets)
        field_ref[:, span(quad)] = field * inv_four_pi
        return 0

    lax.fori_loop(0, LEAF_DEV // 4, fields, 0)


def near_kernel(phase, list_ref, *refs):
    if phase == 0:
        (pack_ref, target_ref, out_ref, source, target, sides, highs, lows) = refs
        packs = (pack_ref,)
        out_ref[...] = jnp.zeros_like(out_ref)
    else:
        (far_ref, *packs, target_ref, node_target_ref, before_ref, out_ref, field_ref) = refs[:9]
        (source, target, sides, highs, lows, *far_parts) = refs[9:]
        out_ref[...] = before_ref[...]
        far_field(far_ref, packs, node_target_ref, field_ref, highs, lows, *far_parts)
        packs = packs[1:]

    def prepare(group, _):
        for leaf in [group * STEP + k for k in range(STEP)]:
            lanes = pl.ds(pl.multiple_of(leaf * LEAF, LEAF), LEAF)
            packed = pl.ds(pl.multiple_of(group * PACK + (leaf - group * STEP) * LEAF, LEAF), LEAF)
            target[leaf] = target_features(target_ref[:, lanes]).astype(bf16)
            for number, pack_ref in enumerate(packs):
                features = source_features(pack_ref[NRHS : NRHS + 8, packed])
                source[number * LEAF_DEV + leaf] = features.T.astype(bf16)
                high, low = two(pack_ref[0:NRHS, packed])
                sides[number * LEAF_DEV + leaf, 0:NRHS] = high
                sides[number * LEAF_DEV + leaf, NRHS : 2 * NRHS] = low
        return 0

    lax.fori_loop(0, LEAF_DEV // STEP, prepare, 0)

    def item(index):
        code = list_ref[0, index if phase == 0 else LIST - 1 - index]
        return lax.shift_right_logical(code, 6) & 63, code & (63 if phase == 1 else LEAF_DEV - 1)

    def values(index, slot):
        to, of = item(index)
        squares = product(source[of], target[to], NN)
        for row in range(0, LEAF, 64):
            high, low = two(lax.rsqrt(squares[row : row + 64]))
            highs[slot, row : row + 64] = high
            lows[slot, row : row + 64] = low

    def apply(index, slot):
        to, of = item(index)
        upper = product(sides[of], highs[slot], NN)
        lower = product(sides[of, 0:NRHS], lows[slot], NN)
        return to, upper[0:NRHS] + upper[NRHS : 2 * NRHS] + lower

    for slot in range(UNROLL):
        values(slot, slot)

    def step(number, _):
        results = []
        for slot in range(UNROLL):
            index = number * UNROLL + slot
            results.append(apply(index, slot))
            values(index + UNROLL, slot)
        for to, result in results:
            out_ref[to] += result
        return 0

    length = list_ref[1, phase]
    lax.fori_loop(0, lax.div(length + (UNROLL - 1), UNROLL), step, 0)


def near(phase, smem, operands):
    rows, sources = LEAF_DEV + 1, LEAF_DEV * (1 + phase)
    shapes = [jax.ShapeDtypeStruct((rows, NRHS, LEAF), f32)]
    parts = []
    if phase == 1:
        shapes.append(jax.ShapeDtypeStruct((NRHS, LEAF_DEV * RANK), f32))
        parts = [pltpu.VMEM((3 * LEAF_DEV, RANK, 2 * RANK), bf16)] * 4
    return pl.pallas_call(
        functools.partial(near_kernel, phase),
        grid=(1,),
        in_specs=[SMEM] * len(smem) + [whole(operand) for operand in operands],
        out_specs=[whole(shape) for shape in shapes],
        out_shape=shapes,
        scratch_shapes=[
            pltpu.VMEM((sources, LEAF, FEAT), bf16),
            pltpu.VMEM((rows, FEAT, LEAF), bf16),
            pltpu.VMEM((sources, 2 * NRHS, LEAF), bf16),
            pltpu.VMEM((UNROLL, LEAF, LEAF), bf16),
            pltpu.VMEM((UNROLL, LEAF, LEAF), bf16),
            *parts,
        ],
        compiler_params=LIMIT,
        cost_estimate=pl.CostEstimate(flops=20_000_000_000, bytes_accessed=4_000_000, transcendentals=14_000_000),
        name="near" + str(phase),
    )(*smem, *operands)


def couple(groups, targets):
    kernels = []
    for _, rows in groups:
        kernels.append(product(targets, source_features(rows).astype(bf16), NN))
    total = jnp.zeros((2 * NRHS, RANK), f32)
    extra = jnp.zeros((NRHS, RANK), f32)
    for (coefs, _), squares in zip(groups, kernels):
        high, low = two(lax.rsqrt(squares))
        side, rest = two(coefs)
        total = total + product(jnp.concatenate([side, rest], axis=0), high, NT)
        extra = extra + product(side, low, NT)
    return total[0:NRHS] + total[NRHS : 2 * NRHS] + extra


def down_kernel(
    mid_row_ref,
    top_mask_ref,
    level_ref,
    top_nodes_ref,
    mid_nodes_ref,
    mid_transfer_ref,
    transfer_ref,
    field_ref,
    near_ref,
    basis_ref,
    out_ref,
    rows,
    tops,
    down,
):
    @pl.when(pl.program_id(0) == 0)
    def _():
        down[...] = mid_field(
            mid_row_ref, top_mask_ref, level_ref, top_nodes_ref, mid_nodes_ref, mid_transfer_ref, transfer_ref, rows, tops
        )

    leaves = GROUPS * STEP
    lanes = pl.ds(pl.multiple_of(pl.program_id(0) * (leaves * RANK), leaves * RANK), leaves * RANK)
    field = field_ref[...] + down[:, lanes]
    for leaf in range(leaves):
        far = fine(field[:, leaf * RANK : (leaf + 1) * RANK], basis_ref[leaf], NN)
        out_ref[:, leaf * LEAF : (leaf + 1) * LEAF] = far + near_ref[leaf]


def mid_field(mid_row_ref, top_mask_ref, level_ref, top_nodes_ref, mid_nodes_ref, mid_transfer_ref, transfer_ref, rows, tops):
    parent = lax.axis_index("clus") // GROUP
    lower = lax.broadcasted_iota(jnp.int32, (1, 2 * RANK), 1) < RANK

    def features(nodes):
        target_rows(rows, nodes)
        return target_features(rows[...]).T.astype(bf16)

    def beside(left, right):
        return jnp.where(lower, left, pltpu.roll(right, RANK, 1))

    source_rows(tops, top_nodes_ref[...])
    own = jnp.zeros((3, RANK), f32)
    for top in range(top_nodes_ref.shape[1] // RANK):
        own = jnp.where(parent == top, top_nodes_ref[:, top * RANK : (top + 1) * RANK], own)
    top_targets = features(own)
    groups = []
    for first in range(0, top_nodes_ref.shape[1] // RANK, 4):
        coefs = []
        for top in range(first, first + 4):
            coef = level_ref[top * GROUP, 0:NRHS]
            for member in range(1, GROUP):
                coef = coef + level_ref[top * GROUP + member, 0:NRHS]
            coefs.append(coef * top_mask_ref[parent, top].astype(f32))
        swapped = [pltpu.roll(coef, RANK, 1) for coef in coefs]
        side = [jnp.where(lower, swapped[k], coefs[k + 1]) for k in (0, 2)]
        groups.append((jnp.concatenate(side, axis=1), tops[:, first * RANK : (first + 4) * RANK]))
    top_field = couple(groups, top_targets)
    mid_targets = features(mid_nodes_ref[...])

    def step(number, total):
        groups = []
        for group in range(8):
            first = number * 32 + group * 4
            coefs = [level_ref[first + k, 0:NRHS] * mid_row_ref[0, first + k].astype(f32) for k in range(4)]
            picked = [level_ref[first + k, NRHS : NRHS + 8] for k in range(4)]
            side = [beside(coefs[0], coefs[1]), beside(coefs[2], coefs[3])]
            node = [beside(picked[0], picked[1]), beside(picked[2], picked[3])]
            groups.append((jnp.concatenate(side, axis=1), jnp.concatenate(node, axis=1)))
        return total + couple(groups, mid_targets)

    field = lax.fori_loop(0, level_ref.shape[0] // 32, step, jnp.zeros((NRHS, RANK), f32))
    field = field * inv_four_pi + fine(top_field * inv_four_pi, mid_transfer_ref[...], NN)
    return fine(field, transfer_ref[...], NN)


def downward(mid_row, top_mask, everyone, top_nodes, mid_nodes, mid_transfer, transfer, field, near_out, basis):
    leaves = GROUPS * STEP
    fixed = (everyone, top_nodes, mid_nodes, mid_transfer, transfer)
    return pl.pallas_call(
        down_kernel,
        grid=(LEAF_DEV // leaves,),
        in_specs=[SMEM, SMEM]
        + [whole(operand) for operand in fixed]
        + [
            pl.BlockSpec((NRHS, leaves * RANK), lambda i: (0, i)),
            pl.BlockSpec((leaves, NRHS, LEAF), lambda i: (i, 0, 0)),
            pl.BlockSpec((leaves, RANK, LEAF), lambda i: (i, 0, 0)),
        ],
        out_specs=pl.BlockSpec((NRHS, leaves * LEAF), lambda i: (0, i)),
        out_shape=jax.ShapeDtypeStruct((NRHS, LEAF_DEV * LEAF), f32),
        scratch_shapes=[
            pltpu.VMEM((8, RANK), f32),
            pltpu.VMEM((8, top_nodes.shape[1]), f32),
            pltpu.VMEM((NRHS, LEAF_DEV * RANK), f32),
        ],
        compiler_params=LIMIT,
        name="downward",
    )(mid_row, top_mask, *fixed, field, near_out, basis)


def shards(
    charges,
    positions,
    quad_weights,
    leaf_basis,
    leaf_nodes,
    leaf_transfer,
    mid_nodes,
    mid_transfer,
    top_nodes,
    near_list,
    near_count,
    far_list,
    mid_mask,
    top_mask,
):
    devices = lax.axis_size("clus")
    partner = [(i, i ^ 1) for i in range(devices)]
    cross = [(i, (i + 1 if i % 2 else i - 1) % devices) for i in range(devices)]
    pack, targets, node_targets, level = upward(
        charges, positions, quad_weights.reshape(1, -1), leaf_basis, leaf_nodes, leaf_transfer, mid_nodes, mid_transfer
    )
    everyone = lax.all_gather(level, "clus", axis=0, tiled=False)
    pack_partner = lax.ppermute(pack, "clus", partner)
    pack_cross = lax.ppermute(pack, "clus", cross)

    items, far_codes = lists(devices, near_list, near_count, far_list.T)
    (near_out,) = near(0, (items,), (pack, targets))
    near_out, field = near(1, (items, far_codes), (pack, pack_partner, pack_cross, targets, node_targets, near_out))
    return downward(
        mid_mask, top_mask, everyone, top_nodes, mid_nodes, mid_transfer, leaf_transfer, field, near_out, leaf_basis
    )


def solution(mesh):
    in_specs = (
        P(None, "clus"),
        P(None, "clus"),
        P("clus"),
        P("clus", None, None),
        P(None, "clus"),
        P(None, "clus"),
        P(None, "clus"),
        P(None, "clus"),
        P(),
        P("clus", None),
        P("clus"),
        P("clus", None),
        P("clus", None),
        P(),
    )
    out_specs = P(None, "clus")
    return jax.shard_map(shards, mesh=mesh, in_specs=in_specs, out_specs=out_specs, check_vma=False)
```

```python
import functools
import math

import jax
import jax.numpy as jnp
from jax import lax
from jax.experimental import pallas as pl
from jax.experimental.pallas import tpu as pltpu
from jax.sharding import PartitionSpec as P

LEAF = 256
RANK = 64
NRHS = 32
LEAF_DEV = 32
NEAR_MAX = 27
FAR2 = 16
GROUP = 8

STEP = 4
LIST = 1024
FEAT = 64
WIDE = STEP * LEAF
PACK = STEP * (LEAF + RANK)
GROUPS = 4
UNROLL = 16

smoothing = 0.05
inv_four_pi = 1.0 / (4.0 * math.pi)
highest = lax.Precision.HIGHEST
bf16 = jnp.bfloat16
f32 = jnp.float32
NN = (((1,), (0,)), ((), ()))
NT = (((1,), (1,)), ((), ()))
LIMIT = pltpu.CompilerParams(vmem_limit_bytes=63 * 2**20)
SMEM = pl.BlockSpec(memory_space=pltpu.SMEM)


def product(left, right, dims, precision=None):
    return lax.dot_general(left, right, dims, precision=precision, preferred_element_type=f32)


def source_rows(out, points):
    width = points.shape[1]
    out[0:3] = points
    out[3:4] = jnp.sum(points * points, axis=0, keepdims=True)
    out[4:5] = jnp.ones((1, width), f32)
    out[5:8] = jnp.zeros((3, width), f32)


def target_rows(out, points):
    width = points.shape[1]
    out[0:3] = points * -2.0
    out[3:4] = jnp.ones((1, width), f32)
    out[4:5] = jnp.sum(points * points, axis=0, keepdims=True) + smoothing * smoothing
    out[5:8] = jnp.zeros((3, width), f32)


def three(rows):
    first = rows.astype(bf16).astype(f32)
    rest = rows - first
    second = rest.astype(bf16).astype(f32)
    third = (rest - second).astype(bf16).astype(f32)
    return first, second, third


def source_features(rows):
    a, b, c = three(rows)
    return jnp.concatenate([a, a, b, a, c, b, b, c], axis=0)


def target_features(rows):
    a, b, c = three(rows)
    return jnp.concatenate([a, b, a, c, a, b, c, b], axis=0)


def two(values):
    high = values.astype(bf16)
    low = (values - high.astype(f32)).astype(bf16)
    return high, low


def fine(left, right, dims):
    rows = left.shape[0]
    high, low = two(left)
    near_high, near_low = two(right)
    both = product(jnp.concatenate([high, low], axis=0), near_high, dims)
    return both[0:rows] + both[rows : 2 * rows] + product(high, near_low, dims)


def whole(array):
    zeros = (0,) * array.ndim
    return pl.BlockSpec(array.shape, lambda i: zeros)


def upward_kernel(
    charges_ref,
    points_ref,
    weights_ref,
    basis_ref,
    nodes_ref,
    transfer_ref,
    mid_nodes_ref,
    mid_transfer_ref,
    pack_ref,
    target_ref,
    node_target_ref,
    level_ref,
    total,
    mid_rows,
):
    step = pl.program_id(0)

    @pl.when(step == 0)
    def _():
        total[...] = jnp.zeros_like(total)

    for group in range(GROUPS):
        wide = slice(group * WIDE, (group + 1) * WIDE)
        narrow = slice(group * STEP * RANK, (group + 1) * STEP * RANK)
        first = group * PACK
        charges = charges_ref[:, wide]
        pack_ref[0:NRHS, first : first + WIDE] = charges * (weights_ref[:, wide] * inv_four_pi)
        source_rows(pack_ref.at[NRHS : NRHS + 8, first : first + WIDE], points_ref[:, wide])
        target_rows(target_ref.at[:, wide], points_ref[:, wide])
        coefs = []
        for k in range(STEP):
            coefs.append(fine(charges[:, k * LEAF : (k + 1) * LEAF], basis_ref[group * STEP + k], NT))
        coef = jnp.concatenate(coefs, axis=1)
        pack_ref[0:NRHS, first + WIDE : first + PACK] = coef
        source_rows(pack_ref.at[NRHS : NRHS + 8, first + WIDE : first + PACK], nodes_ref[:, narrow])
        target_rows(node_target_ref.at[:, narrow], nodes_ref[:, narrow])
        total[...] += fine(coef, transfer_ref[:, narrow], NT)

    @pl.when(step == pl.num_programs(0) - 1)
    def _():
        mid_coef = total[...]
        top_coef = fine(mid_coef, mid_transfer_ref[...], NT)
        level_ref[0:NRHS] = jnp.concatenate([mid_coef, top_coef], axis=1)
        source_rows(mid_rows, mid_nodes_ref[...])
        level_ref[NRHS : NRHS + 8] = jnp.concatenate([mid_rows[...], jnp.zeros((8, RANK), f32)], axis=1)


def upward(charges, points, weights, basis, nodes, transfer, mid_nodes, mid_transfer):
    lanes = lambda rows, width: pl.BlockSpec((rows, width), lambda i: (0, i))
    fixed = lambda rows, width: pl.BlockSpec((rows, width), lambda i: (0, 0))
    wide, narrow, steps = GROUPS * WIDE, GROUPS * STEP * RANK, LEAF_DEV // (GROUPS * STEP)
    shape = jax.ShapeDtypeStruct
    return pl.pallas_call(
        upward_kernel,
        grid=(steps,),
        in_specs=[
            lanes(NRHS, wide),
            lanes(3, wide),
            lanes(1, wide),
            pl.BlockSpec((GROUPS * STEP, RANK, LEAF), lambda i: (i, 0, 0)),
            lanes(3, narrow),
            lanes(RANK, narrow),
            fixed(3, RANK),
            fixed(RANK, RANK),
        ],
        out_specs=[lanes(NRHS + 8, GROUPS * PACK), lanes(8, wide), lanes(8, narrow), fixed(NRHS + 8, 2 * RANK)],
        out_shape=[
            shape((NRHS + 8, steps * GROUPS * PACK), f32),
            shape((8, LEAF_DEV * LEAF), f32),
            shape((8, LEAF_DEV * RANK), f32),
            shape((NRHS + 8, 2 * RANK), f32),
        ],
        scratch_shapes=[pltpu.VMEM((NRHS, RANK), f32), pltpu.VMEM((8, RANK), f32)],
        compiler_params=LIMIT,
        name="upward",
    )(charges, points, weights, basis, nodes, transfer, mid_nodes, mid_transfer)


def lists_kernel(devices, near_ref, count_ref, far_list_ref, list_ref, far_ref):
    myself = lax.axis_index("clus")
    partner_step = jnp.where(myself % 2 == 0, 1, devices - 1)

    def place(leaves):
        steps = lax.shift_right_logical(leaves, 5) - myself
        steps = jnp.where(steps < 0, steps + devices, steps)
        return steps == 0, jnp.where(steps == partner_step, 0, LEAF_DEV) + (leaves & (LEAF_DEV - 1))

    own, other = place(far_list_ref[...])
    far_ref[...] = jnp.where(own, far_list_ref[...] & (LEAF_DEV - 1), other + LEAF_DEV)

    leaves = near_ref[...]
    own, other = place(leaves)
    row = lax.broadcasted_iota(jnp.int32, leaves.shape, 0)
    code = (lax.shift_left(row, 6) | jnp.where(own, leaves & (LEAF_DEV - 1), other)).astype(f32)
    square = (LEAF_DEV, LEAF_DEV)
    up, across = lax.broadcasted_iota(jnp.int32, square, 0), lax.broadcasted_iota(jnp.int32, square, 1)
    counts = jnp.sum(jnp.where(up == across, jnp.broadcast_to(count_ref[...], square), 0).astype(f32), axis=1, keepdims=True)
    live = lax.broadcasted_iota(jnp.int32, leaves.shape, 1).astype(f32) < counts
    slots = (NEAR_MAX, NEAR_MAX)
    earlier_slot = lax.broadcasted_iota(jnp.int32, slots, 0) < lax.broadcasted_iota(jnp.int32, slots, 1)
    earlier_slot = jnp.where(earlier_slot, 1.0, 0.0).astype(bf16)
    earlier_row = jnp.where(across < up, 1.0, 0.0).astype(bf16)
    mine = jnp.where(live, jnp.where(own, 1.0, 0.0), 0.0)
    marks = (mine, jnp.where(live, 1.0 - mine, 0.0))
    places, lengths = [], []
    for chosen in marks:
        mark = chosen.astype(bf16)
        before = jnp.sum(product(earlier_row, mark, NN), axis=1, keepdims=True)
        places.append(before + product(mark, earlier_slot, NN))
        lengths.append(jnp.sum(jnp.sum(chosen, axis=1, keepdims=True), axis=0, keepdims=True))
    spots = jnp.where(marks[0] > 0.0, places[0], jnp.where(marks[1] > 0.0, LIST - 1.0 - places[1], -1.0))
    for first in range(0, LIST, 256):
        spot = (lax.broadcasted_iota(jnp.int32, (1, 256), 1) + first).astype(f32)
        total = jnp.zeros((LEAF_DEV, 256), f32)
        for slot in range(NEAR_MAX):
            total = total + jnp.where(spots[:, slot : slot + 1] == spot, code[:, slot : slot + 1], 0.0)
        words = jnp.sum(total, axis=0, keepdims=True)
        filled = jnp.where(spot < lengths[0], 1.0, jnp.where(spot > LIST - 1.0 - lengths[1], 1.0, 0.0))
        words = jnp.where(filled > 0.0, words, float(LEAF_DEV << 6))
        list_ref[0:1, first : first + 256] = words.astype(jnp.int32)
    lane = lax.broadcasted_iota(jnp.int32, (1, LIST), 1)
    list_ref[1:2] = jnp.where(lane == 0, lengths[0], lengths[1]).astype(jnp.int32)


def lists(devices, near_list, near_count, far_list):
    operands = (near_list, near_count.reshape(1, -1), far_list)
    shapes = [jax.ShapeDtypeStruct((2, LIST), jnp.int32), jax.ShapeDtypeStruct(far_list.shape, jnp.int32)]
    return pl.pallas_call(
        functools.partial(lists_kernel, devices),
        grid=(1,),
        in_specs=[whole(operand) for operand in operands],
        out_specs=[whole(shape) for shape in shapes],
        out_shape=shapes,
        compiler_params=LIMIT,
        name="lists",
    )(*operands)


def far_field(far_ref, packs, node_target_ref, field_ref, highs, lows, nodes_low, nodes_high, coef_low, coef_high):
    lower = lax.broadcasted_iota(jnp.int32, (1, 2 * RANK), 1) < RANK

    for phase, ref in enumerate(packs):

        def prepare(group, _):
            for k in range(4):
                pair = group * 4 + k
                start = (group * 2 + k // 2) * PACK + WIDE + k % 2 * (2 * RANK)
                lanes = pl.ds(pl.multiple_of(start, 2 * RANK), 2 * RANK)
                features = source_features(ref[NRHS : NRHS + 8, lanes])
                turned = jnp.concatenate([features, features], axis=0).T
                coef = ref[0:NRHS, lanes]
                swapped = pltpu.roll(coef, RANK, 1)
                for half in range(2):
                    leaf = phase * LEAF_DEV + 2 * pair + half
                    node = turned[half * RANK : (half + 1) * RANK]
                    nodes_low[leaf] = jnp.where(lower, node, 0.0).astype(bf16)
                    nodes_high[leaf] = jnp.where(lower, 0.0, node).astype(bf16)
                    left, right = (coef, swapped) if half == 0 else (swapped, coef)
                    for store, values in ((coef_low, jnp.where(lower, left, 0.0)), (coef_high, jnp.where(lower, 0.0, right))):
                        high, low = two(values)
                        store[leaf, 0:NRHS] = high
                        store[leaf, NRHS : 2 * NRHS] = low
            return 0

        lax.fori_loop(0, LEAF_DEV // 8, prepare, 0)

    block = lax.broadcasted_iota(jnp.int32, (1, 4 * RANK), 1) // RANK

    def span(quad):
        return pl.ds(pl.multiple_of(quad * 4 * RANK, 4 * RANK), 4 * RANK)

    def sources(quad, chunk):
        return [[far_ref[chunk * 4 + f, quad * 4 + k] for f in range(4)] for k in range(4)]

    def weights(quad):
        features = target_features(node_target_ref[:, span(quad)])
        return jnp.concatenate([jnp.where(block == k, features, 0.0) for k in range(4)], axis=0).astype(bf16)

    def values(quad, chunk, targets):
        leaves = sources(quad, chunk)
        parts = []
        for f in range(4):
            one = nodes_low[leaves[0][f]] + nodes_high[leaves[1][f]]
            other = nodes_low[leaves[2][f]] + nodes_high[leaves[3][f]]
            parts.append(jnp.concatenate([one, other], axis=1))
        squares = product(jnp.concatenate(parts, axis=0), targets, NN)
        for row in range(0, LEAF, 64):
            high, low = two(lax.rsqrt(squares[row : row + 64]))
            highs[chunk, row : row + 64] = high
            lows[chunk, row : row + 64] = low

    def apply(quad, chunk):
        leaves = sources(quad, chunk)
        sides = []
        for k in range(4):
            one = coef_low[leaves[k][0]] + coef_high[leaves[k][1]]
            other = coef_low[leaves[k][2]] + coef_high[leaves[k][3]]
            sides.append(jnp.concatenate([one, other], axis=1))
        upper = product(jnp.concatenate(sides, axis=0), highs[chunk], NN)
        lower = product(jnp.concatenate([side[0:NRHS] for side in sides], axis=0), lows[chunk], NN)
        field = jnp.zeros((NRHS, 4 * RANK), f32)
        for k in range(4):
            own = upper[2 * k * NRHS : (2 * k + 1) * NRHS] + upper[(2 * k + 1) * NRHS : (2 * k + 2) * NRHS]
            field = jnp.where(block == k, own + lower[k * NRHS : (k + 1) * NRHS], field)
        return field

    chunks = FAR2 // 4
    first = weights(0)
    for chunk in range(chunks):
        values(0, chunk, first)

    def fields(quad, _):
        later = jnp.minimum(quad + 1, LEAF_DEV // 4 - 1)
        targets = weights(later)
        field = jnp.zeros((NRHS, 4 * RANK), f32)
        for chunk in range(chunks):
            field = field + apply(quad, chunk)
            values(later, chunk, targets)
        field_ref[:, span(quad)] = field * inv_four_pi
        return 0

    lax.fori_loop(0, LEAF_DEV // 4, fields, 0)


def near_kernel(phase, list_ref, *refs):
    if phase == 0:
        (pack_ref, target_ref, out_ref, source, target, sides, highs, lows) = refs
        packs = (pack_ref,)
        out_ref[...] = jnp.zeros_like(out_ref)
    else:
        (far_ref, *packs, target_ref, node_target_ref, before_ref, out_ref, field_ref) = refs[:9]
        (source, target, sides, highs, lows, *far_parts) = refs[9:]
        out_ref[...] = before_ref[...]
        far_field(far_ref, packs, node_target_ref, field_ref, highs, lows, *far_parts)
        packs = packs[1:]

    def prepare(group, _):
        for leaf in [group * STEP + k for k in range(STEP)]:
            lanes = pl.ds(pl.multiple_of(leaf * LEAF, LEAF), LEAF)
            packed = pl.ds(pl.multiple_of(group * PACK + (leaf - group * STEP) * LEAF, LEAF), LEAF)
            target[leaf] = target_features(target_ref[:, lanes]).astype(bf16)
            for number, pack_ref in enumerate(packs):
                features = source_features(pack_ref[NRHS : NRHS + 8, packed])
                source[number * LEAF_DEV + leaf] = features.T.astype(bf16)
                high, low = two(pack_ref[0:NRHS, packed])
                sides[number * LEAF_DEV + leaf, 0:NRHS] = high
                sides[number * LEAF_DEV + leaf, NRHS : 2 * NRHS] = low
        return 0

    lax.fori_loop(0, LEAF_DEV // STEP, prepare, 0)

    def item(index):
        code = list_ref[0, index if phase == 0 else LIST - 1 - index]
        return lax.shift_right_logical(code, 6) & 63, code & (63 if phase == 1 else LEAF_DEV - 1)

    def values(index, slot):
        to, of = item(index)
        squares = product(source[of], target[to], NN)
        for row in range(0, LEAF, 64):
            high, low = two(lax.rsqrt(squares[row : row + 64]))
            highs[slot, row : row + 64] = high
            lows[slot, row : row + 64] = low

    def apply(index, slot):
        to, of = item(index)
        upper = product(sides[of], highs[slot], NN)
        lower = product(sides[of, 0:NRHS], lows[slot], NN)
        return to, upper[0:NRHS] + upper[NRHS : 2 * NRHS] + lower

    for slot in range(UNROLL):
        values(slot, slot)

    def step(number, _):
        results = []
        for slot in range(UNROLL):
            index = number * UNROLL + slot
            results.append(apply(index, slot))
            values(index + UNROLL, slot)
        for to, result in results:
            out_ref[to] += result
        return 0

    length = list_ref[1, phase]
    lax.fori_loop(0, lax.div(length + (UNROLL - 1), UNROLL), step, 0)


def near(phase, smem, operands):
    rows, sources = LEAF_DEV + 1, LEAF_DEV * (1 + phase)
    shapes = [jax.ShapeDtypeStruct((rows, NRHS, LEAF), f32)]
    parts = []
    if phase == 1:
        shapes.append(jax.ShapeDtypeStruct((NRHS, LEAF_DEV * RANK), f32))
        parts = [pltpu.VMEM((3 * LEAF_DEV, RANK, 2 * RANK), bf16)] * 4
    return pl.pallas_call(
        functools.partial(near_kernel, phase),
        grid=(1,),
        in_specs=[SMEM] * len(smem) + [whole(operand) for operand in operands],
        out_specs=[whole(shape) for shape in shapes],
        out_shape=shapes,
        scratch_shapes=[
            pltpu.VMEM((sources, LEAF, FEAT), bf16),
            pltpu.VMEM((rows, FEAT, LEAF), bf16),
            pltpu.VMEM((sources, 2 * NRHS, LEAF), bf16),
            pltpu.VMEM((UNROLL, LEAF, LEAF), bf16),
            pltpu.VMEM((UNROLL, LEAF, LEAF), bf16),
            *parts,
        ],
        compiler_params=LIMIT,
        cost_estimate=pl.CostEstimate(flops=20_000_000_000, bytes_accessed=4_000_000, transcendentals=14_000_000),
        name="near" + str(phase),
    )(*smem, *operands)


def couple(groups, targets):
    kernels = []
    for _, rows in groups:
        kernels.append(product(targets, source_features(rows).astype(bf16), NN))
    total = jnp.zeros((2 * NRHS, RANK), f32)
    extra = jnp.zeros((NRHS, RANK), f32)
    for (coefs, _), squares in zip(groups, kernels):
        high, low = two(lax.rsqrt(squares))
        side, rest = two(coefs)
        total = total + product(jnp.concatenate([side, rest], axis=0), high, NT)
        extra = extra + product(side, low, NT)
    return total[0:NRHS] + total[NRHS : 2 * NRHS] + extra


def down_kernel(
    mid_row_ref,
    top_mask_ref,
    top_nodes_ref,
    mid_nodes_ref,
    mid_transfer_ref,
    level_hbm,
    transfer_hbm,
    field_hbm,
    near_hbm,
    basis_hbm,
    out_hbm,
    level_ref,
    transfer_ref,
    field_ref,
    near_ref,
    basis_ref,
    out_ref,
    rows,
    tops,
    level_sem,
    side_sem,
    leaf_sem,
    out_sem,
):
    parent = lax.axis_index("clus") // GROUP
    block = 4 * GROUP
    blocks = level_ref.shape[0] // block
    leaves = 2 * GROUPS
    parts = LEAF_DEV // leaves
    copy = pltpu.make_async_copy
    level_copies = [
        copy(level_hbm.at[k * block : (k + 1) * block], level_ref.at[k * block : (k + 1) * block], level_sem.at[k])
        for k in range(blocks)
    ]
    side_copies = [copy(transfer_hbm, transfer_ref, side_sem.at[0]), copy(field_hbm, field_ref, side_sem.at[1])]
    near_copies, basis_copies, out_copies = [], [], []
    for k in range(parts):
        own = slice(k * leaves, (k + 1) * leaves)
        lanes = slice(k * leaves * LEAF, (k + 1) * leaves * LEAF)
        near_copies.append(copy(near_hbm.at[own], near_ref.at[own], leaf_sem.at[0, k]))
        basis_copies.append(copy(basis_hbm.at[own], basis_ref.at[own], leaf_sem.at[1, k]))
        out_copies.append(copy(out_ref.at[:, lanes], out_hbm.at[:, lanes], out_sem.at[k]))
    for started in level_copies + side_copies + basis_copies + near_copies:
        started.start()

    lower = lax.broadcasted_iota(jnp.int32, (1, 2 * RANK), 1) < RANK

    def features(nodes):
        target_rows(rows, nodes)
        return target_features(rows[...]).T.astype(bf16)

    def beside(left, right):
        return jnp.where(lower, left, pltpu.roll(right, RANK, 1))

    source_rows(tops, top_nodes_ref[...])
    own = jnp.zeros((3, RANK), f32)
    for top in range(top_nodes_ref.shape[1] // RANK):
        own = jnp.where(parent == top, top_nodes_ref[:, top * RANK : (top + 1) * RANK], own)
    top_targets = features(own)
    mid_targets = features(mid_nodes_ref[...])
    top_field = jnp.zeros((NRHS, RANK), f32)
    field = jnp.zeros((NRHS, RANK), f32)
    for number in range(blocks):
        level_copies[number].wait()
        groups, coefs = [], []
        for group in range(GROUP):
            first = number * block + group * 4
            picked = [level_ref[first + k] for k in range(4)]
            masked = [picked[k] * mid_row_ref[0, first + k].astype(f32) for k in range(4)]
            side = [beside(masked[0][0:NRHS], masked[1][0:NRHS]), beside(masked[2][0:NRHS], masked[3][0:NRHS])]
            node = [picked[k][NRHS : NRHS + 8] for k in range(4)]
            node = [beside(node[0], node[1]), beside(node[2], node[3])]
            groups.append((jnp.concatenate(side, axis=1), jnp.concatenate(node, axis=1)))
        for top in range(number * 4, number * 4 + 4):
            coef = level_ref[top * GROUP, 0:NRHS]
            for member in range(1, GROUP):
                coef = coef + level_ref[top * GROUP + member, 0:NRHS]
            coefs.append(coef * top_mask_ref[parent, top].astype(f32))
        swapped = [pltpu.roll(coef, RANK, 1) for coef in coefs]
        side = jnp.concatenate([jnp.where(lower, swapped[k], coefs[k + 1]) for k in (0, 2)], axis=1)
        top_field = top_field + couple([(side, tops[:, number * 4 * RANK : (number + 1) * 4 * RANK])], top_targets)
        field = field + couple(groups, mid_targets)
    field = field * inv_four_pi + fine(top_field * inv_four_pi, mid_transfer_ref[...], NN)
    for awaited in side_copies:
        awaited.wait()
    field_ref[...] += fine(field, transfer_ref[...], NN)
    for k in range(parts):
        basis_copies[k].wait()
        near_copies[k].wait()
        for leaf in range(k * leaves, (k + 1) * leaves):
            far = fine(field_ref[:, leaf * RANK : (leaf + 1) * RANK], basis_ref[leaf], NN)
            out_ref[:, leaf * LEAF : (leaf + 1) * LEAF] = far + near_ref[leaf]
        out_copies[k].start()
    for awaited in out_copies:
        awaited.wait()


def downward(mid_row, top_mask, everyone, top_nodes, mid_nodes, mid_transfer, transfer, field, near_out, basis):
    fixed = (top_nodes, mid_nodes, mid_transfer)
    blocks, parts = everyone.shape[0] // (4 * GROUP), LEAF_DEV // (2 * GROUPS)
    return pl.pallas_call(
        down_kernel,
        grid=(1,),
        in_specs=[SMEM, SMEM] + [whole(operand) for operand in fixed] + [pl.BlockSpec(memory_space=pl.ANY)] * 5,
        out_specs=pl.BlockSpec(memory_space=pl.ANY),
        out_shape=jax.ShapeDtypeStruct((NRHS, LEAF_DEV * LEAF), f32),
        scratch_shapes=[
            pltpu.VMEM(everyone.shape, f32),
            pltpu.VMEM(transfer.shape, f32),
            pltpu.VMEM(field.shape, f32),
            pltpu.VMEM(near_out.shape, f32),
            pltpu.VMEM(basis.shape, f32),
            pltpu.VMEM((NRHS, LEAF_DEV * LEAF), f32),
            pltpu.VMEM((8, RANK), f32),
            pltpu.VMEM((8, top_nodes.shape[1]), f32),
            pltpu.SemaphoreType.DMA((blocks,)),
            pltpu.SemaphoreType.DMA((2,)),
            pltpu.SemaphoreType.DMA((2, parts)),
            pltpu.SemaphoreType.DMA((parts,)),
        ],
        compiler_params=LIMIT,
        name="downward",
    )(mid_row, top_mask, *fixed, everyone, transfer, field, near_out, basis)


def shards(
    charges,
    positions,
    quad_weights,
    leaf_basis,
    leaf_nodes,
    leaf_transfer,
    mid_nodes,
    mid_transfer,
    top_nodes,
    near_list,
    near_count,
    far_list,
    mid_mask,
    top_mask,
):
    devices = lax.axis_size("clus")
    partner = [(i, i ^ 1) for i in range(devices)]
    cross = [(i, (i + 1 if i % 2 else i - 1) % devices) for i in range(devices)]
    pack, targets, node_targets, level = upward(
        charges, positions, quad_weights.reshape(1, -1), leaf_basis, leaf_nodes, leaf_transfer, mid_nodes, mid_transfer
    )
    everyone = lax.all_gather(level, "clus", axis=0, tiled=False)
    pack_partner = lax.ppermute(pack, "clus", partner)
    pack_cross = lax.ppermute(pack, "clus", cross)

    items, far_codes = lists(devices, near_list, near_count, far_list.T)
    (near_out,) = near(0, (items,), (pack, targets))
    near_out, field = near(1, (items, far_codes), (pack, pack_partner, pack_cross, targets, node_targets, near_out))
    return downward(
        mid_mask, top_mask, everyone, top_nodes, mid_nodes, mid_transfer, leaf_transfer, field, near_out, leaf_basis
    )


def solution(mesh):
    in_specs = (
        P(None, "clus"),
        P(None, "clus"),
        P("clus"),
        P("clus", None, None),
        P(None, "clus"),
        P(None, "clus"),
        P(None, "clus"),
        P(None, "clus"),
        P(),
        P("clus", None),
        P("clus"),
        P("clus", None),
        P("clus", None),
        P(),
    )
    out_specs = P(None, "clus")
    return jax.shard_map(shards, mesh=mesh, in_specs=in_specs, out_specs=out_specs, check_vma=False)
```

```python
import functools
import math

import jax
import jax.numpy as jnp
from jax import lax
from jax.experimental import pallas as pl
from jax.experimental.pallas import tpu as pltpu
from jax.sharding import PartitionSpec as P

LEAF = 256
RANK = 64
NRHS = 32
LEAF_DEV = 32
NEAR_MAX = 27
FAR2 = 16
GROUP = 8

STEP = 4
LIST = 1024
FEAT = 64
WIDE = STEP * LEAF
PACK = STEP * (LEAF + RANK)
GROUPS = 4
UNROLL = 16

smoothing = 0.05
inv_four_pi = 1.0 / (4.0 * math.pi)
highest = lax.Precision.HIGHEST
bf16 = jnp.bfloat16
f32 = jnp.float32
NN = (((1,), (0,)), ((), ()))
NT = (((1,), (1,)), ((), ()))
LIMIT = pltpu.CompilerParams(vmem_limit_bytes=63 * 2**20)
SMEM = pl.BlockSpec(memory_space=pltpu.SMEM)


def product(left, right, dims, precision=None):
    return lax.dot_general(left, right, dims, precision=precision, preferred_element_type=f32)


def source_rows(out, points):
    width = points.shape[1]
    out[0:3] = points
    out[3:4] = jnp.sum(points * points, axis=0, keepdims=True)
    out[4:5] = jnp.ones((1, width), f32)
    out[5:8] = jnp.zeros((3, width), f32)


def target_rows(out, points):
    width = points.shape[1]
    out[0:3] = points * -2.0
    out[3:4] = jnp.ones((1, width), f32)
    out[4:5] = jnp.sum(points * points, axis=0, keepdims=True) + smoothing * smoothing
    out[5:8] = jnp.zeros((3, width), f32)


def point_rows(part, points, fill):
    fill(part, points)
    return part[...]


def three(rows):
    first = rows.astype(bf16).astype(f32)
    rest = rows - first
    second = rest.astype(bf16).astype(f32)
    third = (rest - second).astype(bf16).astype(f32)
    return first, second, third


def source_features(rows):
    a, b, c = three(rows)
    return jnp.concatenate([a, a, b, a, c, b, b, c], axis=0)


def target_features(rows):
    a, b, c = three(rows)
    return jnp.concatenate([a, b, a, c, a, b, c, b], axis=0)


def two(values):
    high = values.astype(bf16)
    low = (values - high.astype(f32)).astype(bf16)
    return high, low


def fine(left, right, dims):
    rows = left.shape[0]
    high, low = two(left)
    near_high, near_low = two(right)
    both = product(jnp.concatenate([high, low], axis=0), near_high, dims)
    return both[0:rows] + both[rows : 2 * rows] + product(high, near_low, dims)


def whole(array):
    zeros = (0,) * array.ndim
    return pl.BlockSpec(array.shape, lambda i: zeros)


def upward_kernel(
    charges_ref,
    points_ref,
    weights_ref,
    basis_ref,
    nodes_ref,
    transfer_ref,
    mid_nodes_ref,
    mid_transfer_ref,
    pack_ref,
    target_ref,
    node_target_ref,
    level_ref,
    total,
    mid_rows,
    point_part,
    node_part,
):
    step = pl.program_id(0)

    @pl.when(step == 0)
    def _():
        total[...] = jnp.zeros_like(total)

    def work(group, _):
        wide = pl.ds(pl.multiple_of(group * WIDE, WIDE), WIDE)
        narrow = pl.ds(pl.multiple_of(group * STEP * RANK, STEP * RANK), STEP * RANK)
        packed = pl.ds(pl.multiple_of(group * PACK, STEP * RANK), WIDE)
        packed_nodes = pl.ds(pl.multiple_of(group * PACK + WIDE, STEP * RANK), STEP * RANK)
        charges = charges_ref[:, wide]
        pack_ref[0:NRHS, packed] = charges * (weights_ref[:, wide] * inv_four_pi)
        pack_ref[NRHS : NRHS + 8, packed] = point_rows(point_part, points_ref[:, wide], source_rows)
        target_ref[:, wide] = point_rows(point_part, points_ref[:, wide], target_rows)
        coefs = []
        for k in range(STEP):
            coefs.append(fine(charges[:, k * LEAF : (k + 1) * LEAF], basis_ref[group * STEP + k], NT))
        coef = jnp.concatenate(coefs, axis=1)
        pack_ref[0:NRHS, packed_nodes] = coef
        pack_ref[NRHS : NRHS + 8, packed_nodes] = point_rows(node_part, nodes_ref[:, narrow], source_rows)
        node_target_ref[:, narrow] = point_rows(node_part, nodes_ref[:, narrow], target_rows)
        total[...] += fine(coef, transfer_ref[:, narrow], NT)
        return 0

    lax.fori_loop(0, GROUPS, work, 0)

    @pl.when(step == pl.num_programs(0) - 1)
    def _():
        mid_coef = total[...]
        top_coef = fine(mid_coef, mid_transfer_ref[...], NT)
        level_ref[0:NRHS] = jnp.concatenate([mid_coef, top_coef], axis=1)
        source_rows(mid_rows, mid_nodes_ref[...])
        level_ref[NRHS : NRHS + 8] = jnp.concatenate([mid_rows[...], jnp.zeros((8, RANK), f32)], axis=1)


def upward(charges, points, weights, basis, nodes, transfer, mid_nodes, mid_transfer):
    lanes = lambda rows, width: pl.BlockSpec((rows, width), lambda i: (0, i))
    fixed = lambda rows, width: pl.BlockSpec((rows, width), lambda i: (0, 0))
    wide, narrow, steps = GROUPS * WIDE, GROUPS * STEP * RANK, LEAF_DEV // (GROUPS * STEP)
    shape = jax.ShapeDtypeStruct
    return pl.pallas_call(
        upward_kernel,
        grid=(steps,),
        in_specs=[
            lanes(NRHS, wide),
            lanes(3, wide),
            lanes(1, wide),
            pl.BlockSpec((GROUPS * STEP, RANK, LEAF), lambda i: (i, 0, 0)),
            lanes(3, narrow),
            lanes(RANK, narrow),
            fixed(3, RANK),
            fixed(RANK, RANK),
        ],
        out_specs=[lanes(NRHS + 8, GROUPS * PACK), lanes(8, wide), lanes(8, narrow), fixed(NRHS + 8, 2 * RANK)],
        out_shape=[
            shape((NRHS + 8, steps * GROUPS * PACK), f32),
            shape((8, LEAF_DEV * LEAF), f32),
            shape((8, LEAF_DEV * RANK), f32),
            shape((NRHS + 8, 2 * RANK), f32),
        ],
        scratch_shapes=[pltpu.VMEM((rows, width), f32) for rows, width in ((NRHS, RANK), (8, RANK), (8, WIDE), (8, STEP * RANK))],
        compiler_params=LIMIT,
        name="upward",
    )(charges, points, weights, basis, nodes, transfer, mid_nodes, mid_transfer)


def lists_kernel(devices, near_ref, count_ref, far_list_ref, list_ref, far_ref):
    myself = lax.axis_index("clus")
    partner_step = jnp.where(myself % 2 == 0, 1, devices - 1)

    def place(leaves):
        steps = lax.shift_right_logical(leaves, 5) - myself
        steps = jnp.where(steps < 0, steps + devices, steps)
        return steps == 0, jnp.where(steps == partner_step, 0, LEAF_DEV) + (leaves & (LEAF_DEV - 1))

    own, other = place(far_list_ref[...])
    far_ref[...] = jnp.where(own, far_list_ref[...] & (LEAF_DEV - 1), other + LEAF_DEV)

    leaves = near_ref[...]
    own, other = place(leaves)
    row = lax.broadcasted_iota(jnp.int32, leaves.shape, 0)
    code = (lax.shift_left(row, 6) | jnp.where(own, leaves & (LEAF_DEV - 1), other)).astype(f32)
    square = (LEAF_DEV, LEAF_DEV)
    up, across = lax.broadcasted_iota(jnp.int32, square, 0), lax.broadcasted_iota(jnp.int32, square, 1)
    counts = jnp.sum(jnp.where(up == across, jnp.broadcast_to(count_ref[...], square), 0).astype(f32), axis=1, keepdims=True)
    live = lax.broadcasted_iota(jnp.int32, leaves.shape, 1).astype(f32) < counts
    slots = (NEAR_MAX, NEAR_MAX)
    earlier_slot = lax.broadcasted_iota(jnp.int32, slots, 0) < lax.broadcasted_iota(jnp.int32, slots, 1)
    earlier_slot = jnp.where(earlier_slot, 1.0, 0.0).astype(bf16)
    earlier_row = jnp.where(across < up, 1.0, 0.0).astype(bf16)
    mine = jnp.where(live, jnp.where(own, 1.0, 0.0), 0.0)
    marks = (mine, jnp.where(live, 1.0 - mine, 0.0))
    places, lengths = [], []
    for chosen in marks:
        mark = chosen.astype(bf16)
        before = jnp.sum(product(earlier_row, mark, NN), axis=1, keepdims=True)
        places.append(before + product(mark, earlier_slot, NN))
        lengths.append(jnp.sum(jnp.sum(chosen, axis=1, keepdims=True), axis=0, keepdims=True))
    spots = jnp.where(marks[0] > 0.0, places[0], jnp.where(marks[1] > 0.0, LIST - 1.0 - places[1], -1.0))
    for first in range(0, LIST, 256):
        spot = (lax.broadcasted_iota(jnp.int32, (1, 256), 1) + first).astype(f32)
        total = jnp.zeros((LEAF_DEV, 256), f32)
        for slot in range(NEAR_MAX):
            total = total + jnp.where(spots[:, slot : slot + 1] == spot, code[:, slot : slot + 1], 0.0)
        words = jnp.sum(total, axis=0, keepdims=True)
        filled = jnp.where(spot < lengths[0], 1.0, jnp.where(spot > LIST - 1.0 - lengths[1], 1.0, 0.0))
        words = jnp.where(filled > 0.0, words, float(LEAF_DEV << 6))
        list_ref[0:1, first : first + 256] = words.astype(jnp.int32)
    lane = lax.broadcasted_iota(jnp.int32, (1, LIST), 1)
    list_ref[1:2] = jnp.where(lane == 0, lengths[0], lengths[1]).astype(jnp.int32)


def lists(devices, near_list, near_count, far_list):
    operands = (near_list, near_count.reshape(1, -1), far_list)
    shapes = [jax.ShapeDtypeStruct((2, LIST), jnp.int32), jax.ShapeDtypeStruct(far_list.shape, jnp.int32)]
    return pl.pallas_call(
        functools.partial(lists_kernel, devices),
        grid=(1,),
        in_specs=[whole(operand) for operand in operands],
        out_specs=[whole(shape) for shape in shapes],
        out_shape=shapes,
        compiler_params=LIMIT,
        name="lists",
    )(*operands)


def far_field(far_ref, packs, node_target_ref, field_ref, highs, lows, nodes_low, nodes_high, coef_low, coef_high):
    lower = lax.broadcasted_iota(jnp.int32, (1, 2 * RANK), 1) < RANK

    for phase, ref in enumerate(packs):

        def prepare(group, _):
            for k in range(4):
                pair = group * 4 + k
                start = (group * 2 + k // 2) * PACK + WIDE + k % 2 * (2 * RANK)
                lanes = pl.ds(pl.multiple_of(start, 2 * RANK), 2 * RANK)
                features = source_features(ref[NRHS : NRHS + 8, lanes])
                turned = jnp.concatenate([features, features], axis=0).T
                coef = ref[0:NRHS, lanes]
                swapped = pltpu.roll(coef, RANK, 1)
                for half in range(2):
                    leaf = phase * LEAF_DEV + 2 * pair + half
                    node = turned[half * RANK : (half + 1) * RANK]
                    nodes_low[leaf] = jnp.where(lower, node, 0.0).astype(bf16)
                    nodes_high[leaf] = jnp.where(lower, 0.0, node).astype(bf16)
                    left, right = (coef, swapped) if half == 0 else (swapped, coef)
                    for store, values in ((coef_low, jnp.where(lower, left, 0.0)), (coef_high, jnp.where(lower, 0.0, right))):
                        high, low = two(values)
                        store[leaf, 0:NRHS] = high
                        store[leaf, NRHS : 2 * NRHS] = low
            return 0

        lax.fori_loop(0, LEAF_DEV // 8, prepare, 0)

    block = lax.broadcasted_iota(jnp.int32, (1, 4 * RANK), 1) // RANK

    def span(quad):
        return pl.ds(pl.multiple_of(quad * 4 * RANK, 4 * RANK), 4 * RANK)

    def sources(quad, chunk):
        return [[far_ref[chunk * 4 + f, quad * 4 + k] for f in range(4)] for k in range(4)]

    def weights(quad):
        features = target_features(node_target_ref[:, span(quad)])
        return jnp.concatenate([jnp.where(block == k, features, 0.0) for k in range(4)], axis=0).astype(bf16)

    def values(quad, chunk, targets):
        leaves = sources(quad, chunk)
        parts = []
        for f in range(4):
            one = nodes_low[leaves[0][f]] + nodes_high[leaves[1][f]]
            other = nodes_low[leaves[2][f]] + nodes_high[leaves[3][f]]
            parts.append(jnp.concatenate([one, other], axis=1))
        squares = product(jnp.concatenate(parts, axis=0), targets, NN)
        for row in range(0, LEAF, 64):
            high, low = two(lax.rsqrt(squares[row : row + 64]))
            highs[chunk, row : row + 64] = high
            lows[chunk, row : row + 64] = low

    def apply(quad, chunk):
        leaves = sources(quad, chunk)
        sides = []
        for k in range(4):
            one = coef_low[leaves[k][0]] + coef_high[leaves[k][1]]
            other = coef_low[leaves[k][2]] + coef_high[leaves[k][3]]
            sides.append(jnp.concatenate([one, other], axis=1))
        upper = product(jnp.concatenate(sides, axis=0), highs[chunk], NN)
        lower = product(jnp.concatenate([side[0:NRHS] for side in sides], axis=0), lows[chunk], NN)
        field = jnp.zeros((NRHS, 4 * RANK), f32)
        for k in range(4):
            own = upper[2 * k * NRHS : (2 * k + 1) * NRHS] + upper[(2 * k + 1) * NRHS : (2 * k + 2) * NRHS]
            field = jnp.where(block == k, own + lower[k * NRHS : (k + 1) * NRHS], field)
        return field

    chunks = FAR2 // 4
    first = weights(0)
    for chunk in range(chunks):
        values(0, chunk, first)

    def fields(quad, _):
        later = jnp.minimum(quad + 1, LEAF_DEV // 4 - 1)
        targets = weights(later)
        field = jnp.zeros((NRHS, 4 * RANK), f32)
        for chunk in range(chunks):
            field = field + apply(quad, chunk)
            values(later, chunk, targets)
        field_ref[:, span(quad)] = field * inv_four_pi
        return 0

    lax.fori_loop(0, LEAF_DEV // 4, fields, 0)


def near_kernel(phase, list_ref, *refs):
    if phase == 0:
        (pack_ref, target_ref, out_ref, source, target, sides, highs, lows) = refs
        packs = (pack_ref,)
        out_ref[...] = jnp.zeros_like(out_ref)
    else:
        (far_ref, *packs, target_ref, node_target_ref, before_ref, out_ref, field_ref) = refs[:9]
        (source, target, sides, highs, lows, *far_parts) = refs[9:]
        out_ref[...] = before_ref[...]
        far_field(far_ref, packs, node_target_ref, field_ref, highs, lows, *far_parts)
        packs = packs[1:]

    def prepare(group, _):
        for leaf in [group * STEP + k for k in range(STEP)]:
            lanes = pl.ds(pl.multiple_of(leaf * LEAF, LEAF), LEAF)
            packed = pl.ds(pl.multiple_of(group * PACK + (leaf - group * STEP) * LEAF, LEAF), LEAF)
            target[leaf] = target_features(target_ref[:, lanes]).astype(bf16)
            for number, pack_ref in enumerate(packs):
                features = source_features(pack_ref[NRHS : NRHS + 8, packed])
                source[number * LEAF_DEV + leaf] = features.T.astype(bf16)
                high, low = two(pack_ref[0:NRHS, packed])
                sides[number * LEAF_DEV + leaf, 0:NRHS] = high
                sides[number * LEAF_DEV + leaf, NRHS : 2 * NRHS] = low
        return 0

    lax.fori_loop(0, LEAF_DEV // STEP, prepare, 0)

    def item(index):
        code = list_ref[0, index if phase == 0 else LIST - 1 - index]
        return lax.shift_right_logical(code, 6) & 63, code & (63 if phase == 1 else LEAF_DEV - 1)

    def values(index, slot):
        to, of = item(index)
        squares = product(source[of], target[to], NN)
        for row in range(0, LEAF, 64):
            high, low = two(lax.rsqrt(squares[row : row + 64]))
            highs[slot, row : row + 64] = high
            lows[slot, row : row + 64] = low

    def apply(index, slot):
        to, of = item(index)
        upper = product(sides[of], highs[slot], NN)
        lower = product(sides[of, 0:NRHS], lows[slot], NN)
        return to, upper[0:NRHS] + upper[NRHS : 2 * NRHS] + lower

    for slot in range(UNROLL):
        values(slot, slot)

    def step(number, _):
        results = []
        for slot in range(UNROLL):
            index = number * UNROLL + slot
            results.append(apply(index, slot))
            values(index + UNROLL, slot)
        for to, result in results:
            out_ref[to] += result
        return 0

    length = list_ref[1, phase]
    lax.fori_loop(0, lax.div(length + (UNROLL - 1), UNROLL), step, 0)


def near(phase, smem, operands):
    rows, sources = LEAF_DEV + 1, LEAF_DEV * (1 + phase)
    shapes = [jax.ShapeDtypeStruct((rows, NRHS, LEAF), f32)]
    parts = []
    if phase == 1:
        shapes.append(jax.ShapeDtypeStruct((NRHS, LEAF_DEV * RANK), f32))
        parts = [pltpu.VMEM((3 * LEAF_DEV, RANK, 2 * RANK), bf16)] * 4
    return pl.pallas_call(
        functools.partial(near_kernel, phase),
        grid=(1,),
        in_specs=[SMEM] * len(smem) + [whole(operand) for operand in operands],
        out_specs=[whole(shape) for shape in shapes],
        out_shape=shapes,
        scratch_shapes=[
            pltpu.VMEM((sources, LEAF, FEAT), bf16),
            pltpu.VMEM((rows, FEAT, LEAF), bf16),
            pltpu.VMEM((sources, 2 * NRHS, LEAF), bf16),
            pltpu.VMEM((UNROLL, LEAF, LEAF), bf16),
            pltpu.VMEM((UNROLL, LEAF, LEAF), bf16),
            *parts,
        ],
        compiler_params=LIMIT,
        cost_estimate=pl.CostEstimate(flops=20_000_000_000, bytes_accessed=4_000_000, transcendentals=14_000_000),
        name="near" + str(phase),
    )(*smem, *operands)


def couple(groups, targets):
    kernels = []
    for _, rows in groups:
        kernels.append(product(targets, source_features(rows).astype(bf16), NN))
    total = jnp.zeros((2 * NRHS, RANK), f32)
    extra = jnp.zeros((NRHS, RANK), f32)
    for (coefs, _), squares in zip(groups, kernels):
        high, low = two(lax.rsqrt(squares))
        side, rest = two(coefs)
        total = total + product(jnp.concatenate([side, rest], axis=0), high, NT)
        extra = extra + product(side, low, NT)
    return total[0:NRHS] + total[NRHS : 2 * NRHS] + extra


def down_kernel(
    mid_row_ref,
    top_mask_ref,
    top_nodes_ref,
    mid_nodes_ref,
    mid_transfer_ref,
    level_hbm,
    transfer_hbm,
    field_hbm,
    near_hbm,
    basis_hbm,
    out_hbm,
    level_ref,
    transfer_ref,
    field_ref,
    near_ref,
    basis_ref,
    out_ref,
    rows,
    tops,
    level_sem,
    side_sem,
    leaf_sem,
    out_sem,
):
    parent = lax.axis_index("clus") // GROUP
    block = 4 * GROUP
    blocks = level_ref.shape[0] // block
    parts = LEAF_DEV // STEP
    copy = pltpu.make_async_copy

    def level_copy(k):
        own = pl.ds(k * block, block)
        return copy(level_hbm.at[own], level_ref.at[own], level_sem.at[k])

    def near_copy(k):
        own = pl.ds(k * STEP, STEP)
        return copy(near_hbm.at[own], near_ref.at[own], leaf_sem.at[0, k])

    def basis_copy(k):
        own = pl.ds(k * STEP, STEP)
        return copy(basis_hbm.at[own], basis_ref.at[own], leaf_sem.at[1, k])

    def out_copy(k):
        lanes = pl.ds(pl.multiple_of(k * WIDE, WIDE), WIDE)
        return copy(out_ref.at[:, lanes], out_hbm.at[:, lanes], out_sem.at[k])

    side_copies = [copy(transfer_hbm, transfer_ref, side_sem.at[0]), copy(field_hbm, field_ref, side_sem.at[1])]
    for k in range(blocks):
        level_copy(k).start()
    for started in side_copies:
        started.start()
    for k in range(parts):
        basis_copy(k).start()
        near_copy(k).start()

    lower = lax.broadcasted_iota(jnp.int32, (1, 2 * RANK), 1) < RANK

    def features(nodes):
        target_rows(rows, nodes)
        return target_features(rows[...]).T.astype(bf16)

    def beside(left, right):
        return jnp.where(lower, left, pltpu.roll(right, RANK, 1))

    source_rows(tops, top_nodes_ref[...])
    own = jnp.zeros((3, RANK), f32)
    for top in range(top_nodes_ref.shape[1] // RANK):
        own = jnp.where(parent == top, top_nodes_ref[:, top * RANK : (top + 1) * RANK], own)
    top_targets = features(own)
    mid_targets = features(mid_nodes_ref[...])

    def step(number, fields):
        level_copy(number).wait()
        groups, coefs = [], []
        for group in range(GROUP):
            first = number * block + group * 4
            picked = [level_ref[first + k] for k in range(4)]
            masked = [picked[k] * mid_row_ref[0, first + k].astype(f32) for k in range(4)]
            side = [beside(masked[0][0:NRHS], masked[1][0:NRHS]), beside(masked[2][0:NRHS], masked[3][0:NRHS])]
            node = [picked[k][NRHS : NRHS + 8] for k in range(4)]
            node = [beside(node[0], node[1]), beside(node[2], node[3])]
            groups.append((jnp.concatenate(side, axis=1), jnp.concatenate(node, axis=1)))
        for top in [number * 4 + k for k in range(4)]:
            coef = level_ref[top * GROUP, 0:NRHS]
            for member in range(1, GROUP):
                coef = coef + level_ref[top * GROUP + member, 0:NRHS]
            coefs.append(coef * top_mask_ref[parent, top].astype(f32))
        swapped = [pltpu.roll(coef, RANK, 1) for coef in coefs]
        side = jnp.concatenate([jnp.where(lower, swapped[k], coefs[k + 1]) for k in (0, 2)], axis=1)
        picked = tops[:, pl.ds(pl.multiple_of(number * 4 * RANK, 4 * RANK), 4 * RANK)]
        return fields[0] + couple([(side, picked)], top_targets), fields[1] + couple(groups, mid_targets)

    empty = jnp.zeros((NRHS, RANK), f32)
    top_field, field = lax.fori_loop(0, blocks, step, (empty, empty))
    field = field * inv_four_pi + fine(top_field * inv_four_pi, mid_transfer_ref[...], NN)
    for awaited in side_copies:
        awaited.wait()
    field_ref[...] += fine(field, transfer_ref[...], NN)

    def finish(k, _):
        basis_copy(k).wait()
        near_copy(k).wait()
        own = field_ref[:, pl.ds(pl.multiple_of(k * STEP * RANK, STEP * RANK), STEP * RANK)]
        for leaf in range(STEP):
            far = fine(own[:, leaf * RANK : (leaf + 1) * RANK], basis_ref[k * STEP + leaf], NN)
            start = pl.multiple_of(k * WIDE + leaf * LEAF, LEAF)
            out_ref[:, pl.ds(start, LEAF)] = far + near_ref[k * STEP + leaf]
        out_copy(k).start()
        return 0

    lax.fori_loop(0, parts, finish, 0)
    for k in range(parts):
        out_copy(k).wait()


def downward(mid_row, top_mask, everyone, top_nodes, mid_nodes, mid_transfer, transfer, field, near_out, basis):
    fixed = (top_nodes, mid_nodes, mid_transfer)
    blocks, parts = everyone.shape[0] // (4 * GROUP), LEAF_DEV // STEP
    return pl.pallas_call(
        down_kernel,
        grid=(1,),
        in_specs=[SMEM, SMEM] + [whole(operand) for operand in fixed] + [pl.BlockSpec(memory_space=pl.ANY)] * 5,
        out_specs=pl.BlockSpec(memory_space=pl.ANY),
        out_shape=jax.ShapeDtypeStruct((NRHS, LEAF_DEV * LEAF), f32),
        scratch_shapes=[
            pltpu.VMEM(everyone.shape, f32),
            pltpu.VMEM(transfer.shape, f32),
            pltpu.VMEM(field.shape, f32),
            pltpu.VMEM(near_out.shape, f32),
            pltpu.VMEM(basis.shape, f32),
            pltpu.VMEM((NRHS, LEAF_DEV * LEAF), f32),
            pltpu.VMEM((8, RANK), f32),
            pltpu.VMEM((8, top_nodes.shape[1]), f32),
            pltpu.SemaphoreType.DMA((blocks,)),
            pltpu.SemaphoreType.DMA((2,)),
            pltpu.SemaphoreType.DMA((2, parts)),
            pltpu.SemaphoreType.DMA((parts,)),
        ],
        compiler_params=LIMIT,
        name="downward",
    )(mid_row, top_mask, *fixed, everyone, transfer, field, near_out, basis)


def shards(
    charges,
    positions,
    quad_weights,
    leaf_basis,
    leaf_nodes,
    leaf_transfer,
    mid_nodes,
    mid_transfer,
    top_nodes,
    near_list,
    near_count,
    far_list,
    mid_mask,
    top_mask,
):
    devices = lax.axis_size("clus")
    partner = [(i, i ^ 1) for i in range(devices)]
    cross = [(i, (i + 1 if i % 2 else i - 1) % devices) for i in range(devices)]
    pack, targets, node_targets, level = upward(
        charges, positions, quad_weights.reshape(1, -1), leaf_basis, leaf_nodes, leaf_transfer, mid_nodes, mid_transfer
    )
    everyone = lax.all_gather(level, "clus", axis=0, tiled=False)
    pack_partner = lax.ppermute(pack, "clus", partner)
    pack_cross = lax.ppermute(pack, "clus", cross)

    items, far_codes = lists(devices, near_list, near_count, far_list.T)
    (near_out,) = near(0, (items,), (pack, targets))
    near_out, field = near(1, (items, far_codes), (pack, pack_partner, pack_cross, targets, node_targets, near_out))
    return downward(
        mid_mask, top_mask, everyone, top_nodes, mid_nodes, mid_transfer, leaf_transfer, field, near_out, leaf_basis
    )


def solution(mesh):
    in_specs = (
        P(None, "clus"),
        P(None, "clus"),
        P("clus"),
        P("clus", None, None),
        P(None, "clus"),
        P(None, "clus"),
        P(None, "clus"),
        P(None, "clus"),
        P(),
        P("clus", None),
        P("clus"),
        P("clus", None),
        P("clus", None),
        P(),
    )
    out_specs = P(None, "clus")
    return jax.shard_map(shards, mesh=mesh, in_specs=in_specs, out_specs=out_specs, check_vma=False)
```

```python
import functools
import math

import jax
import jax.numpy as jnp
from jax import lax
from jax.experimental import pallas as pl
from jax.experimental.pallas import tpu as pltpu
from jax.sharding import PartitionSpec as P

LEAF = 256
RANK = 64
NRHS = 32
LEAF_DEV = 32
NEAR_MAX = 27
FAR2 = 16
GROUP = 8

STEP = 4
LIST = 1024
FEAT = 64
WIDE = STEP * LEAF
PACK = STEP * (LEAF + RANK)
GROUPS = 4
UNROLL = 16

smoothing = 0.05
inv_four_pi = 1.0 / (4.0 * math.pi)
highest = lax.Precision.HIGHEST
bf16 = jnp.bfloat16
f32 = jnp.float32
NN = (((1,), (0,)), ((), ()))
NT = (((1,), (1,)), ((), ()))
LIMIT = pltpu.CompilerParams(vmem_limit_bytes=63 * 2**20)
SMEM = pl.BlockSpec(memory_space=pltpu.SMEM)


def product(left, right, dims, precision=None):
    return lax.dot_general(left, right, dims, precision=precision, preferred_element_type=f32)


def source_rows(out, points):
    width = points.shape[1]
    out[0:3] = points
    out[3:4] = jnp.sum(points * points, axis=0, keepdims=True)
    out[4:5] = jnp.ones((1, width), f32)
    out[5:8] = jnp.zeros((3, width), f32)


def target_rows(out, points):
    width = points.shape[1]
    out[0:3] = points * -2.0
    out[3:4] = jnp.ones((1, width), f32)
    out[4:5] = jnp.sum(points * points, axis=0, keepdims=True) + smoothing * smoothing
    out[5:8] = jnp.zeros((3, width), f32)


def three(rows):
    first = rows.astype(bf16).astype(f32)
    rest = rows - first
    second = rest.astype(bf16).astype(f32)
    third = (rest - second).astype(bf16).astype(f32)
    return first, second, third


def source_features(rows):
    a, b, c = three(rows)
    return jnp.concatenate([a, a, b, a, c, b, b, c], axis=0)


def target_features(rows):
    a, b, c = three(rows)
    return jnp.concatenate([a, b, a, c, a, b, c, b], axis=0)


def two(values):
    high = values.astype(bf16)
    low = (values - high.astype(f32)).astype(bf16)
    return high, low


def fine(left, right, dims):
    rows = left.shape[0]
    high, low = two(left)
    near_high, near_low = two(right)
    both = product(jnp.concatenate([high, low], axis=0), near_high, dims)
    return both[0:rows] + both[rows : 2 * rows] + product(high, near_low, dims)


def whole(array):
    zeros = (0,) * array.ndim
    return pl.BlockSpec(array.shape, lambda i: zeros)


def upward_kernel(
    charges_ref,
    points_ref,
    weights_ref,
    basis_ref,
    nodes_ref,
    transfer_ref,
    mid_nodes_ref,
    mid_transfer_ref,
    pack_ref,
    target_ref,
    node_target_ref,
    level_ref,
    total,
    mid_rows,
):
    step = pl.program_id(0)

    @pl.when(step == 0)
    def _():
        total[...] = jnp.zeros_like(total)

    for group in range(GROUPS):
        wide = slice(group * WIDE, (group + 1) * WIDE)
        narrow = slice(group * STEP * RANK, (group + 1) * STEP * RANK)
        first = group * PACK
        charges = charges_ref[:, wide]
        pack_ref[0:NRHS, first : first + WIDE] = charges * (weights_ref[:, wide] * inv_four_pi)
        source_rows(pack_ref.at[NRHS : NRHS + 8, first : first + WIDE], points_ref[:, wide])
        target_rows(target_ref.at[:, wide], points_ref[:, wide])
        coefs = []
        for k in range(STEP):
            coefs.append(fine(charges[:, k * LEAF : (k + 1) * LEAF], basis_ref[group * STEP + k], NT))
        coef = jnp.concatenate(coefs, axis=1)
        pack_ref[0:NRHS, first + WIDE : first + PACK] = coef
        source_rows(pack_ref.at[NRHS : NRHS + 8, first + WIDE : first + PACK], nodes_ref[:, narrow])
        target_rows(node_target_ref.at[:, narrow], nodes_ref[:, narrow])
        total[...] += fine(coef, transfer_ref[:, narrow], NT)

    @pl.when(step == pl.num_programs(0) - 1)
    def _():
        mid_coef = total[...]
        top_coef = fine(mid_coef, mid_transfer_ref[...], NT)
        level_ref[0:NRHS] = jnp.concatenate([mid_coef, top_coef], axis=1)
        source_rows(mid_rows, mid_nodes_ref[...])
        level_ref[NRHS : NRHS + 8] = jnp.concatenate([mid_rows[...], jnp.zeros((8, RANK), f32)], axis=1)


def upward(charges, points, weights, basis, nodes, transfer, mid_nodes, mid_transfer):
    lanes = lambda rows, width: pl.BlockSpec((rows, width), lambda i: (0, i))
    fixed = lambda rows, width: pl.BlockSpec((rows, width), lambda i: (0, 0))
    wide, narrow, steps = GROUPS * WIDE, GROUPS * STEP * RANK, LEAF_DEV // (GROUPS * STEP)
    shape = jax.ShapeDtypeStruct
    return pl.pallas_call(
        upward_kernel,
        grid=(steps,),
        in_specs=[
            lanes(NRHS, wide),
            lanes(3, wide),
            lanes(1, wide),
            pl.BlockSpec((GROUPS * STEP, RANK, LEAF), lambda i: (i, 0, 0)),
            lanes(3, narrow),
            lanes(RANK, narrow),
            fixed(3, RANK),
            fixed(RANK, RANK),
        ],
        out_specs=[lanes(NRHS + 8, GROUPS * PACK), lanes(8, wide), lanes(8, narrow), fixed(NRHS + 8, 2 * RANK)],
        out_shape=[
            shape((NRHS + 8, steps * GROUPS * PACK), f32),
            shape((8, LEAF_DEV * LEAF), f32),
            shape((8, LEAF_DEV * RANK), f32),
            shape((NRHS + 8, 2 * RANK), f32),
        ],
        scratch_shapes=[pltpu.VMEM((NRHS, RANK), f32), pltpu.VMEM((8, RANK), f32)],
        compiler_params=LIMIT,
        name="upward",
    )(charges, points, weights, basis, nodes, transfer, mid_nodes, mid_transfer)


def lists_kernel(devices, near_ref, count_ref, far_list_ref, list_ref, far_ref):
    myself = lax.axis_index("clus")
    partner_step = jnp.where(myself % 2 == 0, 1, devices - 1)

    def place(leaves):
        steps = lax.shift_right_logical(leaves, 5) - myself
        steps = jnp.where(steps < 0, steps + devices, steps)
        return steps == 0, jnp.where(steps == partner_step, 0, LEAF_DEV) + (leaves & (LEAF_DEV - 1))

    own, other = place(far_list_ref[...])
    far_ref[...] = jnp.where(own, far_list_ref[...] & (LEAF_DEV - 1), other + LEAF_DEV)

    leaves = near_ref[...]
    own, other = place(leaves)
    row = lax.broadcasted_iota(jnp.int32, leaves.shape, 0)
    code = (lax.shift_left(row, 6) | jnp.where(own, leaves & (LEAF_DEV - 1), other)).astype(f32)
    square = (LEAF_DEV, LEAF_DEV)
    up, across = lax.broadcasted_iota(jnp.int32, square, 0), lax.broadcasted_iota(jnp.int32, square, 1)
    counts = jnp.sum(jnp.where(up == across, jnp.broadcast_to(count_ref[...], square), 0).astype(f32), axis=1, keepdims=True)
    live = lax.broadcasted_iota(jnp.int32, leaves.shape, 1).astype(f32) < counts
    slots = (NEAR_MAX, NEAR_MAX)
    earlier_slot = lax.broadcasted_iota(jnp.int32, slots, 0) < lax.broadcasted_iota(jnp.int32, slots, 1)
    earlier_slot = jnp.where(earlier_slot, 1.0, 0.0).astype(bf16)
    earlier_row = jnp.where(across < up, 1.0, 0.0).astype(bf16)
    mine = jnp.where(live, jnp.where(own, 1.0, 0.0), 0.0)
    marks = (mine, jnp.where(live, 1.0 - mine, 0.0))
    places, lengths = [], []
    for chosen in marks:
        mark = chosen.astype(bf16)
        before = jnp.sum(product(earlier_row, mark, NN), axis=1, keepdims=True)
        places.append(before + product(mark, earlier_slot, NN))
        lengths.append(jnp.sum(jnp.sum(chosen, axis=1, keepdims=True), axis=0, keepdims=True))
    spots = jnp.where(marks[0] > 0.0, places[0], jnp.where(marks[1] > 0.0, LIST - 1.0 - places[1], -1.0))
    for first in range(0, LIST, 256):
        spot = (lax.broadcasted_iota(jnp.int32, (1, 256), 1) + first).astype(f32)
        total = jnp.zeros((LEAF_DEV, 256), f32)
        for slot in range(NEAR_MAX):
            total = total + jnp.where(spots[:, slot : slot + 1] == spot, code[:, slot : slot + 1], 0.0)
        words = jnp.sum(total, axis=0, keepdims=True)
        filled = jnp.where(spot < lengths[0], 1.0, jnp.where(spot > LIST - 1.0 - lengths[1], 1.0, 0.0))
        words = jnp.where(filled > 0.0, words, float(LEAF_DEV << 6))
        list_ref[0:1, first : first + 256] = words.astype(jnp.int32)
    lane = lax.broadcasted_iota(jnp.int32, (1, LIST), 1)
    list_ref[1:2] = jnp.where(lane == 0, lengths[0], lengths[1]).astype(jnp.int32)


def lists(devices, near_list, near_count, far_list):
    operands = (near_list, near_count.reshape(1, -1), far_list)
    shapes = [jax.ShapeDtypeStruct((2, LIST), jnp.int32), jax.ShapeDtypeStruct(far_list.shape, jnp.int32)]
    return pl.pallas_call(
        functools.partial(lists_kernel, devices),
        grid=(1,),
        in_specs=[whole(operand) for operand in operands],
        out_specs=[whole(shape) for shape in shapes],
        out_shape=shapes,
        compiler_params=LIMIT,
        name="lists",
    )(*operands)


def far_field(far_ref, packs, node_target_ref, field_ref, highs, lows, nodes, coefs):
    lower = lax.broadcasted_iota(jnp.int32, (1, 2 * RANK), 1) < RANK

    for phase, ref in enumerate(packs):

        def prepare(group, _):
            for k in range(4):
                pair = group * 4 + k
                start = (group * 2 + k // 2) * PACK + WIDE + k % 2 * (2 * RANK)
                lanes = pl.ds(pl.multiple_of(start, 2 * RANK), 2 * RANK)
                features = source_features(ref[NRHS : NRHS + 8, lanes])
                turned = jnp.concatenate([features, features], axis=0).T
                coef = ref[0:NRHS, lanes]
                swapped = pltpu.roll(coef, RANK, 1)
                for half in range(2):
                    leaf = phase * LEAF_DEV + 2 * pair + half
                    nodes[leaf] = turned[half * RANK : (half + 1) * RANK].astype(bf16)
                    left, right = (coef, swapped) if half == 0 else (swapped, coef)
                    high, low = two(jnp.where(lower, left, right))
                    coefs[leaf, 0:NRHS] = high
                    coefs[leaf, NRHS : 2 * NRHS] = low
            return 0

        lax.fori_loop(0, LEAF_DEV // 8, prepare, 0)

    block = lax.broadcasted_iota(jnp.int32, (1, 4 * RANK), 1) // RANK
    left_half = lax.broadcasted_iota(jnp.int32, (RANK, 2 * RANK), 1) < RANK

    def span(quad):
        if isinstance(quad, int):
            return slice(quad * 4 * RANK, (quad + 1) * 4 * RANK)
        return pl.ds(pl.multiple_of(quad * 4 * RANK, 4 * RANK), 4 * RANK)

    def sources(quad, chunk):
        return [[far_ref[chunk * 4 + f, quad * 4 + k] for f in range(4)] for k in range(4)]

    def weights(quad):
        features = target_features(node_target_ref[:, span(quad)])
        return jnp.concatenate([jnp.where(block == k, features, 0.0) for k in range(4)], axis=0).astype(bf16)

    def values(quad, chunk, slot, targets):
        leaves = sources(quad, chunk)
        parts = []
        for f in range(4):
            one = jnp.where(left_half, nodes[leaves[0][f]], nodes[leaves[1][f]])
            other = jnp.where(left_half, nodes[leaves[2][f]], nodes[leaves[3][f]])
            parts.append(jnp.concatenate([one, other], axis=1))
        squares = product(jnp.concatenate(parts, axis=0), targets, NN)
        for row in range(0, LEAF, 64):
            high, low = two(lax.rsqrt(squares[row : row + 64]))
            highs[slot, row : row + 64] = high
            lows[slot, row : row + 64] = low

    def apply(quad, chunk, slot):
        leaves = sources(quad, chunk)
        sides = []
        for k in range(4):
            one = jnp.where(left_half, coefs[leaves[k][0]], coefs[leaves[k][1]])
            other = jnp.where(left_half, coefs[leaves[k][2]], coefs[leaves[k][3]])
            sides.append(jnp.concatenate([one, other], axis=1))
        upper = product(jnp.concatenate(sides, axis=0), highs[slot], NN)
        lower = product(jnp.concatenate([side[0:NRHS] for side in sides], axis=0), lows[slot], NN)
        field = jnp.zeros((NRHS, 4 * RANK), f32)
        for k in range(4):
            own = upper[2 * k * NRHS : (2 * k + 1) * NRHS] + upper[(2 * k + 1) * NRHS : (2 * k + 2) * NRHS]
            field = jnp.where(block == k, own + lower[k * NRHS : (k + 1) * NRHS], field)
        return field

    chunks = FAR2 // 4
    for half in range(2):
        first = weights(half)
        for chunk in range(chunks):
            values(half, chunk, half * chunks + chunk, first)

    def fields(pair, _):
        for half in range(2):
            quad = pair * 2 + half
            later = jnp.minimum(quad + 2, LEAF_DEV // 4 - 2 + half)
            targets = weights(later)
            field = jnp.zeros((NRHS, 4 * RANK), f32)
            for chunk in range(chunks):
                field = field + apply(quad, chunk, half * chunks + chunk)
                values(later, chunk, half * chunks + chunk, targets)
            field_ref[:, span(quad)] = field * inv_four_pi
        return 0

    lax.fori_loop(0, LEAF_DEV // 8, fields, 0)


def near_kernel(phase, list_ref, *refs):
    if phase == 0:
        (pack_ref, target_ref, out_ref, source, target, sides, highs, lows) = refs
        packs = (pack_ref,)
        out_ref[...] = jnp.zeros_like(out_ref)
    else:
        (far_ref, *packs, target_ref, node_target_ref, before_ref, out_ref, field_ref) = refs[:9]
        (source, target, sides, highs, lows, *far_parts) = refs[9:]
        out_ref[...] = before_ref[...]
        far_field(far_ref, packs, node_target_ref, field_ref, highs, lows, *far_parts)
        packs = packs[1:]

    def prepare(group, _):
        for leaf in [group * STEP + k for k in range(STEP)]:
            lanes = pl.ds(pl.multiple_of(leaf * LEAF, LEAF), LEAF)
            packed = pl.ds(pl.multiple_of(group * PACK + (leaf - group * STEP) * LEAF, LEAF), LEAF)
            target[leaf] = target_features(target_ref[:, lanes]).astype(bf16)
            for number, pack_ref in enumerate(packs):
                features = source_features(pack_ref[NRHS : NRHS + 8, packed])
                source[number * LEAF_DEV + leaf] = features.T.astype(bf16)
                high, low = two(pack_ref[0:NRHS, packed])
                sides[number * LEAF_DEV + leaf, 0:NRHS] = high
                sides[number * LEAF_DEV + leaf, NRHS : 2 * NRHS] = low
        return 0

    lax.fori_loop(0, LEAF_DEV // STEP, prepare, 0)

    def item(index):
        code = list_ref[0, index if phase == 0 else LIST - 1 - index]
        return lax.shift_right_logical(code, 6) & 63, code & (63 if phase == 1 else LEAF_DEV - 1)

    def values(index, slot):
        to, of = item(index)
        squares = product(source[of], target[to], NN)
        for row in range(0, LEAF, 64):
            high, low = two(lax.rsqrt(squares[row : row + 64]))
            highs[slot, row : row + 64] = high
            lows[slot, row : row + 64] = low

    def apply(index, slot):
        to, of = item(index)
        upper = product(sides[of], highs[slot], NN)
        lower = product(sides[of, 0:NRHS], lows[slot], NN)
        return to, upper[0:NRHS] + upper[NRHS : 2 * NRHS] + lower

    for slot in range(UNROLL):
        values(slot, slot)

    def step(number, _):
        results = []
        for slot in range(UNROLL):
            index = number * UNROLL + slot
            results.append(apply(index, slot))
            values(index + UNROLL, slot)
        for to, result in results:
            out_ref[to] += result
        return 0

    length = list_ref[1, phase]
    lax.fori_loop(0, lax.div(length + (UNROLL - 1), UNROLL), step, 0)


def near(phase, smem, operands):
    rows, sources = LEAF_DEV + 1, LEAF_DEV * (1 + phase)
    shapes = [jax.ShapeDtypeStruct((rows, NRHS, LEAF), f32)]
    parts = []
    if phase == 1:
        shapes.append(jax.ShapeDtypeStruct((NRHS, LEAF_DEV * RANK), f32))
        parts = [pltpu.VMEM((3 * LEAF_DEV, RANK, 2 * RANK), bf16)] * 2
    return pl.pallas_call(
        functools.partial(near_kernel, phase),
        grid=(1,),
        in_specs=[SMEM] * len(smem) + [whole(operand) for operand in operands],
        out_specs=[whole(shape) for shape in shapes],
        out_shape=shapes,
        scratch_shapes=[
            pltpu.VMEM((sources, LEAF, FEAT), bf16),
            pltpu.VMEM((rows, FEAT, LEAF), bf16),
            pltpu.VMEM((sources, 2 * NRHS, LEAF), bf16),
            pltpu.VMEM((UNROLL, LEAF, LEAF), bf16),
            pltpu.VMEM((UNROLL, LEAF, LEAF), bf16),
            *parts,
        ],
        compiler_params=LIMIT,
        cost_estimate=pl.CostEstimate(flops=20_000_000_000, bytes_accessed=4_000_000, transcendentals=14_000_000),
        name="near" + str(phase),
    )(*smem, *operands)


def couple(groups, targets):
    kernels = []
    for _, rows in groups:
        kernels.append(product(targets, source_features(rows).astype(bf16), NN))
    total = jnp.zeros((2 * NRHS, RANK), f32)
    extra = jnp.zeros((NRHS, RANK), f32)
    for (coefs, _), squares in zip(groups, kernels):
        high, low = two(lax.rsqrt(squares))
        side, rest = two(coefs)
        total = total + product(jnp.concatenate([side, rest], axis=0), high, NT)
        extra = extra + product(side, low, NT)
    return total[0:NRHS] + total[NRHS : 2 * NRHS] + extra


def down_kernel(
    mid_row_ref,
    top_mask_ref,
    top_nodes_ref,
    mid_nodes_ref,
    mid_transfer_ref,
    level_hbm,
    transfer_hbm,
    field_hbm,
    near_hbm,
    basis_hbm,
    out_hbm,
    level_ref,
    transfer_ref,
    field_ref,
    near_ref,
    basis_ref,
    out_ref,
    rows,
    tops,
    level_sem,
    side_sem,
    leaf_sem,
    out_sem,
):
    parent = lax.axis_index("clus") // GROUP
    block = 4 * GROUP
    blocks = level_ref.shape[0] // block
    leaves = 2 * GROUPS
    parts = LEAF_DEV // leaves
    copy = pltpu.make_async_copy
    level_copies = [
        copy(level_hbm.at[k * block : (k + 1) * block], level_ref.at[k * block : (k + 1) * block], level_sem.at[k])
        for k in range(blocks)
    ]
    side_copies = [copy(transfer_hbm, transfer_ref, side_sem.at[0]), copy(field_hbm, field_ref, side_sem.at[1])]
    near_copies, basis_copies, out_copies = [], [], []
    for k in range(parts):
        own = slice(k * leaves, (k + 1) * leaves)
        lanes = slice(k * leaves * LEAF, (k + 1) * leaves * LEAF)
        near_copies.append(copy(near_hbm.at[own], near_ref.at[own], leaf_sem.at[0, k]))
        basis_copies.append(copy(basis_hbm.at[own], basis_ref.at[own], leaf_sem.at[1, k]))
        out_copies.append(copy(out_ref.at[:, lanes], out_hbm.at[:, lanes], out_sem.at[k]))
    for started in level_copies + side_copies + basis_copies + near_copies:
        started.start()

    lower = lax.broadcasted_iota(jnp.int32, (1, 2 * RANK), 1) < RANK

    def features(nodes):
        target_rows(rows, nodes)
        return target_features(rows[...]).T.astype(bf16)

    def beside(left, right):
        return jnp.where(lower, left, pltpu.roll(right, RANK, 1))

    source_rows(tops, top_nodes_ref[...])
    own = jnp.zeros((3, RANK), f32)
    for top in range(top_nodes_ref.shape[1] // RANK):
        own = jnp.where(parent == top, top_nodes_ref[:, top * RANK : (top + 1) * RANK], own)
    top_targets = features(own)
    mid_targets = features(mid_nodes_ref[...])
    top_field = jnp.zeros((NRHS, RANK), f32)
    field = jnp.zeros((NRHS, RANK), f32)
    for number in range(blocks):
        level_copies[number].wait()
        groups, coefs = [], []
        for group in range(GROUP):
            first = number * block + group * 4
            picked = [level_ref[first + k] for k in range(4)]
            masked = [picked[k] * mid_row_ref[0, first + k].astype(f32) for k in range(4)]
            side = [beside(masked[0][0:NRHS], masked[1][0:NRHS]), beside(masked[2][0:NRHS], masked[3][0:NRHS])]
            node = [picked[k][NRHS : NRHS + 8] for k in range(4)]
            node = [beside(node[0], node[1]), beside(node[2], node[3])]
            groups.append((jnp.concatenate(side, axis=1), jnp.concatenate(node, axis=1)))
        for top in range(number * 4, number * 4 + 4):
            coef = level_ref[top * GROUP, 0:NRHS]
            for member in range(1, GROUP):
                coef = coef + level_ref[top * GROUP + member, 0:NRHS]
            coefs.append(coef * top_mask_ref[parent, top].astype(f32))
        swapped = [pltpu.roll(coef, RANK, 1) for coef in coefs]
        side = jnp.concatenate([jnp.where(lower, swapped[k], coefs[k + 1]) for k in (0, 2)], axis=1)
        top_field = top_field + couple([(side, tops[:, number * 4 * RANK : (number + 1) * 4 * RANK])], top_targets)
        field = field + couple(groups, mid_targets)
    field = field * inv_four_pi + fine(top_field * inv_four_pi, mid_transfer_ref[...], NN)
    for awaited in side_copies:
        awaited.wait()
    field_ref[...] += fine(field, transfer_ref[...], NN)
    for k in range(parts):
        basis_copies[k].wait()
        near_copies[k].wait()
        for leaf in range(k * leaves, (k + 1) * leaves):
            far = fine(field_ref[:, leaf * RANK : (leaf + 1) * RANK], basis_ref[leaf], NN)
            out_ref[:, leaf * LEAF : (leaf + 1) * LEAF] = far + near_ref[leaf]
        out_copies[k].start()
    for awaited in out_copies:
        awaited.wait()


def downward(mid_row, top_mask, everyone, top_nodes, mid_nodes, mid_transfer, transfer, field, near_out, basis):
    fixed = (top_nodes, mid_nodes, mid_transfer)
    blocks, parts = everyone.shape[0] // (4 * GROUP), LEAF_DEV // (2 * GROUPS)
    return pl.pallas_call(
        down_kernel,
        grid=(1,),
        in_specs=[SMEM, SMEM] + [whole(operand) for operand in fixed] + [pl.BlockSpec(memory_space=pl.ANY)] * 5,
        out_specs=pl.BlockSpec(memory_space=pl.ANY),
        out_shape=jax.ShapeDtypeStruct((NRHS, LEAF_DEV * LEAF), f32),
        scratch_shapes=[
            pltpu.VMEM(everyone.shape, f32),
            pltpu.VMEM(transfer.shape, f32),
            pltpu.VMEM(field.shape, f32),
            pltpu.VMEM(near_out.shape, f32),
            pltpu.VMEM(basis.shape, f32),
            pltpu.VMEM((NRHS, LEAF_DEV * LEAF), f32),
            pltpu.VMEM((8, RANK), f32),
            pltpu.VMEM((8, top_nodes.shape[1]), f32),
            pltpu.SemaphoreType.DMA((blocks,)),
            pltpu.SemaphoreType.DMA((2,)),
            pltpu.SemaphoreType.DMA((2, parts)),
            pltpu.SemaphoreType.DMA((parts,)),
        ],
        compiler_params=LIMIT,
        name="downward",
    )(mid_row, top_mask, *fixed, everyone, transfer, field, near_out, basis)


def shards(
    charges,
    positions,
    quad_weights,
    leaf_basis,
    leaf_nodes,
    leaf_transfer,
    mid_nodes,
    mid_transfer,
    top_nodes,
    near_list,
    near_count,
    far_list,
    mid_mask,
    top_mask,
):
    devices = lax.axis_size("clus")
    partner = [(i, i ^ 1) for i in range(devices)]
    cross = [(i, (i + 1 if i % 2 else i - 1) % devices) for i in range(devices)]
    pack, targets, node_targets, level = upward(
        charges, positions, quad_weights.reshape(1, -1), leaf_basis, leaf_nodes, leaf_transfer, mid_nodes, mid_transfer
    )
    everyone = lax.all_gather(level, "clus", axis=0, tiled=False)
    pack_partner = lax.ppermute(pack, "clus", partner)
    pack_cross = lax.ppermute(pack, "clus", cross)

    items, far_codes = lists(devices, near_list, near_count, far_list.T)
    (near_out,) = near(0, (items,), (pack, targets))
    near_out, field = near(1, (items, far_codes), (pack, pack_partner, pack_cross, targets, node_targets, near_out))
    return downward(
        mid_mask, top_mask, everyone, top_nodes, mid_nodes, mid_transfer, leaf_transfer, field, near_out, leaf_basis
    )


def solution(mesh):
    in_specs = (
        P(None, "clus"),
        P(None, "clus"),
        P("clus"),
        P("clus", None, None),
        P(None, "clus"),
        P(None, "clus"),
        P(None, "clus"),
        P(None, "clus"),
        P(),
        P("clus", None),
        P("clus"),
        P("clus", None),
        P("clus", None),
        P(),
    )
    out_specs = P(None, "clus")
    return jax.shard_map(shards, mesh=mesh, in_specs=in_specs, out_specs=out_specs, check_vma=False)
```

```python
import functools
import math

import jax
import jax.numpy as jnp
from jax import lax
from jax.experimental import pallas as pl
from jax.experimental.pallas import tpu as pltpu
from jax.sharding import PartitionSpec as P

LEAF = 256
RANK = 64
NRHS = 32
LEAF_DEV = 32
NEAR_MAX = 27
FAR2 = 16
GROUP = 8

STEP = 4
LIST = 1024
FEAT = 64
WIDE = STEP * LEAF
PACK = STEP * (LEAF + RANK)
GROUPS = 4
UNROLL = 16

smoothing = 0.05
inv_four_pi = 1.0 / (4.0 * math.pi)
highest = lax.Precision.HIGHEST
bf16 = jnp.bfloat16
f32 = jnp.float32
NN = (((1,), (0,)), ((), ()))
NT = (((1,), (1,)), ((), ()))
LIMIT = pltpu.CompilerParams(vmem_limit_bytes=63 * 2**20)
SMEM = pl.BlockSpec(memory_space=pltpu.SMEM)


def product(left, right, dims, precision=None):
    return lax.dot_general(left, right, dims, precision=precision, preferred_element_type=f32)


def source_rows(out, points):
    width = points.shape[1]
    out[0:3] = points
    out[3:4] = jnp.sum(points * points, axis=0, keepdims=True)
    out[4:5] = jnp.ones((1, width), f32)
    out[5:8] = jnp.zeros((3, width), f32)


def target_rows(out, points):
    width = points.shape[1]
    out[0:3] = points * -2.0
    out[3:4] = jnp.ones((1, width), f32)
    out[4:5] = jnp.sum(points * points, axis=0, keepdims=True) + smoothing * smoothing
    out[5:8] = jnp.zeros((3, width), f32)


def three(rows):
    first = rows.astype(bf16).astype(f32)
    rest = rows - first
    second = rest.astype(bf16).astype(f32)
    third = (rest - second).astype(bf16).astype(f32)
    return first, second, third


def source_features(rows):
    a, b, c = three(rows)
    return jnp.concatenate([a, a, b, a, c, b, b, c], axis=0)


def target_features(rows):
    a, b, c = three(rows)
    return jnp.concatenate([a, b, a, c, a, b, c, b], axis=0)


def two(values):
    high = values.astype(bf16)
    low = (values - high.astype(f32)).astype(bf16)
    return high, low


def fine(left, right, dims):
    rows = left.shape[0]
    high, low = two(left)
    near_high, near_low = two(right)
    both = product(jnp.concatenate([high, low], axis=0), near_high, dims)
    return both[0:rows] + both[rows : 2 * rows] + product(high, near_low, dims)


def whole(array):
    zeros = (0,) * array.ndim
    return pl.BlockSpec(array.shape, lambda i: zeros)


def upward_kernel(
    charges_ref,
    points_ref,
    weights_ref,
    basis_ref,
    nodes_ref,
    transfer_ref,
    mid_nodes_ref,
    mid_transfer_ref,
    pack_ref,
    target_ref,
    node_target_ref,
    level_ref,
    total,
    mid_rows,
):
    step = pl.program_id(0)

    @pl.when(step == 0)
    def _():
        total[...] = jnp.zeros_like(total)

    for group in range(GROUPS):
        wide = slice(group * WIDE, (group + 1) * WIDE)
        narrow = slice(group * STEP * RANK, (group + 1) * STEP * RANK)
        first = group * PACK
        charges = charges_ref[:, wide]
        pack_ref[0:NRHS, first : first + WIDE] = charges * (weights_ref[:, wide] * inv_four_pi)
        source_rows(pack_ref.at[NRHS : NRHS + 8, first : first + WIDE], points_ref[:, wide])
        target_rows(target_ref.at[:, wide], points_ref[:, wide])
        coefs = []
        for k in range(STEP):
            coefs.append(fine(charges[:, k * LEAF : (k + 1) * LEAF], basis_ref[group * STEP + k], NT))
        coef = jnp.concatenate(coefs, axis=1)
        pack_ref[0:NRHS, first + WIDE : first + PACK] = coef
        source_rows(pack_ref.at[NRHS : NRHS + 8, first + WIDE : first + PACK], nodes_ref[:, narrow])
        target_rows(node_target_ref.at[:, narrow], nodes_ref[:, narrow])
        total[...] += fine(coef, transfer_ref[:, narrow], NT)

    @pl.when(step == pl.num_programs(0) - 1)
    def _():
        mid_coef = total[...]
        top_coef = fine(mid_coef, mid_transfer_ref[...], NT)
        level_ref[0:NRHS] = jnp.concatenate([mid_coef, top_coef], axis=1)
        source_rows(mid_rows, mid_nodes_ref[...])
        level_ref[NRHS : NRHS + 8] = jnp.concatenate([mid_rows[...], jnp.zeros((8, RANK), f32)], axis=1)


def upward(charges, points, weights, basis, nodes, transfer, mid_nodes, mid_transfer):
    lanes = lambda rows, width: pl.BlockSpec((rows, width), lambda i: (0, i))
    fixed = lambda rows, width: pl.BlockSpec((rows, width), lambda i: (0, 0))
    wide, narrow, steps = GROUPS * WIDE, GROUPS * STEP * RANK, LEAF_DEV // (GROUPS * STEP)
    shape = jax.ShapeDtypeStruct
    return pl.pallas_call(
        upward_kernel,
        grid=(steps,),
        in_specs=[
            lanes(NRHS, wide),
            lanes(3, wide),
            lanes(1, wide),
            pl.BlockSpec((GROUPS * STEP, RANK, LEAF), lambda i: (i, 0, 0)),
            lanes(3, narrow),
            lanes(RANK, narrow),
            fixed(3, RANK),
            fixed(RANK, RANK),
        ],
        out_specs=[lanes(NRHS + 8, GROUPS * PACK), lanes(8, wide), lanes(8, narrow), fixed(NRHS + 8, 2 * RANK)],
        out_shape=[
            shape((NRHS + 8, steps * GROUPS * PACK), f32),
            shape((8, LEAF_DEV * LEAF), f32),
            shape((8, LEAF_DEV * RANK), f32),
            shape((NRHS + 8, 2 * RANK), f32),
        ],
        scratch_shapes=[pltpu.VMEM((NRHS, RANK), f32), pltpu.VMEM((8, RANK), f32)],
        compiler_params=LIMIT,
        name="upward",
    )(charges, points, weights, basis, nodes, transfer, mid_nodes, mid_transfer)


def lists_kernel(devices, near_ref, count_ref, far_list_ref, list_ref, far_ref):
    myself = lax.axis_index("clus")
    partner_step = jnp.where(myself % 2 == 0, 1, devices - 1)

    def place(leaves):
        steps = lax.shift_right_logical(leaves, 5) - myself
        steps = jnp.where(steps < 0, steps + devices, steps)
        return steps == 0, jnp.where(steps == partner_step, 0, LEAF_DEV) + (leaves & (LEAF_DEV - 1))

    own, other = place(far_list_ref[...])
    far_ref[...] = jnp.where(own, far_list_ref[...] & (LEAF_DEV - 1), other + LEAF_DEV)

    leaves = near_ref[...]
    own, other = place(leaves)
    row = lax.broadcasted_iota(jnp.int32, leaves.shape, 0)
    code = (lax.shift_left(row, 6) | jnp.where(own, leaves & (LEAF_DEV - 1), other)).astype(f32)
    square = (LEAF_DEV, LEAF_DEV)
    up, across = lax.broadcasted_iota(jnp.int32, square, 0), lax.broadcasted_iota(jnp.int32, square, 1)
    counts = jnp.sum(jnp.where(up == across, jnp.broadcast_to(count_ref[...], square), 0).astype(f32), axis=1, keepdims=True)
    live = lax.broadcasted_iota(jnp.int32, leaves.shape, 1).astype(f32) < counts
    slots = (NEAR_MAX, NEAR_MAX)
    earlier_slot = lax.broadcasted_iota(jnp.int32, slots, 0) < lax.broadcasted_iota(jnp.int32, slots, 1)
    earlier_slot = jnp.where(earlier_slot, 1.0, 0.0).astype(bf16)
    earlier_row = jnp.where(across < up, 1.0, 0.0).astype(bf16)
    mine = jnp.where(live, jnp.where(own, 1.0, 0.0), 0.0)
    marks = (mine, jnp.where(live, 1.0 - mine, 0.0))
    places, lengths = [], []
    for chosen in marks:
        mark = chosen.astype(bf16)
        before = jnp.sum(product(earlier_row, mark, NN), axis=1, keepdims=True)
        places.append(before + product(mark, earlier_slot, NN))
        lengths.append(jnp.sum(jnp.sum(chosen, axis=1, keepdims=True), axis=0, keepdims=True))
    spots = jnp.where(marks[0] > 0.0, places[0], jnp.where(marks[1] > 0.0, LIST - 1.0 - places[1], -1.0))
    for first in range(0, LIST, 256):
        spot = (lax.broadcasted_iota(jnp.int32, (1, 256), 1) + first).astype(f32)
        total = jnp.zeros((LEAF_DEV, 256), f32)
        for slot in range(NEAR_MAX):
            total = total + jnp.where(spots[:, slot : slot + 1] == spot, code[:, slot : slot + 1], 0.0)
        words = jnp.sum(total, axis=0, keepdims=True)
        filled = jnp.where(spot < lengths[0], 1.0, jnp.where(spot > LIST - 1.0 - lengths[1], 1.0, 0.0))
        words = jnp.where(filled > 0.0, words, float(LEAF_DEV << 6))
        list_ref[0:1, first : first + 256] = words.astype(jnp.int32)
    lane = lax.broadcasted_iota(jnp.int32, (1, LIST), 1)
    list_ref[1:2] = jnp.where(lane == 0, lengths[0], lengths[1]).astype(jnp.int32)


def lists(devices, near_list, near_count, far_list):
    operands = (near_list, near_count.reshape(1, -1), far_list)
    shapes = [jax.ShapeDtypeStruct((2, LIST), jnp.int32), jax.ShapeDtypeStruct(far_list.shape, jnp.int32)]
    return pl.pallas_call(
        functools.partial(lists_kernel, devices),
        grid=(1,),
        in_specs=[whole(operand) for operand in operands],
        out_specs=[whole(shape) for shape in shapes],
        out_shape=shapes,
        compiler_params=LIMIT,
        name="lists",
    )(*operands)


def far_field(far_ref, packs, node_target_ref, field_ref, highs, lows, nodes, coefs):
    lower = lax.broadcasted_iota(jnp.int32, (1, 2 * RANK), 1) < RANK

    for phase, ref in enumerate(packs):

        def prepare(group, _):
            for k in range(4):
                pair = group * 4 + k
                start = (group * 2 + k // 2) * PACK + WIDE + k % 2 * (2 * RANK)
                lanes = pl.ds(pl.multiple_of(start, 2 * RANK), 2 * RANK)
                features = source_features(ref[NRHS : NRHS + 8, lanes])
                turned = jnp.concatenate([features, features], axis=0).T
                coef = ref[0:NRHS, lanes]
                swapped = pltpu.roll(coef, RANK, 1)
                for half in range(2):
                    leaf = phase * LEAF_DEV + 2 * pair + half
                    nodes[leaf] = turned[half * RANK : (half + 1) * RANK].astype(bf16)
                    left, right = (coef, swapped) if half == 0 else (swapped, coef)
                    high, low = two(jnp.where(lower, left, right))
                    coefs[leaf, 0:NRHS] = high
                    coefs[leaf, NRHS : 2 * NRHS] = low
            return 0

        lax.fori_loop(0, LEAF_DEV // 8, prepare, 0)

    block = lax.broadcasted_iota(jnp.int32, (1, 4 * RANK), 1) // RANK
    left_half = lax.broadcasted_iota(jnp.int32, (RANK, 2 * RANK), 1) < RANK

    def span(quad):
        if isinstance(quad, int):
            return slice(quad * 4 * RANK, (quad + 1) * 4 * RANK)
        return pl.ds(pl.multiple_of(quad * 4 * RANK, 4 * RANK), 4 * RANK)

    def sources(quad, chunk):
        return [[far_ref[chunk * 4 + f, quad * 4 + k] for f in range(4)] for k in range(4)]

    def weights(quad):
        features = target_features(node_target_ref[:, span(quad)])
        return jnp.concatenate([jnp.where(block == k, features, 0.0) for k in range(4)], axis=0).astype(bf16)

    def values(quad, chunk, slot, targets):
        leaves = sources(quad, chunk)
        parts = []
        for f in range(4):
            one = jnp.where(left_half, nodes[leaves[0][f]], nodes[leaves[1][f]])
            other = jnp.where(left_half, nodes[leaves[2][f]], nodes[leaves[3][f]])
            parts.append(jnp.concatenate([one, other], axis=1))
        squares = product(jnp.concatenate(parts, axis=0), targets, NN)
        for row in range(0, LEAF, 64):
            high, low = two(lax.rsqrt(squares[row : row + 64]))
            highs[slot, row : row + 64] = high
            lows[slot, row : row + 64] = low

    def apply(quad, chunk, slot):
        leaves = sources(quad, chunk)
        sides = []
        for k in range(4):
            one = jnp.where(left_half, coefs[leaves[k][0]], coefs[leaves[k][1]])
            other = jnp.where(left_half, coefs[leaves[k][2]], coefs[leaves[k][3]])
            sides.append(jnp.concatenate([one, other], axis=1))
        upper = product(jnp.concatenate(sides, axis=0), highs[slot], NN)
        lower = product(jnp.concatenate([side[0:NRHS] for side in sides], axis=0), lows[slot], NN)
        field = jnp.zeros((NRHS, 4 * RANK), f32)
        for k in range(4):
            own = upper[2 * k * NRHS : (2 * k + 1) * NRHS] + upper[(2 * k + 1) * NRHS : (2 * k + 2) * NRHS]
            field = jnp.where(block == k, own + lower[k * NRHS : (k + 1) * NRHS], field)
        return field

    chunks = FAR2 // 4
    for half in range(2):
        first = weights(half)
        for chunk in range(chunks):
            values(half, chunk, half * chunks + chunk, first)

    def fields(pair, _):
        for half in range(2):
            quad = pair * 2 + half
            later = jnp.minimum(quad + 2, LEAF_DEV // 4 - 2 + half)
            targets = weights(later)
            field = jnp.zeros((NRHS, 4 * RANK), f32)
            for chunk in range(chunks):
                field = field + apply(quad, chunk, half * chunks + chunk)
                values(later, chunk, half * chunks + chunk, targets)
            field_ref[:, span(quad)] = field * inv_four_pi
        return 0

    lax.fori_loop(0, LEAF_DEV // 8, fields, 0)


def near_kernel(phase, list_ref, *refs):
    if phase == 0:
        (pack_ref, target_ref, out_ref, source, target, sides, highs, lows) = refs
        packs = (pack_ref,)
        out_ref[...] = jnp.zeros_like(out_ref)
    else:
        (far_ref, *packs, target_ref, node_target_ref, before_ref, out_ref, field_ref) = refs[:9]
        (source, target, sides, highs, lows, *far_parts) = refs[9:]
        out_ref[...] = before_ref[...]
        far_field(far_ref, packs, node_target_ref, field_ref, highs, lows, *far_parts)
        packs = packs[1:]

    def prepare(group, _):
        for leaf in [group * STEP + k for k in range(STEP)]:
            lanes = pl.ds(pl.multiple_of(leaf * LEAF, LEAF), LEAF)
            packed = pl.ds(pl.multiple_of(group * PACK + (leaf - group * STEP) * LEAF, LEAF), LEAF)
            target[leaf] = target_features(target_ref[:, lanes]).astype(bf16)
            for number, pack_ref in enumerate(packs):
                features = source_features(pack_ref[NRHS : NRHS + 8, packed])
                source[number * LEAF_DEV + leaf] = features.T.astype(bf16)
                high, low = two(pack_ref[0:NRHS, packed])
                sides[number * LEAF_DEV + leaf, 0:NRHS] = high
                sides[number * LEAF_DEV + leaf, NRHS : 2 * NRHS] = low
        return 0

    lax.fori_loop(0, LEAF_DEV // STEP, prepare, 0)

    def item(index):
        code = list_ref[0, index if phase == 0 else LIST - 1 - index]
        return lax.shift_right_logical(code, 6) & 63, code & (63 if phase == 1 else LEAF_DEV - 1)

    def values(index, slot):
        to, of = item(index)
        squares = product(source[of], target[to], NN)
        for row in range(0, LEAF, 64):
            high, low = two(lax.rsqrt(squares[row : row + 64]))
            highs[slot, row : row + 64] = high
            lows[slot, row : row + 64] = low

    def apply(index, slot):
        to, of = item(index)
        upper = product(sides[of], highs[slot], NN)
        lower = product(sides[of, 0:NRHS], lows[slot], NN)
        return to, upper[0:NRHS] + upper[NRHS : 2 * NRHS] + lower

    for slot in range(UNROLL):
        values(slot, slot)

    def step(number, _):
        results = []
        for slot in range(UNROLL):
            index = number * UNROLL + slot
            results.append(apply(index, slot))
            values(index + UNROLL, slot)
        for to, result in results:
            out_ref[to] += result
        return 0

    length = list_ref[1, phase]
    lax.fori_loop(0, lax.div(length + (UNROLL - 1), UNROLL), step, 0)


def near(phase, smem, operands):
    rows, sources = LEAF_DEV + 1, LEAF_DEV * (1 + phase)
    shapes = [jax.ShapeDtypeStruct((rows, NRHS, LEAF), f32)]
    parts = []
    if phase == 1:
        shapes.append(jax.ShapeDtypeStruct((NRHS, LEAF_DEV * RANK), f32))
        parts = [pltpu.VMEM((3 * LEAF_DEV, RANK, 2 * RANK), bf16)] * 2
    return pl.pallas_call(
        functools.partial(near_kernel, phase),
        grid=(1,),
        in_specs=[SMEM] * len(smem) + [whole(operand) for operand in operands],
        out_specs=[whole(shape) for shape in shapes],
        out_shape=shapes,
        scratch_shapes=[
            pltpu.VMEM((sources, LEAF, FEAT), bf16),
            pltpu.VMEM((rows, FEAT, LEAF), bf16),
            pltpu.VMEM((sources, 2 * NRHS, LEAF), bf16),
            pltpu.VMEM((UNROLL, LEAF, LEAF), bf16),
            pltpu.VMEM((UNROLL, LEAF, LEAF), bf16),
            *parts,
        ],
        compiler_params=LIMIT,
        cost_estimate=pl.CostEstimate(flops=20_000_000_000, bytes_accessed=4_000_000, transcendentals=14_000_000),
        name="near" + str(phase),
    )(*smem, *operands)


def couple(groups, targets):
    kernels = []
    for _, rows in groups:
        kernels.append(product(targets, source_features(rows).astype(bf16), NN))
    total = jnp.zeros((2 * NRHS, RANK), f32)
    extra = jnp.zeros((NRHS, RANK), f32)
    for (coefs, _), squares in zip(groups, kernels):
        high, low = two(lax.rsqrt(squares))
        side, rest = two(coefs)
        total = total + product(jnp.concatenate([side, rest], axis=0), high, NT)
        extra = extra + product(side, low, NT)
    return total[0:NRHS] + total[NRHS : 2 * NRHS] + extra


def down_kernel(
    mid_row_ref,
    top_mask_ref,
    top_nodes_ref,
    mid_nodes_ref,
    mid_transfer_ref,
    level_hbm,
    transfer_hbm,
    field_hbm,
    near_hbm,
    basis_hbm,
    out_hbm,
    level_ref,
    transfer_ref,
    field_ref,
    near_ref,
    basis_ref,
    out_ref,
    rows,
    tops,
    level_sem,
    side_sem,
    leaf_sem,
    out_sem,
):
    parent = lax.axis_index("clus") // GROUP
    block = 4 * GROUP
    blocks = level_ref.shape[0] // block
    leaves = 2 * GROUPS
    parts = LEAF_DEV // leaves
    copy = pltpu.make_async_copy
    level_copies = [
        copy(level_hbm.at[k * block : (k + 1) * block], level_ref.at[k * block : (k + 1) * block], level_sem.at[k])
        for k in range(blocks)
    ]
    side_copies = [copy(transfer_hbm, transfer_ref, side_sem.at[0]), copy(field_hbm, field_ref, side_sem.at[1])]
    near_copies, basis_copies, out_copies = [], [], []
    for k in range(parts):
        own = slice(k * leaves, (k + 1) * leaves)
        lanes = slice(k * leaves * LEAF, (k + 1) * leaves * LEAF)
        near_copies.append(copy(near_hbm.at[own], near_ref.at[own], leaf_sem.at[0, k]))
        basis_copies.append(copy(basis_hbm.at[own], basis_ref.at[own], leaf_sem.at[1, k]))
        out_copies.append(copy(out_ref.at[:, lanes], out_hbm.at[:, lanes], out_sem.at[k]))
    for started in level_copies + side_copies + basis_copies + near_copies:
        started.start()

    lower = lax.broadcasted_iota(jnp.int32, (1, 2 * RANK), 1) < RANK

    def features(nodes):
        target_rows(rows, nodes)
        return target_features(rows[...]).T.astype(bf16)

    def beside(left, right):
        return jnp.where(lower, left, pltpu.roll(right, RANK, 1))

    source_rows(tops, top_nodes_ref[...])
    own = jnp.zeros((3, RANK), f32)
    for top in range(top_nodes_ref.shape[1] // RANK):
        own = jnp.where(parent == top, top_nodes_ref[:, top * RANK : (top + 1) * RANK], own)
    top_targets = features(own)
    mid_targets = features(mid_nodes_ref[...])
    top_field = jnp.zeros((NRHS, RANK), f32)
    field = jnp.zeros((NRHS, RANK), f32)
    for number in range(blocks):
        level_copies[number].wait()
        groups, coefs = [], []
        for group in range(GROUP):
            first = number * block + group * 4
            picked = [level_ref[first + k] for k in range(4)]
            masked = [picked[k] * mid_row_ref[0, first + k].astype(f32) for k in range(4)]
            side = [beside(masked[0][0:NRHS], masked[1][0:NRHS]), beside(masked[2][0:NRHS], masked[3][0:NRHS])]
            node = [picked[k][NRHS : NRHS + 8] for k in range(4)]
            node = [beside(node[0], node[1]), beside(node[2], node[3])]
            groups.append((jnp.concatenate(side, axis=1), jnp.concatenate(node, axis=1)))
        for top in range(number * 4, number * 4 + 4):
            coef = level_ref[top * GROUP, 0:NRHS]
            for member in range(1, GROUP):
                coef = coef + level_ref[top * GROUP + member, 0:NRHS]
            coefs.append(coef * top_mask_ref[parent, top].astype(f32))
        swapped = [pltpu.roll(coef, RANK, 1) for coef in coefs]
        side = jnp.concatenate([jnp.where(lower, swapped[k], coefs[k + 1]) for k in (0, 2)], axis=1)
        top_field = top_field + couple([(side, tops[:, number * 4 * RANK : (number + 1) * 4 * RANK])], top_targets)
        field = field + couple(groups, mid_targets)
    field = field * inv_four_pi + fine(top_field * inv_four_pi, mid_transfer_ref[...], NN)
    for awaited in side_copies:
        awaited.wait()
    field_ref[...] += fine(field, transfer_ref[...], NN)
    for k in range(parts):
        basis_copies[k].wait()
        near_copies[k].wait()
        for leaf in range(k * leaves, (k + 1) * leaves):
            far = fine(field_ref[:, leaf * RANK : (leaf + 1) * RANK], basis_ref[leaf], NN)
            out_ref[:, leaf * LEAF : (leaf + 1) * LEAF] = far + near_ref[leaf]
        out_copies[k].start()
    for awaited in out_copies:
        awaited.wait()


def downward(mid_row, top_mask, everyone, top_nodes, mid_nodes, mid_transfer, transfer, field, near_out, basis):
    fixed = (top_nodes, mid_nodes, mid_transfer)
    blocks, parts = everyone.shape[0] // (4 * GROUP), LEAF_DEV // (2 * GROUPS)
    return pl.pallas_call(
        down_kernel,
        grid=(1,),
        in_specs=[SMEM, SMEM] + [whole(operand) for operand in fixed] + [pl.BlockSpec(memory_space=pl.ANY)] * 5,
        out_specs=pl.BlockSpec(memory_space=pl.ANY),
        out_shape=jax.ShapeDtypeStruct((NRHS, LEAF_DEV * LEAF), f32),
        scratch_shapes=[
            pltpu.VMEM(everyone.shape, f32),
            pltpu.VMEM(transfer.shape, f32),
            pltpu.VMEM(field.shape, f32),
            pltpu.VMEM(near_out.shape, f32),
            pltpu.VMEM(basis.shape, f32),
            pltpu.VMEM((NRHS, LEAF_DEV * LEAF), f32),
            pltpu.VMEM((8, RANK), f32),
            pltpu.VMEM((8, top_nodes.shape[1]), f32),
            pltpu.SemaphoreType.DMA((blocks,)),
            pltpu.SemaphoreType.DMA((2,)),
            pltpu.SemaphoreType.DMA((2, parts)),
            pltpu.SemaphoreType.DMA((parts,)),
        ],
        compiler_params=LIMIT,
        name="downward",
    )(mid_row, top_mask, *fixed, everyone, transfer, field, near_out, basis)


def shards(
    charges,
    positions,
    quad_weights,
    leaf_basis,
    leaf_nodes,
    leaf_transfer,
    mid_nodes,
    mid_transfer,
    top_nodes,
    near_list,
    near_count,
    far_list,
    mid_mask,
    top_mask,
):
    devices = lax.axis_size("clus")
    partner = [(i, i ^ 1) for i in range(devices)]
    cross = [(i, (i + 1 if i % 2 else i - 1) % devices) for i in range(devices)]
    pack, targets, node_targets, level = upward(
        charges, positions, quad_weights.reshape(1, -1), leaf_basis, leaf_nodes, leaf_transfer, mid_nodes, mid_transfer
    )
    everyone = lax.all_gather(level, "clus", axis=0, tiled=False)
    items, far_codes = lists(devices, near_list, near_count, far_list.T)
    pack, items = lax.optimization_barrier((pack, items))
    pack_partner = lax.ppermute(pack, "clus", partner)
    pack_cross = lax.ppermute(pack, "clus", cross)

    (near_out,) = near(0, (items,), (pack, targets))
    near_out, field = near(1, (items, far_codes), (pack, pack_partner, pack_cross, targets, node_targets, near_out))
    return downward(
        mid_mask, top_mask, everyone, top_nodes, mid_nodes, mid_transfer, leaf_transfer, field, near_out, leaf_basis
    )


def solution(mesh):
    in_specs = (
        P(None, "clus"),
        P(None, "clus"),
        P("clus"),
        P("clus", None, None),
        P(None, "clus"),
        P(None, "clus"),
        P(None, "clus"),
        P(None, "clus"),
        P(),
        P("clus", None),
        P("clus"),
        P("clus", None),
        P("clus", None),
        P(),
    )
    out_specs = P(None, "clus")
    return jax.shard_map(shards, mesh=mesh, in_specs=in_specs, out_specs=out_specs, check_vma=False)
```
